512 devices in a mesh: gx: 4 (over x_lo, core), gy: 8 (over x_hi, y), gz: 16 (over z).
Axes of the slice: x: 4 (x_hi: 2, x_lo: 2; x = x_hi * 2 + x_lo), y: 4, z: 16, core: 2. Of those that a mesh axis runs over, the one named last changes fastest.
Arguments:
- e_field: float32 [3, 256, 128, 1024], P(None, 'gz', 'gx', 'gy'), may hold values from -6 to 6
- h_field: float32 [3, 256, 128, 1024], P(None, 'gz', 'gx', 'gy'), may hold values from -6 to 6
- material: int32 [256, 128, 1024], P('gz', 'gx', 'gy'), may hold values from 0 to 7
- inv_permittivity: float32 [8], replicated, may hold values from 0.08 to 1
- block_cells: int32 [65536, 128], P(('gx', 'gy', 'gz')), may hold values from 0 to 65535, as said below
- block_count: int32 [512], P(('gx', 'gy', 'gz')), may hold values from 1 to 128, 33024 in all
- block_decay: float32 [65536], P(('gx', 'gy', 'gz')), may hold values from 0.6 to 0.98
- block_restore: float32 [65536], P(('gx', 'gy', 'gz')), may hold values from 0.02 to 0.3
- block_drive: float32 [65536], P(('gx', 'gy', 'gz')), may hold values from 0.05 to 0.5
- polarization: float32 [3, 65536, 128], P(None, ('gx', 'gy', 'gz')), may hold values from -6 to 6
- current: float32 [3, 65536, 128], P(None, ('gx', 'gy', 'gz')), may hold values from -6 to 6
Outputs:
- e_out: float32 [3, 256, 128, 1024], P(None, 'gz', 'gx', 'gy')
- h_out: float32 [3, 256, 128, 1024], P(None, 'gz', 'gx', 'gy')
- pol_out: float32 [3, 65536, 128], P(None, ('gx', 'gy', 'gz'))
- cur_out: float32 [3, 65536, 128], P(None, ('gx', 'gy', 'gz'))
The draws below stay inside these ranges and needn't reach their ends.
Inputs may be any that keep to these rules, and one draw needn't show every extreme that they name: `block_cells`: each row of a device's 128 rows holds, in some order, all 128 local cells of one aligned run [s * 128, (s + 1) * 128); different rows of one device hold different runs. `block_count`: the number of live leading rows among each device's 128 rows; the counts sum to 512 * 129 // 2.
All inputs are finite; a program needn't handle non-finite values.
Results may differ from the reference program's by a relative error of at most 0.00013.
Values sent between devices are 32-bit elements; how exact they have to be, the bound alone decides.
No kernel may reach another device: no remote copies, remote signals or barrier semaphores. Data moves between devices by JAX's collectives and lax.ppermute only.
A program may use at most 128 MiB of HBM per device.

```python
import math
import jax
import jax.numpy as jnp
import numpy as np
from jax import lax

CZ = 16
CX = 32
CY = 128
NB = 128
BLOCK = 128
NMAT = 8
STEPS = 2
NZ = 256
NX = 128
NY = 1024
NBT = 65536
N_GY = 8
N_GZ = 16
DEVICES = 512


def draw_block_cells(key, part):
    key = jax.random.fold_in(key, 11)
    run_count = CZ * CX * CY // BLOCK
    device_keys = jax.random.split(key, DEVICES)

    def one_device(device_key):
        run_key, order_key = jax.random.split(device_key)
        runs = jax.random.permutation(run_key, run_count)[:NB].astype(jnp.int32)
        order_keys = jax.random.split(order_key, NB)
        orders = jax.vmap(lambda k: jax.random.permutation(k, BLOCK).astype(jnp.int32))(order_keys)
        return runs[:, None] * BLOCK + orders
    chosen = jax.vmap(one_device)(device_keys)
    return chosen.reshape(DEVICES * NB, BLOCK).astype(jnp.int32)


def place_ends(array, rng, smallest, top_value):
    longest = array.shape.index(max(array.shape))
    spots = []
    for shift in (0, 1):
        where = [jax.random.randint(jax.random.fold_in(rng, axis), (), 0, length) for axis, length in enumerate(array.shape)]
        where[longest] = (where[longest] + shift) % array.shape[longest]
        spots.append(tuple(where))
    return array.at[spots[0]].set(smallest).at[spots[1]].set(top_value)


def block_levels(rng, shape, cuts, low, high):
    def one(axis_at, parts):
        heights = jax.random.uniform(jax.random.fold_in(jax.random.fold_in(rng, 6), axis_at), (parts,), jnp.float32, low / len(cuts), high / len(cuts))
        return jnp.repeat(jnp.exp(heights), shape[axis_at] // parts).reshape((-1,) + (1,) * (len(shape) - axis_at - 1))

    loudness = one(*cuts[0])
    for cut in cuts[1:]:
        loudness = loudness * one(*cut)
    return loudness


def profile(number_of, total, bound, slope):
    loads = [(1 << 20) // math.isqrt(grade ** slope) + 1 for grade in range(2, number_of + 1)]
    spare, holding = total - bound - (number_of - 1), [1] * (number_of - 1)
    while spare > 0:
        movable = [i for i in range(number_of - 1) if holding[i] < bound]
        pool, left = sum([loads[i] for i in movable]), spare
        for i in movable:
            addition = min(bound - holding[i], max(1, left * loads[i] // pool), spare)
            holding[i] = holding[i] + addition
            spare = spare - addition
    return np.array([bound] + holding)


def ragged(key, amount, total, limit, lean):
    if amount == 2:
        one = jax.random.randint(key, (), max(1, total - limit), min(limit, total - 1) + 1)
        return jnp.stack([one, total - one])
    tallies = jnp.asarray(profile(amount, total, limit, lean), jnp.int32)
    twos = (amount - 1) // 2
    source_of, taker = tallies[1:1 + 2 * twos:2], tallies[2:2 + 2 * twos:2]
    room = jnp.minimum(source_of - 1, limit - taker)
    passed = jax.random.randint(jax.random.fold_in(key, 1), (twos,), 0, 1 << 20) % (room + 1)
    tallies = tallies.at[1:1 + 2 * twos:2].set(source_of - passed).at[2:2 + 2 * twos:2].set(taker + passed)
    return tallies[jax.random.permutation(jax.random.fold_in(key, 2), amount)]


def scatter_about(key, extent, width, bound, cuts=(), held_as=jnp.bfloat16):
    entries = width * jax.random.normal(key, extent, jnp.float32)
    if cuts:
        entries = entries * block_levels(key, extent, cuts, -0.22, 0.18)
    return jnp.clip(entries, -bound, bound).astype(held_as)


def setup_inputs(seed: int = 0) -> dict:
    key_list = jax.random.split(jax.random.key(seed), 12)
    return {
        "e_field": scatter_about(key_list[0], (3, NZ, NX, NY), 1.0, 6.0, ((1, 16), (2, 4), (3, 8)), jnp.float32),
        "h_field": scatter_about(key_list[1], (3, NZ, NX, NY), 1.0, 6.0, ((1, 16), (2, 4), (3, 8)), jnp.float32),
        "material": place_ends(jax.random.randint(key_list[2], (NZ, NX, NY), 0, NMAT), jax.random.fold_in(key_list[2], 1), 0, NMAT - 1).astype(jnp.int32),
        "inv_permittivity": jnp.clip(jnp.exp(jax.random.uniform(key_list[3], (NMAT,), jnp.float32, math.log(0.08), math.log(1.0))), 0.08, 1.0),
        "block_cells": draw_block_cells(jax.random.fold_in(key_list[11], 71), 0),
        "block_count": ragged(key_list[5], DEVICES, DEVICES * (NB + 1) // 2, NB, 2).astype(jnp.int32),
        "block_decay": jnp.clip(0.6 + 0.38 * jax.random.uniform(key_list[6], (NBT,), jnp.float32) ** block_levels(key_list[6], (NBT,), ((0, 512),), -0.2, 0.2), 0.6, 0.98),
        "block_restore": jnp.clip(jnp.exp(math.log(0.3) - 2.7080503 * jax.random.uniform(key_list[7], (NBT,), jnp.float32) ** block_levels(key_list[7], (NBT,), ((0, 512),), -0.2, 0.2)), 0.02, 0.3),
        "block_drive": jnp.clip(jnp.exp(math.log(0.5) - 2.3025851 * jax.random.uniform(key_list[8], (NBT,), jnp.float32) ** block_levels(key_list[8], (NBT,), ((0, 512),), -0.2, 0.2)), 0.05, 0.5),
        "polarization": scatter_about(key_list[9], (3, NBT, BLOCK), 1.0, 6.0, ((1, 512),), jnp.float32),
        "current": scatter_about(key_list[10], (3, NBT, BLOCK), 1.0, 6.0, ((1, 512),), jnp.float32),
    }


TIME_STEP = 0.5


def rising(values, along):
    length = values.shape[along]
    upper = lax.slice_in_dim(values, 1, length, axis=along)
    extended = jnp.concatenate([upper, jnp.zeros_like(lax.slice_in_dim(values, 0, 1, axis=along))], along)
    return extended - values


def falling(values, along):
    length = values.shape[along]
    lower = lax.slice_in_dim(values, 0, length - 1, axis=along)
    extended = jnp.concatenate([jnp.zeros_like(lax.slice_in_dim(values, 0, 1, axis=along)), lower], along)
    return values - extended


def curl_forward(field):
    curl_x = rising(field[2], 2) - rising(field[1], 0)
    curl_y = rising(field[0], 0) - rising(field[2], 1)
    curl_z = rising(field[1], 1) - rising(field[0], 2)
    return jnp.stack([curl_x, curl_y, curl_z])


def curl_backward(field):
    curl_x = falling(field[2], 2) - falling(field[1], 0)
    curl_y = falling(field[0], 0) - falling(field[2], 1)
    curl_z = falling(field[1], 1) - falling(field[0], 2)
    return jnp.stack([curl_x, curl_y, curl_z])


def global_cells(block_cells):
    rows = jnp.arange(block_cells.shape[0], dtype=jnp.int32)
    device = rows // NB
    index_x = device // (N_GY * N_GZ)
    index_y = (device // N_GZ) % N_GY
    index_z = device % N_GZ
    local_z = block_cells // (CX * CY)
    local_x = (block_cells // CY) % CX
    local_y = block_cells % CY
    glob_z = index_z[:, None] * CZ + local_z
    glob_x = index_x[:, None] * CX + local_x
    glob_y = index_y[:, None] * CY + local_y
    return ((glob_z * NX + glob_x) * NY + glob_y).astype(jnp.int32)


def reference(e_field, h_field, material, inv_permittivity, block_cells, block_count, block_decay, block_restore, block_drive, polarization, current):
    rows = jnp.arange(block_cells.shape[0], dtype=jnp.int32)
    live = ((rows % NB) < block_count[rows // NB])[None, :, None]
    where_cells = global_cells(block_cells)
    flat_cells = where_cells.reshape(-1)
    cell_inv = inv_permittivity[material]
    decay = block_decay[None, :, None]
    restore = block_restore[None, :, None]
    drive = block_drive[None, :, None]
    for step in range(STEPS):
        h_field = h_field - TIME_STEP * curl_forward(e_field)
        at_cells = e_field.reshape(3, -1)[:, where_cells]
        current = jnp.where(live, decay * current - restore * polarization + drive * at_cells, current)
        polarization = jnp.where(live, polarization + TIME_STEP * current, polarization)
        placed = jnp.where(live, current, jnp.float32(0.0)).reshape(3, -1)
        j_cells = jnp.zeros((3, NZ * NX * NY), jnp.float32).at[:, flat_cells].add(placed).reshape(e_field.shape)
        e_field = e_field + TIME_STEP * cell_inv * (curl_backward(h_field) - j_cells)
    return e_field, h_field, polarization, current
```

```python
import functools

import jax
import jax.numpy as jnp
from jax import lax
from jax.experimental import pallas as pl
from jax.experimental.pallas import tpu as pltpu
from jax.sharding import PartitionSpec as P

STEPS = 2
TIME_STEP = 0.5
VMEM_LIMIT = 48 * 1024 * 1024


def passed_along(value, axis, steps):
    count = lax.axis_size(axis)
    first, last = (max(0, -steps), min(count, count - steps))
    return lax.ppermute(value, axis, [(source, source + steps) for source in range(first, last)])


def rising(values, plane, along):
    length = values.shape[along]
    upper = lax.slice_in_dim(values, 1, length, axis=along)
    return jnp.concatenate([upper, plane], along) - values


def falling(values, plane, along):
    length = values.shape[along]
    lower = lax.slice_in_dim(values, 0, length - 1, axis=along)
    return values - jnp.concatenate([plane, lower], along)


def curl(step_of, field, plane_x, plane_y, plane_z):
    curl_x = step_of(field[2], plane_y[1][:, :, None], 2) - step_of(field[1], plane_z[1][None], 0)
    curl_y = step_of(field[0], plane_z[0][None], 0) - step_of(field[2], plane_x[1][:, None, :], 1)
    curl_z = step_of(field[1], plane_x[0][:, None, :], 1) - step_of(
        field[0], plane_y[0][:, :, None], 2
    )
    return jnp.stack([curl_x, curl_y, curl_z])


def e_planes(e_field):
    first_x = jnp.stack([e_field[1][:, 0, :], e_field[2][:, 0, :]])
    first_y = jnp.stack([e_field[0][:, :, 0], e_field[2][:, :, 0]])
    first_z = e_field[0:2, 0]
    got_x = passed_along(first_x, "gx", -1)
    got_y = passed_along(first_y, "gy", -1)
    got_z = passed_along(first_z, "gz", -1)
    return (got_x, got_y, got_z)


def h_planes(h_field):
    last_x = jnp.stack([h_field[1][:, -1, :], h_field[2][:, -1, :]])
    last_y = jnp.stack([h_field[0][:, :, -1], h_field[2][:, :, -1]])
    last_z = h_field[0:2, -1]
    got_x = passed_along(last_x, "gx", 1)
    got_y = passed_along(last_y, "gy", 1)
    got_z = passed_along(last_z, "gz", 1)
    return (got_x, got_y, got_z)


def as_column(row_ref, eye):
    return jnp.sum(jnp.where(eye, row_ref[...], 0.0), axis=1, keepdims=True)


def advance_blocks(e, cells, inverse, runs, count, decay, restore, drive, pol, cur, pol_out, cur_out, rows, j_rows):
    slots, width = cells.shape
    for b in range(slots):
        run = runs[0, b]
        for comp in range(3):
            rows[comp, pl.ds(b, 1), :] = e[comp, pl.ds(run, 1), :]
    j_rows[...] = jnp.zeros_like(j_rows)
    offsets = lax.bitwise_and(cells[...], width - 1)
    down = lax.broadcasted_iota(jnp.int32, (slots, width), 0)
    across = lax.broadcasted_iota(jnp.int32, (slots, width), 1)
    eye = down == across
    live = down < count[0]
    decay_c, restore_c, drive_c = (as_column(ref, eye) for ref in (decay, restore, drive))
    back = inverse[...]
    for comp in range(3):
        at_cells = jnp.take_along_axis(rows[comp], offsets, axis=1)
        held, polar = cur[comp], pol[comp]
        new = jnp.where(live, decay_c * held - restore_c * polar + drive_c * at_cells, held)
        cur_out[comp] = new
        pol_out[comp] = jnp.where(live, polar + TIME_STEP * new, polar)
        rows[comp] = jnp.take_along_axis(jnp.where(live, new, 0.0), back, axis=1)
    for b in range(slots):
        run = runs[0, b]
        for comp in range(3):
            j_rows[comp, pl.ds(run, 1), :] = rows[comp, pl.ds(b, 1), :]


def first_blocks(
    e, material, inv_perm, cells, count, decay, restore, drive, pol, cur,
    pol_out, cur_out, a_out, scale_out, inverse_out, runs_out, rows, j_rows, run_row, runs, sem,
):
    slots, width = cells.shape
    down = lax.broadcasted_iota(jnp.int32, (slots, width), 0)
    across = lax.broadcasted_iota(jnp.int32, (slots, width), 1)
    run_of = lax.shift_right_logical(cells[...], width.bit_length() - 1)
    run_row[...] = jnp.sum(jnp.where(down == across, run_of, 0), axis=0, keepdims=True)
    runs_out[...] = run_row[...]
    copy = pltpu.make_async_copy(run_row, runs, sem)
    copy.start()
    offsets = lax.bitwise_and(cells[...], width - 1)
    for block in range(slots // 8):
        part = offsets[block * 8 : block * 8 + 8]
        lanes = across[:8]
        found = jnp.zeros((8, width), jnp.int32)
        for k in range(width):
            found = jnp.where(part[:, k : k + 1] == lanes, k, found)
        inverse_out[block * 8 : block * 8 + 8, :] = found
    table = jnp.zeros((8, width), jnp.float32)
    for kind in range(inv_perm.shape[0]):
        table = jnp.where(across[:8] == kind, TIME_STEP * inv_perm[kind], table)
    for row in range(0, material.shape[0], 8):
        scale_out[row : row + 8, :] = jnp.take_along_axis(table, material[row : row + 8, :], axis=1)
    copy.wait()
    advance_blocks(e, cells, inverse_out, runs, count, decay, restore, drive, pol, cur, pol_out, cur_out, rows, j_rows)
    for comp in range(3):
        a_out[comp] = e[comp] - scale_out[...] * j_rows[comp]


def next_blocks(
    e, scale, inverse, runs, cells, count, decay, restore, drive, pol, cur,
    pol_out, cur_out, a_out, rows, j_rows,
):
    advance_blocks(e, cells, inverse, runs, count, decay, restore, drive, pol, cur, pol_out, cur_out, rows, j_rows)
    for comp in range(3):
        a_out[comp] = e[comp] - scale[...] * j_rows[comp]


def on_device(
    e_field, h_field, material, inv_permittivity, block_cells, block_count,
    block_decay, block_restore, block_drive, polarization, current,
):
    slots, width = block_cells.shape
    shape = e_field.shape
    runs_all = shape[1] * shape[2] * shape[3] // width
    f32, i32 = jnp.float32, jnp.int32
    vmem, smem = pl.BlockSpec(memory_space=pltpu.VMEM), pl.BlockSpec(memory_space=pltpu.SMEM)
    flat = (3, runs_all, width)
    coefficients = [v.reshape(1, slots) for v in (block_decay, block_restore, block_drive)]
    blocks = jax.ShapeDtypeStruct((3, slots, width), f32)
    params = pltpu.CompilerParams(vmem_limit_bytes=VMEM_LIMIT)
    scratch = [pltpu.VMEM((3, slots, width), f32), pltpu.VMEM(flat, f32)]
    pol1, cur1, a1, scale, inverse, runs = pl.pallas_call(
        first_blocks,
        out_shape=[
            blocks, blocks, jax.ShapeDtypeStruct(flat, f32), jax.ShapeDtypeStruct((runs_all, width), f32),
            jax.ShapeDtypeStruct((slots, width), i32), jax.ShapeDtypeStruct((1, slots), i32),
        ],
        in_specs=[vmem, vmem, smem, vmem, smem, vmem, vmem, vmem, vmem, vmem],
        out_specs=[vmem] * 6,
        scratch_shapes=scratch + [pltpu.VMEM((1, slots), i32), pltpu.SMEM((1, slots), i32), pltpu.SemaphoreType.DMA],
        compiler_params=params,
        name="first_blocks",
    )(
        e_field.reshape(flat), material.reshape(runs_all, width), inv_permittivity, block_cells, block_count,
        *coefficients, polarization, current,
    )
    scale_cells = scale.reshape(shape[1:])
    got = e_planes(e_field)
    h_field = h_field - TIME_STEP * curl(rising, e_field, *got)
    got_h = h_planes(h_field)
    e_field = a1.reshape(shape) + scale_cells * curl(falling, h_field, *got_h)
    pol2, cur2, a2 = pl.pallas_call(
        next_blocks,
        out_shape=[blocks, blocks, jax.ShapeDtypeStruct(flat, f32)],
        in_specs=[vmem, vmem, vmem, smem, vmem, smem, vmem, vmem, vmem, vmem, vmem],
        out_specs=[vmem] * 3,
        scratch_shapes=scratch,
        compiler_params=params,
        name="next_blocks",
    )(e_field.reshape(flat), scale, inverse, runs, block_cells, block_count, *coefficients, pol1, cur1)
    got = e_planes(e_field)
    h_field = h_field - TIME_STEP * curl(rising, e_field, *got)
    got_h = h_planes(h_field)
    e_field = a2.reshape(shape) + scale_cells * curl(falling, h_field, *got_h)
    return (e_field, h_field, pol2, cur2)


def solution(mesh):
    grid = P(None, "gz", "gx", "gy")
    rows = ("gx", "gy", "gz")
    return jax.shard_map(
        on_device,
        mesh=mesh,
        in_specs=(
            grid, grid, P("gz", "gx", "gy"), P(), P(rows, None), P(rows), P(rows), P(rows), P(rows),
            P(None, rows, None), P(None, rows, None),
        ),
        out_specs=(grid, grid, P(None, rows, None), P(None, rows, None)),
        check_vma=False,
    )
```

```python
import jax
import jax.numpy as jnp
from jax import lax
from jax.experimental import pallas as pl
from jax.experimental.pallas import tpu as pltpu
from jax.sharding import PartitionSpec as P

TIME_STEP = 0.5
VMEM_LIMIT = 32 * 1024 * 1024

SLABS, ROWS, HALO, LANES, COLUMNS = 16, 32, 8, 128, 7
EXT = ROWS + HALO

FIELDS = 10
UP_X = [(f, 30, 6) for f in (0, 1, 2, 4, 5)] + [(f, 31, 7) for f in range(FIELDS)]
DOWN_X = [(f, 0, 0) for f in (0, 1, 2, 3, 4, 5, 7, 8, 9)] + [(f, 1, 1) for f in (1, 2)]


def passed_along(value, axis, steps):
    count = lax.axis_size(axis)
    first, last = (max(0, -steps), min(count, count - steps))
    return lax.ppermute(value, axis, [(source, source + steps) for source in range(first, last)])


def lanes_by(value, shift):
    shift = shift % LANES
    return pltpu.roll(value, shift, 1) if shift else value


def x_next(value):
    return pltpu.roll(value, EXT - 1, 0)


def x_before(value):
    return pltpu.roll(value, 1, 0)


def lane_ids(rows=EXT):
    return lax.broadcasted_iota(jnp.int32, (rows, LANES), 1)


def column_of(packed, z, slot, lane):
    return lanes_by(packed, lane - ((z + 1) * COLUMNS + slot))


def row_factor(flags):
    row = lax.broadcasted_iota(jnp.int32, (EXT, LANES), 0)
    return jnp.where(row >= ROWS + 4, TIME_STEP * flags[0], TIME_STEP)


def packed_places(rows=EXT):
    lane = lane_ids(rows)
    z_at = lax.shift_right_logical(lane * 9363, 16)
    return z_at, lane - z_at * COLUMNS


def h_slab(h, e, e_above, e_y, factor):
    return (
        h[0] - factor * ((e_y[1] - e[2]) - (e_above[1] - e[1])),
        h[1] - factor * ((e_above[0] - e[0]) - (x_next(e[2]) - e[2])),
        h[2] - factor * ((x_next(e[1]) - e[1]) - (e_y[0] - e[0])),
    )


def e_slab(a, scale, h, h_below, h_y):
    return (
        a[0] + scale * ((h[2] - h_y[1]) - (h[1] - h_below[1])),
        a[1] + scale * ((h[0] - h_below[0]) - (h[2] - x_before(h[2]))),
        a[2] + scale * ((h[1] - x_before(h[1])) - (h[0] - h_y[0])),
    )


def y_next_pair(e, packed_e, z, last):
    return tuple(
        jnp.where(last, column_of(packed_e[c], z, 5, LANES - 1), lanes_by(e[c], -1)) for c in (0, 2)
    )


def y_before_pair(h, packed_h, z, first):
    return tuple(jnp.where(first, column_of(packed_h[c], z, 1, 0), lanes_by(h[c], 1)) for c in (0, 2))


def as_column(row_ref, eye):
    return jnp.sum(jnp.where(eye, row_ref[...], 0.0), axis=1, keepdims=True)


def advance_blocks(e, pitch, cells, inverse, runs, count, decay, restore, drive, pol, cur, pol_out, cur_out, rows, j_rows):
    slots, width = cells.shape
    for b in range(slots):
        run = runs[0, b]
        at = run + lax.shift_right_logical(run, 5) * (pitch - ROWS)
        for comp in range(3):
            rows[comp, pl.ds(b, 1), :] = e[comp, pl.ds(at, 1), :]
    j_rows[...] = jnp.zeros_like(j_rows)
    offsets = lax.bitwise_and(cells[...], width - 1)
    down = lax.broadcasted_iota(jnp.int32, (slots, width), 0)
    across = lax.broadcasted_iota(jnp.int32, (slots, width), 1)
    eye = down == across
    live = down < count[0]
    decay_c, restore_c, drive_c = (as_column(ref, eye) for ref in (decay, restore, drive))
    back = inverse[...]
    for comp in range(3):
        at_cells = jnp.take_along_axis(rows[comp], offsets, axis=1)
        held, polar = cur[comp], pol[comp]
        new = jnp.where(live, decay_c * held - restore_c * polar + drive_c * at_cells, held)
        cur_out[comp] = new
        pol_out[comp] = jnp.where(live, polar + TIME_STEP * new, polar)
        rows[comp] = jnp.take_along_axis(jnp.where(live, new, 0.0), back, axis=1)
    for b in range(slots):
        run = runs[0, b]
        for comp in range(3):
            j_rows[comp, pl.ds(run, 1), :] = rows[comp, pl.ds(b, 1), :]


def spread(value):
    return value * 0x01010101


def invert_rows(offsets, lane):
    words = jnp.full(lane.shape, -0x7F7F7F80, jnp.int32)
    for t, part in enumerate(offsets):
        words = lax.bitwise_or(words, lax.shift_left(lax.bitwise_and(part - lane, LANES - 1), 8 * t))
    low, high = {}, {}
    for s in range(1, LANES):
        misses = lax.bitwise_xor(pltpu.roll(words, s, 1), spread(s)) - spread(1)
        for table, at in ((low, s % 8), (high, s // 8)):
            table[at] = lax.bitwise_and(table[at], misses) if at in table else misses
    found = jnp.zeros(lane.shape, jnp.int32)
    for bit in range(7):
        table, mask = (low, 1 << bit) if bit < 3 else (high, 1 << (bit - 3))
        every = None
        for at, value in table.items():
            if at & mask:
                every = value if every is None else lax.bitwise_and(every, value)
        hit = lax.bitwise_and(lax.shift_right_logical(lax.bitwise_xor(every, -1), 7), spread(1))
        found = lax.bitwise_or(found, lax.shift_left(hit, bit))
    return [
        lax.bitwise_and(lane - lax.bitwise_and(lax.shift_right_logical(found, 8 * t), LANES - 1), LANES - 1)
        for t in range(len(offsets))
    ]


def first_kernel(
    e_in, h_in, material_in, inv_perm_in, cells_in, count, decay_in, restore_in, drive_in, pol_in, cur_in,
    e, h, pol_out, cur_out, a_out, scale_out, inverse_out, cells, runs_out, decay, restore, drive, up_out, down_out,
    material, inv_perm, pol, cur, rows, j_rows, run_row, runs, sems,
):
    copies = {}
    for i, (name, source, target) in enumerate(
        (
            ("cells", cells_in, cells), ("inv_perm", inv_perm_in, inv_perm), ("material", material_in, material),
            ("decay", decay_in, decay), ("restore", restore_in, restore), ("drive", drive_in, drive),
            ("e", e_in, e), ("cur", cur_in, cur), ("pol", pol_in, pol), ("h", h_in, h),
        )
    ):
        copies[name] = pltpu.make_async_copy(source, target, sems.at[i])
        copies[name].start()
    slots, width = cells.shape
    down = lax.broadcasted_iota(jnp.int32, (slots, width), 0)
    across = lax.broadcasted_iota(jnp.int32, (slots, width), 1)
    lane = lane_ids(8)
    copies["cells"].wait()
    run_of = lax.shift_right_logical(cells[...], 7)
    run_row[...] = jnp.sum(jnp.where(down == across, run_of, 0), axis=0, keepdims=True)
    runs_out[...] = run_row[...]
    copy = pltpu.make_async_copy(run_row, runs, sems.at[10])
    copy.start()
    for row in range(0, slots, 32):
        parts = [lax.bitwise_and(cells[row + 8 * t : row + 8 * t + 8, :], width - 1) for t in range(4)]
        for t, part in enumerate(invert_rows(parts, lane)):
            inverse_out[row + 8 * t : row + 8 * t + 8, :] = part
    copies["inv_perm"].wait()
    copies["material"].wait()
    table = jnp.zeros((8, width), jnp.float32)
    for kind in range(inv_perm.shape[0]):
        table = jnp.where(lane == kind, TIME_STEP * inv_perm[kind], table)
    for row in range(0, material.shape[0], 8):
        scale_out[row : row + 8, :] = jnp.take_along_axis(table, material[row : row + 8, :], axis=1)
    for name in ("decay", "restore", "drive", "e", "cur", "pol"):
        copies[name].wait()
    copy.wait()
    advance_blocks(
        e, ROWS, cells, inverse_out, runs, count, decay, restore, drive, pol, cur, pol_out, cur_out, rows, j_rows
    )
    for comp in range(3):
        a_out[comp] = e[comp] - scale_out[...] * j_rows[comp]
    copies["h"].wait()

    def plane(f, x):
        at = pl.ds(x, SLABS, stride=ROWS)
        if f == 9:
            return scale_out[at, :]
        return (e, h, a_out)[f // 3][f % 3, at, :]

    for out, planes in ((up_out, UP_X), (down_out, DOWN_X)):
        for i, (f, x, _) in enumerate(planes):
            out[i] = plane(f, x)


def pack_tiles(tile, tiles):
    lane = lane_ids(8)
    z_at, slot = packed_places(8)
    low = jnp.logical_or(slot == 2, slot == 3)
    inside = jnp.logical_and(z_at >= 1, z_at <= SLABS)
    low, high = jnp.logical_and(low, inside), jnp.logical_and(slot >= 5, inside)
    tops = [jnp.zeros((8, LANES), jnp.float32) for _ in range(tiles)]
    bottoms = list(tops)
    for z in range(SLABS):
        place = (z + 1) * COLUMNS + 5
        top_at, bottom_at = lane >= place, lane >= place + 2
        for t in range(tiles):
            moved = lanes_by(tile(z, t), place - (LANES - 2))
            tops[t] = jnp.where(top_at, moved, tops[t])
            bottoms[t] = jnp.where(bottom_at, moved, bottoms[t])
    return [
        jnp.where(high, top, jnp.where(low, lanes_by(bottom, -5), 0.0)) for top, bottom in zip(tops, bottoms)
    ]


def own_kernel(e, h, a, scale, own_out):
    for f in range(FIELDS):
        def tile(z, t):
            at = slice(z * ROWS + t * 8, z * ROWS + t * 8 + 8)
            return scale[at, :] if f == 9 else (e, h, a)[f // 3][f % 3, at, :]

        for t, value in enumerate(pack_tiles(tile, ROWS // 8)):
            own_out[f, t * 8 : t * 8 + 8, :] = value


UP_E0X, UP_E0Y, UP_E0Y_2, UP_H1Y = 1, 2, 3, 4
DOWN_H1Y = 1


def faces_kernel(from_below, from_above, own, flags, halo_out, pe_out, pscale_out, ph1_out, pe1_out, up_out, down_out):
    halo_out[...] = jnp.zeros_like(halo_out)
    for got, planes in ((from_below, UP_X), (from_above, DOWN_X)):
        for i, (f, _, row) in enumerate(planes):
            halo_out[f, pl.ds(row, SLABS, stride=HALO), :] = got[i]
    packed = []
    for f in range(FIELDS):
        (tile,) = pack_tiles(lambda z, t: halo_out[f, z * HALO : z * HALO + 8, :], 1)
        packed.append(jnp.concatenate([own[f], tile], axis=0))
    z_at, slot = packed_places()
    inside = jnp.logical_and(z_at >= 1, z_at <= SLABS)
    factor = jnp.where(inside, row_factor(flags), 0.0)
    factor = jnp.where(jnp.logical_or(slot >= 5, jnp.logical_or(slot == 2, slot == 3)), factor, 0.0)
    pe, pscale = packed[0:3], packed[9]
    ph1 = packed_h(packed[3:6], pe, factor)
    pe1 = e_slab(
        packed[6:9], pscale, ph1, (lanes_by(ph1[0], COLUMNS), lanes_by(ph1[1], COLUMNS)),
        (lanes_by(ph1[0], 1), lanes_by(ph1[2], 1)),
    )
    for c in range(3):
        pe_out[c], ph1_out[c], pe1_out[c] = pe[c], ph1[c], pe1[c]
    pscale_out[...] = pscale
    up = jnp.zeros((EXT, LANES), jnp.float32)
    for i, value in enumerate((ph1[0], ph1[2], *pe1, pscale)):
        up = jnp.where(slot == i, lanes_by(value, i - 6), up)
    for z_to, value, slot_from, z_from in (
        (UP_E0X, pe[0], 6, 1), (UP_E0Y, pe[1], 6, 1), (UP_E0Y_2, pe[1], 5, 1), (UP_H1Y, ph1[1], 6, SLABS),
    ):
        here = jnp.logical_and(slot == 6, z_at == z_to)
        up = jnp.where(here, lanes_by(value, 6 - slot_from + (z_to - z_from) * COLUMNS), up)
    up_out[...] = up
    low = jnp.zeros((EXT, LANES), jnp.float32)
    for i, value in enumerate((pe1[0], pe1[2], pscale, pe[0], pe[2], pe[1])):
        low = jnp.where(slot == i, lanes_by(value, i - 2), low)
    here = jnp.logical_and(slot == 6, z_at == DOWN_H1Y)
    down_out[...] = jnp.where(here, lanes_by(ph1[1], 4 + (DOWN_H1Y - SLABS) * COLUMNS), low)


def slab_reader(e, h, a, scale, halo):
    def read(f, z):
        if f == 9:
            own = scale[z * ROWS : (z + 1) * ROWS, :]
        else:
            own = (e, h, a)[f // 3][f % 3, z * ROWS : (z + 1) * ROWS, :]
        return jnp.concatenate([own, halo[f, z * HALO : (z + 1) * HALO, :]], axis=0)

    return read


def packed_h(h, e, factor):
    return h_slab(
        h, e, (lanes_by(e[0], -COLUMNS), lanes_by(e[1], -COLUMNS)), (lanes_by(e[0], -1), lanes_by(e[2], -1)), factor
    )


END_H = (0, 14, 15)
END_E = (0, 15)


def ends_kernel(
    e, h, a, scale, halo, pe_in, pscale_in, ph1_in, pe1_in, from_below, from_above, flags,
    pe_out, pscale_out, ph1_out, pe1_out, h1_out, e1_out, up_out, down_out,
):
    z_at, slot = packed_places()
    inside = jnp.logical_and(z_at >= 1, z_at <= SLABS)
    factor = row_factor(flags)
    packed_factor = jnp.where(slot < 2, factor * flags[1], factor)
    packed_factor = jnp.where(inside, packed_factor, 0.0)
    up_got, down_got = from_below[...], from_above[...]
    last_low, first_high = slot == 1, slot == 5

    def columns(value, low=None, high=None):
        value = jnp.where(slot == 2, value, jnp.where(slot == 4, lanes_by(value, -2), 0.0))
        if low is not None:
            value = jnp.where(last_low, lanes_by(up_got, 1 - low), value)
        if high is not None:
            value = jnp.where(first_high, lanes_by(down_got, 5 - high), value)
        return jnp.where(inside, value, 0.0)

    def single(got, slot_to, z_to, z_from, value):
        here = jnp.logical_and(slot == slot_to, z_at == z_to)
        return jnp.where(here, lanes_by(got, slot_to - 6 + (z_to - z_from) * COLUMNS), value)

    pe = [columns(pe_in[0], None, 3), columns(pe_in[1], None, 5), columns(pe_in[2], None, 4)]
    pe[0] = single(up_got, 1, 1, UP_E0X, pe[0])
    pe[1] = single(up_got, 1, 1, UP_E0Y, pe[1])
    pe[1] = single(up_got, 0, 1, UP_E0Y_2, pe[1])
    pscale = columns(pscale_in[...], 5, 2)
    ph1 = [columns(ph1_in[0], 0), columns(ph1_in[1]), columns(ph1_in[2], 1)]
    ph1[1] = single(up_got, 1, SLABS, UP_H1Y, ph1[1])
    ph1[1] = single(down_got, 5, SLABS, DOWN_H1Y, ph1[1])
    pe1 = [columns(pe1_in[0], 2, 0), columns(pe1_in[1], 3), columns(pe1_in[2], 4, 1)]
    upper = jnp.logical_or(slot == 1, slot == 4)
    lower = jnp.logical_or(slot == 2, slot == 5)
    step = jnp.where(upper, packed_factor, 0.0)
    pdx = -(step * lanes_by(pe[2], -1))
    pdz = step * lanes_by(pe[0], -1)
    ph1[0], ph1[2] = ph1[0] + pdx, ph1[2] + pdz
    px = jnp.where(lower, lanes_by(ph1[0], 1), 0.0)
    pz = jnp.where(lower, lanes_by(ph1[2], 1), 0.0)
    pe1[0] = pe1[0] + pscale * (pdz - pz)
    pe1[1] = pe1[1] + pscale * ((pdx - lanes_by(pdx, COLUMNS)) - (pdz - x_before(pdz)))
    pe1[2] = pe1[2] + pscale * (px - pdx)
    for c in range(3):
        pe_out[c], ph1_out[c], pe1_out[c] = pe[c], ph1[c], pe1[c]
    pscale_out[...] = pscale
    read = slab_reader(e, h, a, scale, halo)
    lane = lane_ids()
    first, last = lane == 0, lane == LANES - 1
    zero = jnp.zeros((EXT, LANES), jnp.float32)
    made = {}
    for i, z in enumerate(END_H):
        ez = [read(c, z) for c in range(3)]
        above = (read(0, z + 1), read(1, z + 1)) if z < SLABS - 1 else (zero, zero)
        made[z] = h_slab([read(3 + c, z) for c in range(3)], ez, above, y_next_pair(ez, pe, z, last), factor)
        for c in range(3):
            h1_out[c, i] = made[z][c]
    ends = {}
    for i, z in enumerate(END_E):
        below = made[z - 1][:2] if z else (zero, zero)
        ends[z] = e_slab(
            [read(6 + c, z) for c in range(3)], read(9, z), made[z], below, y_before_pair(made[z], ph1, z, first)
        )
        for c in range(3):
            e1_out[c, i] = ends[z][c]
    top = SLABS - 1
    up = [made[top][0], made[top][1], *ends[top], read(9, top)]
    packed_up = [ph1[0], ph1[1], *pe1, pscale]
    low = [ends[0][0], ends[0][1], read(9, 0), read(0, 0), read(1, 0)]
    packed_down = [pe1[0], pe1[1], pscale, pe[0], pe[1]]
    for out, slabs, columns, z_from in ((up_out, up, packed_up, SLABS), (down_out, low, packed_down, 1)):
        together = zero
        for i, (slab, column) in enumerate(zip(slabs, columns)):
            out[i] = slab
            together = jnp.where(z_at == i, lanes_by(column, (i - z_from) * COLUMNS), together)
        out[len(slabs)] = together


def middle_kernel(
    e, h, a, scale, halo, pe_in, pscale, ph1_in, pe1_in, h1_in, flags,
    e1_out, h2_out, e2_out, h1, h2,
):
    z_at, slot = packed_places()
    factor = row_factor(flags)
    packed_factor = jnp.where(slot < 2, factor * flags[1], factor)
    pe, ph1, pe1 = ([ref[c] for c in range(3)] for ref in (pe_in, ph1_in, pe1_in))
    read = slab_reader(e, h, a, scale, halo)
    lane = lane_ids()
    first, last = lane == 0, lane == LANES - 1
    zero = jnp.zeros((EXT, LANES), jnp.float32)

    def h1_of(c, z):
        return h1_in[c, END_H.index(z)] if z in END_H else h1[c, z]

    for z in range(1, 14):
        ez = [read(c, z) for c in range(3)]
        new = h_slab(
            [read(3 + c, z) for c in range(3)], ez, (read(0, z + 1), read(1, z + 1)), y_next_pair(ez, pe, z, last), factor
        )
        for c in range(3):
            h1[c, z] = new[c]
    for z in range(1, 15):
        hz = [h1_of(c, z) for c in range(3)]
        new = e_slab(
            [read(6 + c, z) for c in range(3)], read(9, z), hz, (h1_of(0, z - 1), h1_of(1, z - 1)),
            y_before_pair(hz, ph1, z, first),
        )
        for c in range(3):
            e1_out[c, z] = new[c]
    ph2 = packed_h(ph1, pe1, packed_factor)
    for z in range(1, 14):
        ez = [e1_out[c, z] for c in range(3)]
        new = h_slab(
            [h1[c, z] for c in range(3)], ez, (e1_out[0, z + 1], e1_out[1, z + 1]), y_next_pair(ez, pe1, z, last), factor
        )
        for c in range(3):
            h2[c, z] = new[c]
            h2_out[c, z * ROWS : (z + 1) * ROWS, :] = new[c][:ROWS]
    for z in range(1, 14):
        hz = [h2[c, z] for c in range(3)]
        below = (h2[0, z - 1], h2[1, z - 1]) if z > 1 else (zero, zero)
        new = e_slab(
            [e1_out[c, z] for c in range(3)], read(9, z), hz, below, y_before_pair(hz, ph2, z, first)
        )
        for c in range(3):
            e2_out[c, z * ROWS : (z + 1) * ROWS, :] = new[c][:ROWS]


def last_kernel(
    e, scale, halo, from_below, from_above, flags, pe_in, pscale_in, ph1_in, pe1_in, h1_in, e1_ends, e1_in, h2_in, e2_in,
    inverse, runs, cells, count, decay, restore, drive, pol, cur,
    e_to, h_to, pol_to, cur_to, e_out, h_out, pol_out, cur_out, e1, rows, j_rows, sems,
):
    started = []

    def send(source, target):
        copy = pltpu.make_async_copy(source, target, sems.at[len(started)])
        copy.start()
        started.append(copy)

    middle = pl.ds(ROWS, 13 * ROWS)
    send(h2_in.at[:, middle, :], h_to.at[:, middle, :])
    z_at, slot = packed_places()
    factor = row_factor(flags)
    below_factor = factor * flags[2]
    packed_factor = jnp.where(slot < 2, factor * flags[1], factor)
    packed_factor = jnp.where(z_at == 0, packed_factor * flags[2], packed_factor)
    packed_factor = jnp.where(z_at <= SLABS, packed_factor, 0.0)
    lane = lane_ids()
    first, last = lane == 0, lane == LANES - 1
    top = SLABS - 1

    def field(f, z):
        if f == 9:
            own = scale[z * ROWS : (z + 1) * ROWS, :]
        else:
            own = e[f, z * ROWS : (z + 1) * ROWS, :]
        return jnp.concatenate([own, halo[f, z * HALO : (z + 1) * HALO, :]], axis=0)

    def columns_below(i):
        return jnp.where(z_at == 0, lanes_by(from_below[6], -i * COLUMNS), 0.0)

    def columns_above(i):
        return jnp.where(z_at == SLABS + 1, lanes_by(from_above[5], (SLABS + 1 - i) * COLUMNS), 0.0)

    in_z = jnp.logical_and(z_at >= 1, z_at <= SLABS)
    far_e = [columns_above(3 + c) + jnp.where(z_at == 1, pe_in[c], 0.0) for c in range(2)]
    pdx = packed_factor * lanes_by(far_e[1], -COLUMNS)
    pdy = -(packed_factor * lanes_by(far_e[0], -COLUMNS))
    ph1 = [
        jnp.where(in_z, ph1_in[0], columns_below(0)) + pdx,
        jnp.where(in_z, ph1_in[1], columns_below(1)) + pdy,
        ph1_in[2],
    ]
    pscale = jnp.where(in_z, pscale_in[...], columns_below(5) + columns_above(2))
    edge = jnp.logical_or(z_at == 1, z_at == SLABS + 1)
    px = jnp.where(edge, lanes_by(ph1[0], COLUMNS), 0.0)
    py = jnp.where(edge, lanes_by(ph1[1], COLUMNS), 0.0)
    pe1 = [
        jnp.where(in_z, pe1_in[0], columns_below(2) + columns_above(0)) + pscale * (py - pdy),
        jnp.where(in_z, pe1_in[1], columns_below(3) + columns_above(1)) + pscale * (pdx - px),
        jnp.where(in_z, pe1_in[2], columns_below(4))
        + pscale * ((pdy - x_before(pdy)) - (pdx - lanes_by(pdx, 1))),
    ]
    ph2 = packed_h(ph1, pe1, packed_factor)

    def shifted_curl(dx, dy, z):
        dx_before = jnp.where(first, column_of(pdx, z, 1, 0), lanes_by(dx, 1))
        return (dy - x_before(dy)) - (dx - dx_before)

    dx, dy = factor * from_above[4], -(factor * from_above[3])
    h1_top = [h1_in[0, 2] + dx, h1_in[1, 2] + dy, h1_in[2, 2]]
    scale_top = field(9, top)
    e1_top = [
        e1_ends[0, 1] - scale_top * dy,
        e1_ends[1, 1] + scale_top * dx,
        e1_ends[2, 1] + scale_top * shifted_curl(dx, dy, top),
    ]
    e1_over = (from_above[0] + from_above[2] * h1_top[1], from_above[1] - from_above[2] * h1_top[0])
    dx, dy = below_factor * field(1, 0), -(below_factor * field(0, 0))
    h1_under = (from_below[0] + dx, from_below[1] + dy)
    scale_under = from_below[5]
    e1_under = [
        from_below[2] - scale_under * dy,
        from_below[3] + scale_under * dx,
        from_below[4] + scale_under * shifted_curl(dx, dy, -1),
    ]
    scale_0 = field(9, 0)
    e1_0 = [
        e1_ends[0, 0] + scale_0 * h1_under[1],
        e1_ends[1, 0] - scale_0 * h1_under[0],
        e1_ends[2, 0],
    ]
    for c in range(3):
        e1[c, 0:EXT, :] = e1_0[c]
        e1[c, top * EXT : (top + 1) * EXT, :] = e1_top[c]
        for z in range(1, top):
            e1[c, z * EXT : z * EXT + ROWS, :] = e1_in[c, z][:ROWS]
    advance_blocks(
        e1, EXT, cells, inverse, runs, count, decay, restore, drive, pol, cur, pol_out, cur_out, rows, j_rows
    )

    e1_1, e1_14 = ([e1_in[c, z] for c in range(3)] for z in (1, 14))
    under = h_slab(
        (*h1_under, h1_under[0]), e1_under, e1_0[:2], y_next_pair(e1_under, pe1, -1, last), below_factor
    )[:2]
    h2_0 = h_slab([h1_in[c, 0] for c in range(3)], e1_0, e1_1[:2], y_next_pair(e1_0, pe1, 0, last), factor)
    h2_14 = h_slab([h1_in[c, 1] for c in range(3)], e1_14, e1_top[:2], y_next_pair(e1_14, pe1, 14, last), factor)
    h2_top = h_slab(h1_top, e1_top, e1_over, y_next_pair(e1_top, pe1, top, last), factor)
    pad = jnp.zeros((HALO, LANES), jnp.float32)
    h2_13 = tuple(jnp.concatenate([h2_in[c, 13 * ROWS : 14 * ROWS, :], pad], axis=0) for c in range(2))
    e2 = {
        0: e_slab(e1_0, scale_0, h2_0, under, y_before_pair(h2_0, ph2, 0, first)),
        14: e_slab(e1_14, field(9, 14), h2_14, h2_13, y_before_pair(h2_14, ph2, 14, first)),
        top: e_slab(e1_top, scale_top, h2_top, h2_14[:2], y_before_pair(h2_top, ph2, top, first)),
    }
    ends = {0: (h2_0, slice(0, ROWS)), 14: (h2_14, slice(ROWS, 2 * ROWS)), top: (h2_top, slice(2 * ROWS, 3 * ROWS))}
    for value, at in ends.values():
        for c in range(3):
            h_out[c, at, :] = value[c][:ROWS]
    send(h_out.at[:, pl.ds(0, ROWS), :], h_to.at[:, pl.ds(0, ROWS), :])
    send(h_out.at[:, pl.ds(ROWS, 2 * ROWS), :], h_to.at[:, pl.ds(14 * ROWS, 2 * ROWS), :])
    send(pol_out, pol_to)
    send(cur_out, cur_to)
    for z in range(SLABS):
        at = slice(z * ROWS, (z + 1) * ROWS)
        own_scale = scale[at, :]
        for c in range(3):
            value = e2[z][c][:ROWS] if z in e2 else e2_in[c, at, :]
            if z == 1 and c == 0:
                value = value + own_scale * h2_0[1][:ROWS]
            if z == 1 and c == 1:
                value = value - own_scale * h2_0[0][:ROWS]
            e_out[c, at, :] = value - own_scale * j_rows[c, at, :]
        if z % 4 == 3:
            part = pl.ds((z - 3) * ROWS, 4 * ROWS)
            send(e_out.at[:, part, :], e_to.at[:, part, :])
    for copy in started:
        copy.wait()


def on_device(
    e_field, h_field, material, inv_permittivity, block_cells, block_count,
    block_decay, block_restore, block_drive, polarization, current,
):
    slots, width = block_cells.shape
    shape = e_field.shape
    runs_all = SLABS * ROWS
    f32, i32 = jnp.float32, jnp.int32
    vmem, smem, hbm = (pl.BlockSpec(memory_space=space) for space in (pltpu.VMEM, pltpu.SMEM, pltpu.HBM))
    params = pltpu.CompilerParams(vmem_limit_bytes=VMEM_LIMIT)

    def arr(*dims, dtype=f32):
        return jax.ShapeDtypeStruct(dims, dtype)

    def call(kernel, outs, ins, name, scratch=(), in_space=vmem, out_space=vmem):
        specs = [smem if id(v) in scalars else in_space for v in ins]
        return pl.pallas_call(
            kernel, out_shape=outs, in_specs=specs, out_specs=[out_space] * len(outs), scratch_shapes=list(scratch),
            compiler_params=params, name=name,
        )(*ins)

    e, h = (v.reshape(3, runs_all, width) for v in (e_field, h_field))
    coefficients = [v.reshape(1, slots) for v in (block_decay, block_restore, block_drive)]
    flags = jnp.stack([lax.axis_index(name) > 0 for name in ("gx", "gy", "gz")]).astype(f32)
    scalars = {id(flags), id(block_count)}
    blocks, flat, ext, tile = arr(3, slots, width), arr(3, runs_all, width), arr(3, EXT, width), arr(EXT, width)
    row = arr(1, slots)
    blocks_vmem, flat_vmem = pltpu.VMEM((3, slots, width), f32), pltpu.VMEM((3, runs_all, width), f32)
    e, h, pol1, cur1, a, scale, inverse, cells, runs, decay, restore, drive, x_up, x_down = call(
        first_kernel,
        [
            flat, flat, blocks, blocks, flat, arr(runs_all, width), arr(slots, width, dtype=i32),
            arr(slots, width, dtype=i32), arr(1, slots, dtype=i32), row, row, row,
            arr(len(UP_X), SLABS, width), arr(len(DOWN_X), SLABS, width),
        ],
        [
            e, h, material.reshape(runs_all, width), inv_permittivity, block_cells, block_count, *coefficients,
            polarization, current,
        ],
        "first",
        [
            pltpu.VMEM((runs_all, width), i32), pltpu.SMEM(inv_permittivity.shape, f32), blocks_vmem, blocks_vmem,
            blocks_vmem, flat_vmem, pltpu.VMEM((1, slots), i32), pltpu.SMEM((1, slots), i32),
            pltpu.SemaphoreType.DMA((11,)),
        ],
        in_space=hbm,
    )
    x_below, x_above = passed_along(x_up, "gx", 1), passed_along(x_down, "gx", -1)
    (own,) = call(own_kernel, [arr(FIELDS, ROWS, width)], [e, h, a, scale], "own")
    halo, pe, pscale, ph1, pe1, y_up, y_down = call(
        faces_kernel,
        [arr(FIELDS, SLABS * HALO, width), ext, tile, ext, ext, tile, tile],
        [x_below, x_above, own, flags],
        "faces",
    )
    y_below, y_above = passed_along(y_up, "gy", 1), passed_along(y_down, "gy", -1)
    pe, pscale, ph1, pe1, h1_ends, e1_ends, z_up, z_down = call(
        ends_kernel,
        [ext, tile, ext, ext, arr(3, 3, EXT, width), arr(3, 2, EXT, width), arr(7, EXT, width), arr(6, EXT, width)],
        [e, h, a, scale, halo, pe, pscale, ph1, pe1, y_below, y_above, flags],
        "ends",
    )
    z_below, z_above = passed_along(z_up, "gz", 1), passed_along(z_down, "gz", -1)
    slabs = (3, SLABS, EXT, width)
    e1, h2, e2 = call(
        middle_kernel,
        [arr(*slabs), flat, flat],
        [e, h, a, scale, halo, pe, pscale, ph1, pe1, h1_ends, flags],
        "middle",
        [pltpu.VMEM(slabs, f32), pltpu.VMEM(slabs, f32)],
    )
    scalars.add(id(runs))
    e_out, h_out, pol2, cur2 = call(
        last_kernel,
        [flat, flat, blocks, blocks],
        [
            e, scale, halo, z_below, z_above, flags, pe, pscale, ph1, pe1, h1_ends, e1_ends, e1, h2, e2,
            inverse, runs, cells, block_count, decay, restore, drive, pol1, cur1,
        ],
        "last",
        [
            flat_vmem, pltpu.VMEM((3, 3 * ROWS, width), f32), blocks_vmem, blocks_vmem,
            pltpu.VMEM((3, SLABS * EXT, width), f32), blocks_vmem, flat_vmem, pltpu.SemaphoreType.DMA((9,)),
        ],
        out_space=hbm,
    )
    return e_out.reshape(shape), h_out.reshape(shape), pol2, cur2


def solution(mesh):
    grid = P(None, "gz", "gx", "gy")
    rows = ("gx", "gy", "gz")
    return jax.shard_map(
        on_device,
        mesh=mesh,
        in_specs=(
            grid, grid, P("gz", "gx", "gy"), P(), P(rows, None), P(rows), P(rows), P(rows), P(rows),
            P(None, rows, None), P(None, rows, None),
        ),
        out_specs=(grid, grid, P(None, rows, None), P(None, rows, None)),
        check_vma=False,
    )
```

```python
import jax
import jax.numpy as jnp
from jax import lax
from jax.experimental import pallas as pl
from jax.experimental.pallas import tpu as pltpu
from jax.sharding import PartitionSpec as P

TIME_STEP = 0.5
VMEM_LIMIT = 32 * 1024 * 1024

SLABS, ROWS, HALO, LANES, COLUMNS = 16, 32, 8, 128, 7
EXT = ROWS + HALO

FIELDS = 10
UP_X = [(f, 30, 6) for f in (0, 1, 2, 4, 5)] + [(f, 31, 7) for f in range(FIELDS)]
DOWN_X = [(f, 0, 0) for f in (0, 1, 2, 3, 4, 5, 7, 8, 9)] + [(f, 1, 1) for f in (1, 2)]


def swapped(value, axis, first):
    pairs = [(k, k + 1) for k in range(first, lax.axis_size(axis) - 1, 2)]
    return lax.ppermute(value, axis, pairs + [(upper, lower) for lower, upper in pairs])


def is_even(flags, axis):
    return flags[3 + axis] > 0.5


def to_swap(even, even_out, odd_out, up, down):
    for i, value in enumerate(up):
        if i < len(down):
            even_out[i] = jnp.where(even, value, down[i])
            odd_out[i] = jnp.where(even, down[i], value)
        else:
            even_out[i] = value
            odd_out[i] = value


class Swapped:
    def __init__(self, even, when_even, when_odd):
        self.even, self.when_even, self.when_odd = even, when_even, when_odd

    def __getitem__(self, at):
        return jnp.where(self.even, self.when_even[at], self.when_odd[at])


def lanes_by(value, shift):
    shift = shift % LANES
    return pltpu.roll(value, shift, 1) if shift else value


def x_next(value):
    return pltpu.roll(value, EXT - 1, 0)


def x_before(value):
    return pltpu.roll(value, 1, 0)


def lane_ids(rows=EXT):
    return lax.broadcasted_iota(jnp.int32, (rows, LANES), 1)


def column_of(packed, z, slot, lane):
    return lanes_by(packed, lane - ((z + 1) * COLUMNS + slot))


def row_factor(flags):
    row = lax.broadcasted_iota(jnp.int32, (EXT, LANES), 0)
    return jnp.where(row >= ROWS + 4, TIME_STEP * flags[0], TIME_STEP)


def packed_places(rows=EXT):
    lane = lane_ids(rows)
    z_at = lax.shift_right_logical(lane * 9363, 16)
    return z_at, lane - z_at * COLUMNS


def h_slab(h, e, e_above, e_y, factor):
    return (
        h[0] - factor * ((e_y[1] - e[2]) - (e_above[1] - e[1])),
        h[1] - factor * ((e_above[0] - e[0]) - (x_next(e[2]) - e[2])),
        h[2] - factor * ((x_next(e[1]) - e[1]) - (e_y[0] - e[0])),
    )


def e_slab(a, scale, h, h_below, h_y):
    return (
        a[0] + scale * ((h[2] - h_y[1]) - (h[1] - h_below[1])),
        a[1] + scale * ((h[0] - h_below[0]) - (h[2] - x_before(h[2]))),
        a[2] + scale * ((h[1] - x_before(h[1])) - (h[0] - h_y[0])),
    )


def y_next_pair(e, packed_e, z, last):
    return tuple(
        jnp.where(last, column_of(packed_e[c], z, 5, LANES - 1), lanes_by(e[c], -1)) for c in (0, 2)
    )


def y_before_pair(h, packed_h, z, first):
    return tuple(jnp.where(first, column_of(packed_h[c], z, 1, 0), lanes_by(h[c], 1)) for c in (0, 2))


def as_column(row_ref, eye):
    return jnp.sum(jnp.where(eye, row_ref[...], 0.0), axis=1, keepdims=True)


def advance_blocks(e, pitch, cells, inverse, runs, count, decay, restore, drive, pol, cur, pol_out, cur_out, rows, j_rows):
    slots, width = cells.shape
    for b in range(slots):
        run = runs[0, b]
        at = run + lax.shift_right_logical(run, 5) * (pitch - ROWS)
        for comp in range(3):
            rows[comp, pl.ds(b, 1), :] = e[comp, pl.ds(at, 1), :]
    j_rows[...] = jnp.zeros_like(j_rows)
    offsets = lax.bitwise_and(cells[...], width - 1)
    down = lax.broadcasted_iota(jnp.int32, (slots, width), 0)
    across = lax.broadcasted_iota(jnp.int32, (slots, width), 1)
    eye = down == across
    live = down < count[0]
    decay_c, restore_c, drive_c = (as_column(ref, eye) for ref in (decay, restore, drive))
    back = inverse[...]
    for comp in range(3):
        at_cells = jnp.take_along_axis(rows[comp], offsets, axis=1)
        held, polar = cur[comp], pol[comp]
        new = jnp.where(live, decay_c * held - restore_c * polar + drive_c * at_cells, held)
        cur_out[comp] = new
        pol_out[comp] = jnp.where(live, polar + TIME_STEP * new, polar)
        rows[comp] = jnp.take_along_axis(jnp.where(live, new, 0.0), back, axis=1)
    for b in range(slots):
        run = runs[0, b]
        for comp in range(3):
            j_rows[comp, pl.ds(run, 1), :] = rows[comp, pl.ds(b, 1), :]


def spread(value):
    return value * 0x01010101


def invert_rows(offsets, lane):
    words = jnp.full(lane.shape, -0x7F7F7F80, jnp.int32)
    for t, part in enumerate(offsets):
        words = lax.bitwise_or(words, lax.shift_left(lax.bitwise_and(part - lane, LANES - 1), 8 * t))
    low, high = {}, {}
    for s in range(1, LANES):
        misses = lax.bitwise_xor(pltpu.roll(words, s, 1), spread(s)) - spread(1)
        for table, at in ((low, s % 8), (high, s // 8)):
            table[at] = lax.bitwise_and(table[at], misses) if at in table else misses
    found = jnp.zeros(lane.shape, jnp.int32)
    for bit in range(7):
        table, mask = (low, 1 << bit) if bit < 3 else (high, 1 << (bit - 3))
        every = None
        for at, value in table.items():
            if at & mask:
                every = value if every is None else lax.bitwise_and(every, value)
        hit = lax.bitwise_and(lax.shift_right_logical(lax.bitwise_xor(every, -1), 7), spread(1))
        found = lax.bitwise_or(found, lax.shift_left(hit, bit))
    return [
        lax.bitwise_and(lane - lax.bitwise_and(lax.shift_right_logical(found, 8 * t), LANES - 1), LANES - 1)
        for t in range(len(offsets))
    ]


def first_kernel(
    e_in, h_in, material_in, inv_perm_in, cells_in, count, decay_in, restore_in, drive_in, pol_in, cur_in, flags,
    e, h, pol_out, cur_out, a_out, scale_out, inverse_out, cells, runs_out, decay, restore, drive, up_out, down_out,
    material, inv_perm, pol, cur, rows, j_rows, run_row, runs, sems,
):
    copies = {}
    for i, (name, source, target) in enumerate(
        (
            ("cells", cells_in, cells), ("inv_perm", inv_perm_in, inv_perm), ("material", material_in, material),
            ("decay", decay_in, decay), ("restore", restore_in, restore), ("drive", drive_in, drive),
            ("e", e_in, e), ("cur", cur_in, cur), ("pol", pol_in, pol), ("h", h_in, h),
        )
    ):
        copies[name] = pltpu.make_async_copy(source, target, sems.at[i])
        copies[name].start()
    slots, width = cells.shape
    down = lax.broadcasted_iota(jnp.int32, (slots, width), 0)
    across = lax.broadcasted_iota(jnp.int32, (slots, width), 1)
    lane = lane_ids(8)
    copies["cells"].wait()
    run_of = lax.shift_right_logical(cells[...], 7)
    run_row[...] = jnp.sum(jnp.where(down == across, run_of, 0), axis=0, keepdims=True)
    runs_out[...] = run_row[...]
    copy = pltpu.make_async_copy(run_row, runs, sems.at[10])
    copy.start()
    for row in range(0, slots, 32):
        parts = [lax.bitwise_and(cells[row + 8 * t : row + 8 * t + 8, :], width - 1) for t in range(4)]
        for t, part in enumerate(invert_rows(parts, lane)):
            inverse_out[row + 8 * t : row + 8 * t + 8, :] = part
    copies["inv_perm"].wait()
    copies["material"].wait()
    table = jnp.zeros((8, width), jnp.float32)
    for kind in range(inv_perm.shape[0]):
        table = jnp.where(lane == kind, TIME_STEP * inv_perm[kind], table)
    for row in range(0, material.shape[0], 8):
        scale_out[row : row + 8, :] = jnp.take_along_axis(table, material[row : row + 8, :], axis=1)
    for name in ("decay", "restore", "drive", "e", "cur", "pol"):
        copies[name].wait()
    copy.wait()
    advance_blocks(
        e, ROWS, cells, inverse_out, runs, count, decay, restore, drive, pol, cur, pol_out, cur_out, rows, j_rows
    )
    for comp in range(3):
        a_out[comp] = e[comp] - scale_out[...] * j_rows[comp]
    copies["h"].wait()

    def plane(f, x):
        at = pl.ds(x, SLABS, stride=ROWS)
        if f == 9:
            return scale_out[at, :]
        return (e, h, a_out)[f // 3][f % 3, at, :]

    up, down = ([plane(f, x) for f, x, _ in planes] for planes in (UP_X, DOWN_X))
    to_swap(is_even(flags, 0), up_out, down_out, up, down)


def pack_tiles(tile, tiles):
    lane = lane_ids(8)
    z_at, slot = packed_places(8)
    low = jnp.logical_or(slot == 2, slot == 3)
    inside = jnp.logical_and(z_at >= 1, z_at <= SLABS)
    low, high = jnp.logical_and(low, inside), jnp.logical_and(slot >= 5, inside)
    tops = [jnp.zeros((8, LANES), jnp.float32) for _ in range(tiles)]
    bottoms = list(tops)
    for z in range(SLABS):
        place = (z + 1) * COLUMNS + 5
        top_at, bottom_at = lane >= place, lane >= place + 2
        for t in range(tiles):
            moved = lanes_by(tile(z, t), place - (LANES - 2))
            tops[t] = jnp.where(top_at, moved, tops[t])
            bottoms[t] = jnp.where(bottom_at, moved, bottoms[t])
    return [
        jnp.where(high, top, jnp.where(low, lanes_by(bottom, -5), 0.0)) for top, bottom in zip(tops, bottoms)
    ]


def own_kernel(e, h, a, scale, own_out):
    for f in range(FIELDS):
        def tile(z, t):
            at = slice(z * ROWS + t * 8, z * ROWS + t * 8 + 8)
            return scale[at, :] if f == 9 else (e, h, a)[f // 3][f % 3, at, :]

        for t, value in enumerate(pack_tiles(tile, ROWS // 8)):
            own_out[f, t * 8 : t * 8 + 8, :] = value


UP_E0X, UP_E0Y, UP_E0Y_2, UP_H1Y = 1, 2, 3, 4
DOWN_H1Y = 1


def faces_kernel(got_first, got_second, own, flags, halo_out, pe_out, pscale_out, ph1_out, pe1_out, up_out, down_out):
    even = is_even(flags, 0)
    from_above, from_below = Swapped(even, got_first, got_second), Swapped(even, got_second, got_first)
    halo_out[...] = jnp.zeros_like(halo_out)
    for got, planes in ((from_below, UP_X), (from_above, DOWN_X)):
        for i, (f, _, row) in enumerate(planes):
            halo_out[f, pl.ds(row, SLABS, stride=HALO), :] = got[i]
    packed = []
    for f in range(FIELDS):
        (tile,) = pack_tiles(lambda z, t: halo_out[f, z * HALO : z * HALO + 8, :], 1)
        packed.append(jnp.concatenate([own[f], tile], axis=0))
    z_at, slot = packed_places()
    inside = jnp.logical_and(z_at >= 1, z_at <= SLABS)
    factor = jnp.where(inside, row_factor(flags), 0.0)
    factor = jnp.where(jnp.logical_or(slot >= 5, jnp.logical_or(slot == 2, slot == 3)), factor, 0.0)
    pe, pscale = packed[0:3], packed[9]
    ph1 = packed_h(packed[3:6], pe, factor)
    pe1 = e_slab(
        packed[6:9], pscale, ph1, (lanes_by(ph1[0], COLUMNS), lanes_by(ph1[1], COLUMNS)),
        (lanes_by(ph1[0], 1), lanes_by(ph1[2], 1)),
    )
    for c in range(3):
        pe_out[c], ph1_out[c], pe1_out[c] = pe[c], ph1[c], pe1[c]
    pscale_out[...] = pscale
    up = jnp.zeros((EXT, LANES), jnp.float32)
    for i, value in enumerate((ph1[0], ph1[2], *pe1, pscale)):
        up = jnp.where(slot == i, lanes_by(value, i - 6), up)
    for z_to, value, slot_from, z_from in (
        (UP_E0X, pe[0], 6, 1), (UP_E0Y, pe[1], 6, 1), (UP_E0Y_2, pe[1], 5, 1), (UP_H1Y, ph1[1], 6, SLABS),
    ):
        here = jnp.logical_and(slot == 6, z_at == z_to)
        up = jnp.where(here, lanes_by(value, 6 - slot_from + (z_to - z_from) * COLUMNS), up)
    low = jnp.zeros((EXT, LANES), jnp.float32)
    for i, value in enumerate((pe1[0], pe1[2], pscale, pe[0], pe[2], pe[1])):
        low = jnp.where(slot == i, lanes_by(value, i - 2), low)
    here = jnp.logical_and(slot == 6, z_at == DOWN_H1Y)
    low = jnp.where(here, lanes_by(ph1[1], 4 + (DOWN_H1Y - SLABS) * COLUMNS), low)
    to_swap(is_even(flags, 1), up_out, down_out, [up], [low])


def slab_reader(e, h, a, scale, halo):
    def read(f, z):
        if f == 9:
            own = scale[z * ROWS : (z + 1) * ROWS, :]
        else:
            own = (e, h, a)[f // 3][f % 3, z * ROWS : (z + 1) * ROWS, :]
        return jnp.concatenate([own, halo[f, z * HALO : (z + 1) * HALO, :]], axis=0)

    return read


def packed_h(h, e, factor):
    return h_slab(
        h, e, (lanes_by(e[0], -COLUMNS), lanes_by(e[1], -COLUMNS)), (lanes_by(e[0], -1), lanes_by(e[2], -1)), factor
    )


END_H = (0, 14, 15)
END_E = (0, 15)


def ends_kernel(
    e, h, a, scale, halo, pe_in, pscale_in, ph1_in, pe1_in, got_first, got_second, flags,
    pe_out, pscale_out, ph1_out, pe1_out, h1_out, e1_out, up_out, down_out,
):
    z_at, slot = packed_places()
    inside = jnp.logical_and(z_at >= 1, z_at <= SLABS)
    factor = row_factor(flags)
    packed_factor = jnp.where(slot < 2, factor * flags[1], factor)
    packed_factor = jnp.where(inside, packed_factor, 0.0)
    even = is_even(flags, 1)
    up_got, down_got = Swapped(even, got_second, got_first)[0], Swapped(even, got_first, got_second)[0]
    last_low, first_high = slot == 1, slot == 5

    def columns(value, low=None, high=None):
        value = jnp.where(slot == 2, value, jnp.where(slot == 4, lanes_by(value, -2), 0.0))
        if low is not None:
            value = jnp.where(last_low, lanes_by(up_got, 1 - low), value)
        if high is not None:
            value = jnp.where(first_high, lanes_by(down_got, 5 - high), value)
        return jnp.where(inside, value, 0.0)

    def single(got, slot_to, z_to, z_from, value):
        here = jnp.logical_and(slot == slot_to, z_at == z_to)
        return jnp.where(here, lanes_by(got, slot_to - 6 + (z_to - z_from) * COLUMNS), value)

    pe = [columns(pe_in[0], None, 3), columns(pe_in[1], None, 5), columns(pe_in[2], None, 4)]
    pe[0] = single(up_got, 1, 1, UP_E0X, pe[0])
    pe[1] = single(up_got, 1, 1, UP_E0Y, pe[1])
    pe[1] = single(up_got, 0, 1, UP_E0Y_2, pe[1])
    pscale = columns(pscale_in[...], 5, 2)
    ph1 = [columns(ph1_in[0], 0), columns(ph1_in[1]), columns(ph1_in[2], 1)]
    ph1[1] = single(up_got, 1, SLABS, UP_H1Y, ph1[1])
    ph1[1] = single(down_got, 5, SLABS, DOWN_H1Y, ph1[1])
    pe1 = [columns(pe1_in[0], 2, 0), columns(pe1_in[1], 3), columns(pe1_in[2], 4, 1)]
    upper = jnp.logical_or(slot == 1, slot == 4)
    lower = jnp.logical_or(slot == 2, slot == 5)
    step = jnp.where(upper, packed_factor, 0.0)
    pdx = -(step * lanes_by(pe[2], -1))
    pdz = step * lanes_by(pe[0], -1)
    ph1[0], ph1[2] = ph1[0] + pdx, ph1[2] + pdz
    px = jnp.where(lower, lanes_by(ph1[0], 1), 0.0)
    pz = jnp.where(lower, lanes_by(ph1[2], 1), 0.0)
    pe1[0] = pe1[0] + pscale * (pdz - pz)
    pe1[1] = pe1[1] + pscale * ((pdx - lanes_by(pdx, COLUMNS)) - (pdz - x_before(pdz)))
    pe1[2] = pe1[2] + pscale * (px - pdx)
    for c in range(3):
        pe_out[c], ph1_out[c], pe1_out[c] = pe[c], ph1[c], pe1[c]
    pscale_out[...] = pscale
    read = slab_reader(e, h, a, scale, halo)
    lane = lane_ids()
    first, last = lane == 0, lane == LANES - 1
    zero = jnp.zeros((EXT, LANES), jnp.float32)
    made = {}
    for i, z in enumerate(END_H):
        ez = [read(c, z) for c in range(3)]
        above = (read(0, z + 1), read(1, z + 1)) if z < SLABS - 1 else (zero, zero)
        made[z] = h_slab([read(3 + c, z) for c in range(3)], ez, above, y_next_pair(ez, pe, z, last), factor)
        for c in range(3):
            h1_out[c, i] = made[z][c]
    ends = {}
    for i, z in enumerate(END_E):
        below = made[z - 1][:2] if z else (zero, zero)
        ends[z] = e_slab(
            [read(6 + c, z) for c in range(3)], read(9, z), made[z], below, y_before_pair(made[z], ph1, z, first)
        )
        for c in range(3):
            e1_out[c, i] = ends[z][c]
    top = SLABS - 1
    up = [made[top][0], made[top][1], *ends[top], read(9, top)]
    packed_up = [ph1[0], ph1[1], *pe1, pscale]
    low = [ends[0][0], ends[0][1], read(9, 0), read(0, 0), read(1, 0)]
    packed_down = [pe1[0], pe1[1], pscale, pe[0], pe[1]]
    for slabs, columns, z_from in ((up, packed_up, SLABS), (low, packed_down, 1)):
        together = zero
        for i, column in enumerate(columns):
            together = jnp.where(z_at == i, lanes_by(column, (i - z_from) * COLUMNS), together)
        slabs.insert(0, together)
    to_swap(is_even(flags, 2), up_out, down_out, up, low)


def middle_kernel(
    e, h, a, scale, halo, pe_in, pscale, ph1_in, pe1_in, h1_in, flags,
    e1_out, h2_out, e2_out, h1, h2,
):
    z_at, slot = packed_places()
    factor = row_factor(flags)
    packed_factor = jnp.where(slot < 2, factor * flags[1], factor)
    pe, ph1, pe1 = ([ref[c] for c in range(3)] for ref in (pe_in, ph1_in, pe1_in))
    read = slab_reader(e, h, a, scale, halo)
    lane = lane_ids()
    first, last = lane == 0, lane == LANES - 1
    zero = jnp.zeros((EXT, LANES), jnp.float32)

    def h1_of(c, z):
        return h1_in[c, END_H.index(z)] if z in END_H else h1[c, z]

    for z in range(1, 14):
        ez = [read(c, z) for c in range(3)]
        new = h_slab(
            [read(3 + c, z) for c in range(3)], ez, (read(0, z + 1), read(1, z + 1)), y_next_pair(ez, pe, z, last), factor
        )
        for c in range(3):
            h1[c, z] = new[c]
    for z in range(1, 15):
        hz = [h1_of(c, z) for c in range(3)]
        new = e_slab(
            [read(6 + c, z) for c in range(3)], read(9, z), hz, (h1_of(0, z - 1), h1_of(1, z - 1)),
            y_before_pair(hz, ph1, z, first),
        )
        for c in range(3):
            e1_out[c, z] = new[c]
    ph2 = packed_h(ph1, pe1, packed_factor)
    for z in range(1, 14):
        ez = [e1_out[c, z] for c in range(3)]
        new = h_slab(
            [h1[c, z] for c in range(3)], ez, (e1_out[0, z + 1], e1_out[1, z + 1]), y_next_pair(ez, pe1, z, last), factor
        )
        for c in range(3):
            h2[c, z] = new[c]
            h2_out[c, z * ROWS : (z + 1) * ROWS, :] = new[c][:ROWS]
    for z in range(1, 14):
        hz = [h2[c, z] for c in range(3)]
        below = (h2[0, z - 1], h2[1, z - 1]) if z > 1 else (zero, zero)
        new = e_slab(
            [e1_out[c, z] for c in range(3)], read(9, z), hz, below, y_before_pair(hz, ph2, z, first)
        )
        for c in range(3):
            e2_out[c, z * ROWS : (z + 1) * ROWS, :] = new[c][:ROWS]


def last_kernel(
    e, scale, halo, got_first, got_second, flags, pe_in, pscale_in, ph1_in, pe1_in, h1_in, e1_ends, e1_in, h2_in, e2_in,
    inverse, runs, cells, count, decay, restore, drive, pol, cur,
    e_to, h_to, pol_to, cur_to, e_out, h_out, pol_out, cur_out, e1, rows, j_rows, sems,
):
    started = []

    def send(source, target):
        copy = pltpu.make_async_copy(source, target, sems.at[len(started)])
        copy.start()
        started.append(copy)

    even = is_even(flags, 2)
    from_above, from_below = Swapped(even, got_first, got_second), Swapped(even, got_second, got_first)
    middle = pl.ds(ROWS, 13 * ROWS)
    send(h2_in.at[:, middle, :], h_to.at[:, middle, :])
    z_at, slot = packed_places()
    factor = row_factor(flags)
    below_factor = factor * flags[2]
    packed_factor = jnp.where(slot < 2, factor * flags[1], factor)
    packed_factor = jnp.where(z_at == 0, packed_factor * flags[2], packed_factor)
    packed_factor = jnp.where(z_at <= SLABS, packed_factor, 0.0)
    lane = lane_ids()
    first, last = lane == 0, lane == LANES - 1
    top = SLABS - 1

    def field(f, z):
        if f == 9:
            own = scale[z * ROWS : (z + 1) * ROWS, :]
        else:
            own = e[f, z * ROWS : (z + 1) * ROWS, :]
        return jnp.concatenate([own, halo[f, z * HALO : (z + 1) * HALO, :]], axis=0)

    below_columns, above_columns = from_below[0], from_above[0]

    def columns_below(i):
        return jnp.where(z_at == 0, lanes_by(below_columns, -i * COLUMNS), 0.0)

    def columns_above(i):
        return jnp.where(z_at == SLABS + 1, lanes_by(above_columns, (SLABS + 1 - i) * COLUMNS), 0.0)

    in_z = jnp.logical_and(z_at >= 1, z_at <= SLABS)
    far_e = [columns_above(3 + c) + jnp.where(z_at == 1, pe_in[c], 0.0) for c in range(2)]
    pdx = packed_factor * lanes_by(far_e[1], -COLUMNS)
    pdy = -(packed_factor * lanes_by(far_e[0], -COLUMNS))
    ph1 = [
        jnp.where(in_z, ph1_in[0], columns_below(0)) + pdx,
        jnp.where(in_z, ph1_in[1], columns_below(1)) + pdy,
        ph1_in[2],
    ]
    pscale = jnp.where(in_z, pscale_in[...], columns_below(5) + columns_above(2))
    edge = jnp.logical_or(z_at == 1, z_at == SLABS + 1)
    px = jnp.where(edge, lanes_by(ph1[0], COLUMNS), 0.0)
    py = jnp.where(edge, lanes_by(ph1[1], COLUMNS), 0.0)
    pe1 = [
        jnp.where(in_z, pe1_in[0], columns_below(2) + columns_above(0)) + pscale * (py - pdy),
        jnp.where(in_z, pe1_in[1], columns_below(3) + columns_above(1)) + pscale * (pdx - px),
        jnp.where(in_z, pe1_in[2], columns_below(4))
        + pscale * ((pdy - x_before(pdy)) - (pdx - lanes_by(pdx, 1))),
    ]
    ph2 = packed_h(ph1, pe1, packed_factor)

    def shifted_curl(dx, dy, z):
        dx_before = jnp.where(first, column_of(pdx, z, 1, 0), lanes_by(dx, 1))
        return (dy - x_before(dy)) - (dx - dx_before)

    dx, dy = factor * from_above[5], -(factor * from_above[4])
    h1_top = [h1_in[0, 2] + dx, h1_in[1, 2] + dy, h1_in[2, 2]]
    scale_top = field(9, top)
    e1_top = [
        e1_ends[0, 1] - scale_top * dy,
        e1_ends[1, 1] + scale_top * dx,
        e1_ends[2, 1] + scale_top * shifted_curl(dx, dy, top),
    ]
    e1_over = (from_above[1] + from_above[3] * h1_top[1], from_above[2] - from_above[3] * h1_top[0])
    dx, dy = below_factor * field(1, 0), -(below_factor * field(0, 0))
    h1_under = (from_below[1] + dx, from_below[2] + dy)
    scale_under = from_below[6]
    e1_under = [
        from_below[3] - scale_under * dy,
        from_below[4] + scale_under * dx,
        from_below[5] + scale_under * shifted_curl(dx, dy, -1),
    ]
    scale_0 = field(9, 0)
    e1_0 = [
        e1_ends[0, 0] + scale_0 * h1_under[1],
        e1_ends[1, 0] - scale_0 * h1_under[0],
        e1_ends[2, 0],
    ]
    for c in range(3):
        e1[c, 0:EXT, :] = e1_0[c]
        e1[c, top * EXT : (top + 1) * EXT, :] = e1_top[c]
        for z in range(1, top):
            e1[c, z * EXT : z * EXT + ROWS, :] = e1_in[c, z][:ROWS]
    advance_blocks(
        e1, EXT, cells, inverse, runs, count, decay, restore, drive, pol, cur, pol_out, cur_out, rows, j_rows
    )

    e1_1, e1_14 = ([e1_in[c, z] for c in range(3)] for z in (1, 14))
    under = h_slab(
        (*h1_under, h1_under[0]), e1_under, e1_0[:2], y_next_pair(e1_under, pe1, -1, last), below_factor
    )[:2]
    h2_0 = h_slab([h1_in[c, 0] for c in range(3)], e1_0, e1_1[:2], y_next_pair(e1_0, pe1, 0, last), factor)
    h2_14 = h_slab([h1_in[c, 1] for c in range(3)], e1_14, e1_top[:2], y_next_pair(e1_14, pe1, 14, last), factor)
    h2_top = h_slab(h1_top, e1_top, e1_over, y_next_pair(e1_top, pe1, top, last), factor)
    pad = jnp.zeros((HALO, LANES), jnp.float32)
    h2_13 = tuple(jnp.concatenate([h2_in[c, 13 * ROWS : 14 * ROWS, :], pad], axis=0) for c in range(2))
    e2 = {
        0: e_slab(e1_0, scale_0, h2_0, under, y_before_pair(h2_0, ph2, 0, first)),
        14: e_slab(e1_14, field(9, 14), h2_14, h2_13, y_before_pair(h2_14, ph2, 14, first)),
        top: e_slab(e1_top, scale_top, h2_top, h2_14[:2], y_before_pair(h2_top, ph2, top, first)),
    }
    ends = {0: (h2_0, slice(0, ROWS)), 14: (h2_14, slice(ROWS, 2 * ROWS)), top: (h2_top, slice(2 * ROWS, 3 * ROWS))}
    for value, at in ends.values():
        for c in range(3):
            h_out[c, at, :] = value[c][:ROWS]
    send(h_out.at[:, pl.ds(0, ROWS), :], h_to.at[:, pl.ds(0, ROWS), :])
    send(h_out.at[:, pl.ds(ROWS, 2 * ROWS), :], h_to.at[:, pl.ds(14 * ROWS, 2 * ROWS), :])
    send(pol_out, pol_to)
    send(cur_out, cur_to)
    for z in range(SLABS):
        at = slice(z * ROWS, (z + 1) * ROWS)
        own_scale = scale[at, :]
        for c in range(3):
            value = e2[z][c][:ROWS] if z in e2 else e2_in[c, at, :]
            if z == 1 and c == 0:
                value = value + own_scale * h2_0[1][:ROWS]
            if z == 1 and c == 1:
                value = value - own_scale * h2_0[0][:ROWS]
            e_out[c, at, :] = value - own_scale * j_rows[c, at, :]
        if z % 4 == 3:
            part = pl.ds((z - 3) * ROWS, 4 * ROWS)
            send(e_out.at[:, part, :], e_to.at[:, part, :])
    for copy in started:
        copy.wait()


def on_device(
    e_field, h_field, material, inv_permittivity, block_cells, block_count,
    block_decay, block_restore, block_drive, polarization, current,
):
    slots, width = block_cells.shape
    shape = e_field.shape
    runs_all = SLABS * ROWS
    f32, i32 = jnp.float32, jnp.int32
    vmem, smem, hbm = (pl.BlockSpec(memory_space=space) for space in (pltpu.VMEM, pltpu.SMEM, pltpu.HBM))
    params = pltpu.CompilerParams(vmem_limit_bytes=VMEM_LIMIT)

    def arr(*dims, dtype=f32):
        return jax.ShapeDtypeStruct(dims, dtype)

    def call(kernel, outs, ins, name, scratch=(), in_space=vmem, out_space=vmem):
        specs = [smem if id(v) in scalars else in_space for v in ins]
        return pl.pallas_call(
            kernel, out_shape=outs, in_specs=specs, out_specs=[out_space] * len(outs), scratch_shapes=list(scratch),
            compiler_params=params, name=name,
        )(*ins)

    def in_hbm(value):
        return pltpu.with_memory_space_constraint(value, pltpu.HBM)

    e, h = (v.reshape(3, runs_all, width) for v in (e_field, h_field))
    coefficients = [v.reshape(1, slots) for v in (block_decay, block_restore, block_drive)]
    place = [lax.axis_index(name) for name in ("gx", "gy", "gz")]
    flags = jnp.stack([k > 0 for k in place] + [k % 2 == 0 for k in place]).astype(f32)
    scalars = {id(flags), id(block_count)}
    blocks, flat, ext, tile = arr(3, slots, width), arr(3, runs_all, width), arr(3, EXT, width), arr(EXT, width)
    row = arr(1, slots)
    blocks_vmem, flat_vmem = pltpu.VMEM((3, slots, width), f32), pltpu.VMEM((3, runs_all, width), f32)
    e, h, pol1, cur1, a, scale, inverse, cells, runs, decay, restore, drive, x_first, x_second = call(
        first_kernel,
        [
            flat, flat, blocks, blocks, flat, arr(runs_all, width), arr(slots, width, dtype=i32),
            arr(slots, width, dtype=i32), arr(1, slots, dtype=i32), row, row, row,
            arr(len(UP_X), SLABS, width), arr(len(UP_X), SLABS, width),
        ],
        [
            *(in_hbm(v) for v in (e, h, material.reshape(runs_all, width), inv_permittivity, block_cells)), block_count,
            *(in_hbm(v) for v in (*coefficients, polarization, current)), flags,
        ],
        "first",
        [
            pltpu.VMEM((runs_all, width), i32), pltpu.SMEM(inv_permittivity.shape, f32), blocks_vmem, blocks_vmem,
            blocks_vmem, flat_vmem, pltpu.VMEM((1, slots), i32), pltpu.SMEM((1, slots), i32),
            pltpu.SemaphoreType.DMA((11,)),
        ],
        in_space=hbm,
    )
    x_first, x_second = swapped(x_first, "gx", 0), swapped(x_second, "gx", 1)
    (own,) = call(own_kernel, [arr(FIELDS, ROWS, width)], [e, h, a, scale], "own")
    halo, pe, pscale, ph1, pe1, y_first, y_second = call(
        faces_kernel,
        [arr(FIELDS, SLABS * HALO, width), ext, tile, ext, ext, arr(1, EXT, width), arr(1, EXT, width)],
        [x_first, x_second, own, flags],
        "faces",
    )
    y_first, y_second = swapped(y_first, "gy", 0), swapped(y_second, "gy", 1)
    pe, pscale, ph1, pe1, h1_ends, e1_ends, z_first, z_second = call(
        ends_kernel,
        [ext, tile, ext, ext, arr(3, 3, EXT, width), arr(3, 2, EXT, width), arr(7, EXT, width), arr(7, EXT, width)],
        [e, h, a, scale, halo, pe, pscale, ph1, pe1, y_first, y_second, flags],
        "ends",
    )
    z_first, z_second = swapped(z_first, "gz", 0), swapped(z_second, "gz", 1)
    slabs = (3, SLABS, EXT, width)
    e1, h2, e2 = call(
        middle_kernel,
        [arr(*slabs), flat, flat],
        [e, h, a, scale, halo, pe, pscale, ph1, pe1, h1_ends, flags],
        "middle",
        [pltpu.VMEM(slabs, f32), pltpu.VMEM(slabs, f32)],
    )
    scalars.add(id(runs))
    e_out, h_out, pol2, cur2 = call(
        last_kernel,
        [flat, flat, blocks, blocks],
        [
            e, scale, halo, z_first, z_second, flags, pe, pscale, ph1, pe1, h1_ends, e1_ends, e1, h2, e2,
            inverse, runs, cells, block_count, decay, restore, drive, pol1, cur1,
        ],
        "last",
        [
            flat_vmem, pltpu.VMEM((3, 3 * ROWS, width), f32), blocks_vmem, blocks_vmem,
            pltpu.VMEM((3, SLABS * EXT, width), f32), blocks_vmem, flat_vmem, pltpu.SemaphoreType.DMA((9,)),
        ],
        out_space=hbm,
    )
    return e_out.reshape(shape), h_out.reshape(shape), pol2, cur2


def solution(mesh):
    grid = P(None, "gz", "gx", "gy")
    rows = ("gx", "gy", "gz")
    return jax.shard_map(
        on_device,
        mesh=mesh,
        in_specs=(
            grid, grid, P("gz", "gx", "gy"), P(), P(rows, None), P(rows), P(rows), P(rows), P(rows),
            P(None, rows, None), P(None, rows, None),
        ),
        out_specs=(grid, grid, P(None, rows, None), P(None, rows, None)),
        check_vma=False,
    )
```

```python
import jax
import jax.numpy as jnp
from jax import lax
from jax.experimental import pallas as pl
from jax.experimental.pallas import tpu as pltpu
from jax.sharding import PartitionSpec as P

TIME_STEP = 0.5
VMEM_LIMIT = 32 * 1024 * 1024

SLABS, ROWS, HALO, LANES, COLUMNS = 16, 32, 8, 128, 7
EXT = ROWS + HALO

FIELDS = 10
UP_X = [(f, 30, 6) for f in (0, 1, 2, 4, 5)] + [(f, 31, 7) for f in range(FIELDS)]
DOWN_X = [(f, 0, 0) for f in (0, 1, 2, 3, 4, 5, 7, 8, 9)] + [(f, 1, 1) for f in (1, 2)]


def swapped(value, axis, first):
    pairs = [(k, k + 1) for k in range(first, lax.axis_size(axis) - 1, 2)]
    return lax.ppermute(value, axis, pairs + [(upper, lower) for lower, upper in pairs])


def is_even(flags, axis):
    return flags[3 + axis] > 0.5


def to_swap(even, even_out, odd_out, up, down):
    for i, value in enumerate(up):
        if i < len(down):
            even_out[i] = jnp.where(even, value, down[i])
            odd_out[i] = jnp.where(even, down[i], value)
        else:
            even_out[i] = value
            odd_out[i] = value


class Swapped:
    def __init__(self, even, when_even, when_odd):
        self.even, self.when_even, self.when_odd = even, when_even, when_odd

    def __getitem__(self, at):
        return jnp.where(self.even, self.when_even[at], self.when_odd[at])


def lanes_by(value, shift):
    shift = shift % LANES
    return pltpu.roll(value, shift, 1) if shift else value


def x_next(value):
    return pltpu.roll(value, EXT - 1, 0)


def x_before(value):
    return pltpu.roll(value, 1, 0)


def lane_ids(rows=EXT):
    return lax.broadcasted_iota(jnp.int32, (rows, LANES), 1)


def column_of(packed, z, slot, lane):
    return lanes_by(packed, lane - ((z + 1) * COLUMNS + slot))


def row_factor(flags):
    row = lax.broadcasted_iota(jnp.int32, (EXT, LANES), 0)
    return jnp.where(row >= ROWS + 4, TIME_STEP * flags[0], TIME_STEP)


def packed_places(rows=EXT):
    lane = lane_ids(rows)
    z_at = lax.shift_right_logical(lane * 9363, 16)
    return z_at, lane - z_at * COLUMNS


def h_slab(h, e, e_above, e_y, factor):
    return (
        h[0] - factor * ((e_y[1] - e[2]) - (e_above[1] - e[1])),
        h[1] - factor * ((e_above[0] - e[0]) - (x_next(e[2]) - e[2])),
        h[2] - factor * ((x_next(e[1]) - e[1]) - (e_y[0] - e[0])),
    )


def e_slab(a, scale, h, h_below, h_y):
    return (
        a[0] + scale * ((h[2] - h_y[1]) - (h[1] - h_below[1])),
        a[1] + scale * ((h[0] - h_below[0]) - (h[2] - x_before(h[2]))),
        a[2] + scale * ((h[1] - x_before(h[1])) - (h[0] - h_y[0])),
    )


def y_next_pair(e, packed_e, z, last):
    return tuple(
        jnp.where(last, column_of(packed_e[c], z, 5, LANES - 1), lanes_by(e[c], -1)) for c in (0, 2)
    )


def y_before_pair(h, packed_h, z, first):
    return tuple(jnp.where(first, column_of(packed_h[c], z, 1, 0), lanes_by(h[c], 1)) for c in (0, 2))


def as_column(row_ref, eye):
    return jnp.sum(jnp.where(eye, row_ref[...], 0.0), axis=1, keepdims=True)


def gather_rows(e, pitch, runs, rows):
    for b in range(rows.shape[1]):
        run = runs[0, b]
        at = run + lax.shift_right_logical(run, 5) * (pitch - ROWS)
        for comp in range(3):
            rows[comp, pl.ds(b, 1), :] = e[comp, pl.ds(at, 1), :]


def advance_blocks(cells, inverse, runs, count, decay, restore, drive, pol, cur, pol_out, cur_out, rows, j_rows):
    slots, width = cells.shape
    offsets = lax.bitwise_and(cells[...], width - 1)
    down = lax.broadcasted_iota(jnp.int32, (slots, width), 0)
    across = lax.broadcasted_iota(jnp.int32, (slots, width), 1)
    eye = down == across
    live = down < count[0]
    decay_c, restore_c, drive_c = (as_column(ref, eye) for ref in (decay, restore, drive))
    back = inverse[...]
    for comp in range(3):
        at_cells = jnp.take_along_axis(rows[comp], offsets, axis=1)
        held, polar = cur[comp], pol[comp]
        new = jnp.where(live, decay_c * held - restore_c * polar + drive_c * at_cells, held)
        cur_out[comp] = new
        pol_out[comp] = jnp.where(live, polar + TIME_STEP * new, polar)
        rows[comp] = jnp.take_along_axis(jnp.where(live, new, 0.0), back, axis=1)
    for b in range(slots):
        run = runs[0, b]
        for comp in range(3):
            j_rows[comp, pl.ds(run, 1), :] = rows[comp, pl.ds(b, 1), :]
    return jnp.where(live, drive_c, 0.0)


def spread(value):
    return value * 0x01010101


def invert_rows(offsets, lane):
    words = jnp.full(lane.shape, -0x7F7F7F80, jnp.int32)
    for t, part in enumerate(offsets):
        words = lax.bitwise_or(words, lax.shift_left(lax.bitwise_and(part - lane, LANES - 1), 8 * t))
    low, high = {}, {}
    for s in range(1, LANES):
        misses = lax.bitwise_xor(pltpu.roll(words, s, 1), spread(s)) - spread(1)
        for table, at in ((low, s % 8), (high, s // 8)):
            table[at] = lax.bitwise_and(table[at], misses) if at in table else misses
    found = jnp.zeros(lane.shape, jnp.int32)
    for bit in range(7):
        table, mask = (low, 1 << bit) if bit < 3 else (high, 1 << (bit - 3))
        every = None
        for at, value in table.items():
            if at & mask:
                every = value if every is None else lax.bitwise_and(every, value)
        hit = lax.bitwise_and(lax.shift_right_logical(lax.bitwise_xor(every, -1), 7), spread(1))
        found = lax.bitwise_or(found, lax.shift_left(hit, bit))
    return [
        lax.bitwise_and(lane - lax.bitwise_and(lax.shift_right_logical(found, 8 * t), LANES - 1), LANES - 1)
        for t in range(len(offsets))
    ]


def first_kernel(
    e_in, h_in, material_in, inv_perm_in, cells_in, count, decay_in, restore_in, drive_in, pol_in, cur_in, flags,
    e, h, pol_out, cur_out, a_out, scale_out, inverse_out, cells, runs_out, decay, restore, drive, up_out, down_out,
    material, inv_perm, pol, cur, rows, j_rows, run_row, runs, sems,
):
    copies = {}
    for i, (name, source, target) in enumerate(
        (
            ("cells", cells_in, cells), ("inv_perm", inv_perm_in, inv_perm), ("material", material_in, material),
            ("decay", decay_in, decay), ("restore", restore_in, restore), ("drive", drive_in, drive),
            ("e", e_in, e), ("cur", cur_in, cur), ("pol", pol_in, pol), ("h", h_in, h),
        )
    ):
        copies[name] = pltpu.make_async_copy(source, target, sems.at[i])
        copies[name].start()
    slots, width = cells.shape
    down = lax.broadcasted_iota(jnp.int32, (slots, width), 0)
    across = lax.broadcasted_iota(jnp.int32, (slots, width), 1)
    lane = lane_ids(8)
    j_rows[...] = jnp.zeros_like(j_rows)
    copies["cells"].wait()
    run_of = lax.shift_right_logical(cells[...], 7)
    run_row[...] = jnp.sum(jnp.where(down == across, run_of, 0), axis=0, keepdims=True)
    runs_out[...] = run_row[...]
    copy = pltpu.make_async_copy(run_row, runs, sems.at[10])
    copy.start()
    def invert(row):
        parts = [lax.bitwise_and(cells[row + 8 * t : row + 8 * t + 8, :], width - 1) for t in range(4)]
        for t, part in enumerate(invert_rows(parts, lane)):
            inverse_out[row + 8 * t : row + 8 * t + 8, :] = part

    for row in range(0, slots // 2, 32):
        invert(row)
    copies["e"].wait()
    copy.wait()
    gather_rows(e, ROWS, runs, rows)
    for row in range(slots // 2, slots, 32):
        invert(row)
    copies["inv_perm"].wait()
    copies["material"].wait()
    table = jnp.zeros((8, width), jnp.float32)
    for kind in range(inv_perm.shape[0]):
        table = jnp.where(lane == kind, TIME_STEP * inv_perm[kind], table)
    for row in range(0, material.shape[0], 8):
        scale_out[row : row + 8, :] = jnp.take_along_axis(table, material[row : row + 8, :], axis=1)
    for name in ("decay", "restore", "drive", "cur", "pol"):
        copies[name].wait()
    advance_blocks(
        cells, inverse_out, runs, count, decay, restore, drive, pol, cur, pol_out, cur_out, rows, j_rows
    )
    for comp in range(3):
        a_out[comp] = e[comp] - scale_out[...] * j_rows[comp]
    copies["h"].wait()

    def plane(f, x):
        at = pl.ds(x, SLABS, stride=ROWS)
        if f == 9:
            return scale_out[at, :]
        return (e, h, a_out)[f // 3][f % 3, at, :]

    up, down = ([plane(f, x) for f, x, _ in planes] for planes in (UP_X, DOWN_X))
    to_swap(is_even(flags, 0), up_out, down_out, up, down)


def pack_tiles(tile, tiles):
    lane = lane_ids(8)
    z_at, slot = packed_places(8)
    low = jnp.logical_or(slot == 2, slot == 3)
    inside = jnp.logical_and(z_at >= 1, z_at <= SLABS)
    low, high = jnp.logical_and(low, inside), jnp.logical_and(slot >= 5, inside)
    tops = [jnp.zeros((8, LANES), jnp.float32) for _ in range(tiles)]
    bottoms = list(tops)
    for z in range(SLABS):
        place = (z + 1) * COLUMNS + 5
        top_at, bottom_at = lane >= place, lane >= place + 2
        for t in range(tiles):
            moved = lanes_by(tile(z, t), place - (LANES - 2))
            tops[t] = jnp.where(top_at, moved, tops[t])
            bottoms[t] = jnp.where(bottom_at, moved, bottoms[t])
    return [
        jnp.where(high, top, jnp.where(low, lanes_by(bottom, -5), 0.0)) for top, bottom in zip(tops, bottoms)
    ]


def own_kernel(e, h, a, scale, own_out):
    for f in range(FIELDS):
        def tile(z, t):
            at = slice(z * ROWS + t * 8, z * ROWS + t * 8 + 8)
            return scale[at, :] if f == 9 else (e, h, a)[f // 3][f % 3, at, :]

        for t, value in enumerate(pack_tiles(tile, ROWS // 8)):
            own_out[f, t * 8 : t * 8 + 8, :] = value


UP_E0X, UP_E0Y, UP_E0Y_2, UP_H1Y = 1, 2, 3, 4
DOWN_H1Y = 1


def faces_kernel(got_first, got_second, own, flags, halo_out, pe_out, pscale_out, ph1_out, pe1_out, up_out, down_out):
    even = is_even(flags, 0)
    from_above, from_below = Swapped(even, got_first, got_second), Swapped(even, got_second, got_first)
    halo_out[...] = jnp.zeros_like(halo_out)
    for got, planes in ((from_below, UP_X), (from_above, DOWN_X)):
        for i, (f, _, row) in enumerate(planes):
            halo_out[f, pl.ds(row, SLABS, stride=HALO), :] = got[i]
    packed = []
    for f in range(FIELDS):
        (tile,) = pack_tiles(lambda z, t: halo_out[f, z * HALO : z * HALO + 8, :], 1)
        packed.append(jnp.concatenate([own[f], tile], axis=0))
    z_at, slot = packed_places()
    inside = jnp.logical_and(z_at >= 1, z_at <= SLABS)
    factor = jnp.where(inside, row_factor(flags), 0.0)
    factor = jnp.where(jnp.logical_or(slot >= 5, jnp.logical_or(slot == 2, slot == 3)), factor, 0.0)
    pe, pscale = packed[0:3], packed[9]
    ph1 = packed_h(packed[3:6], pe, factor)
    pe1 = e_slab(
        packed[6:9], pscale, ph1, (lanes_by(ph1[0], COLUMNS), lanes_by(ph1[1], COLUMNS)),
        (lanes_by(ph1[0], 1), lanes_by(ph1[2], 1)),
    )
    for c in range(3):
        pe_out[c], ph1_out[c], pe1_out[c] = pe[c], ph1[c], pe1[c]
    pscale_out[...] = pscale
    up = jnp.zeros((EXT, LANES), jnp.float32)
    for i, value in enumerate((ph1[0], ph1[2], *pe1, pscale)):
        up = jnp.where(slot == i, lanes_by(value, i - 6), up)
    for z_to, value, slot_from, z_from in (
        (UP_E0X, pe[0], 6, 1), (UP_E0Y, pe[1], 6, 1), (UP_E0Y_2, pe[1], 5, 1), (UP_H1Y, ph1[1], 6, SLABS),
    ):
        here = jnp.logical_and(slot == 6, z_at == z_to)
        up = jnp.where(here, lanes_by(value, 6 - slot_from + (z_to - z_from) * COLUMNS), up)
    low = jnp.zeros((EXT, LANES), jnp.float32)
    for i, value in enumerate((pe1[0], pe1[2], pscale, pe[0], pe[2], pe[1])):
        low = jnp.where(slot == i, lanes_by(value, i - 2), low)
    here = jnp.logical_and(slot == 6, z_at == DOWN_H1Y)
    low = jnp.where(here, lanes_by(ph1[1], 4 + (DOWN_H1Y - SLABS) * COLUMNS), low)
    to_swap(is_even(flags, 1), up_out, down_out, [up], [low])


def slab_reader(e, h, a, scale, halo):
    def read(f, z):
        if f == 9:
            own = scale[z * ROWS : (z + 1) * ROWS, :]
        else:
            own = (e, h, a)[f // 3][f % 3, z * ROWS : (z + 1) * ROWS, :]
        return jnp.concatenate([own, halo[f, z * HALO : (z + 1) * HALO, :]], axis=0)

    return read


def packed_h(h, e, factor):
    return h_slab(
        h, e, (lanes_by(e[0], -COLUMNS), lanes_by(e[1], -COLUMNS)), (lanes_by(e[0], -1), lanes_by(e[2], -1)), factor
    )


END_H = (0, 14, 15)
END_E = (0, 15)


def ends_kernel(
    e, h, a, scale, halo, pe_in, pscale_in, ph1_in, pe1_in, got_first, got_second, flags,
    pe_out, pscale_out, ph1_out, pe1_out, h1_out, e1_out, up_out, down_out,
):
    z_at, slot = packed_places()
    inside = jnp.logical_and(z_at >= 1, z_at <= SLABS)
    factor = row_factor(flags)
    packed_factor = jnp.where(slot < 2, factor * flags[1], factor)
    packed_factor = jnp.where(inside, packed_factor, 0.0)
    even = is_even(flags, 1)
    up_got, down_got = Swapped(even, got_second, got_first)[0], Swapped(even, got_first, got_second)[0]
    last_low, first_high = slot == 1, slot == 5

    def columns(value, low=None, high=None):
        value = jnp.where(slot == 2, value, jnp.where(slot == 4, lanes_by(value, -2), 0.0))
        if low is not None:
            value = jnp.where(last_low, lanes_by(up_got, 1 - low), value)
        if high is not None:
            value = jnp.where(first_high, lanes_by(down_got, 5 - high), value)
        return jnp.where(inside, value, 0.0)

    def single(got, slot_to, z_to, z_from, value):
        here = jnp.logical_and(slot == slot_to, z_at == z_to)
        return jnp.where(here, lanes_by(got, slot_to - 6 + (z_to - z_from) * COLUMNS), value)

    pe = [columns(pe_in[0], None, 3), columns(pe_in[1], None, 5), columns(pe_in[2], None, 4)]
    pe[0] = single(up_got, 1, 1, UP_E0X, pe[0])
    pe[1] = single(up_got, 1, 1, UP_E0Y, pe[1])
    pe[1] = single(up_got, 0, 1, UP_E0Y_2, pe[1])
    pscale = columns(pscale_in[...], 5, 2)
    ph1 = [columns(ph1_in[0], 0), columns(ph1_in[1]), columns(ph1_in[2], 1)]
    ph1[1] = single(up_got, 1, SLABS, UP_H1Y, ph1[1])
    ph1[1] = single(down_got, 5, SLABS, DOWN_H1Y, ph1[1])
    pe1 = [columns(pe1_in[0], 2, 0), columns(pe1_in[1], 3), columns(pe1_in[2], 4, 1)]
    upper = jnp.logical_or(slot == 1, slot == 4)
    lower = jnp.logical_or(slot == 2, slot == 5)
    step = jnp.where(upper, packed_factor, 0.0)
    pdx = -(step * lanes_by(pe[2], -1))
    pdz = step * lanes_by(pe[0], -1)
    ph1[0], ph1[2] = ph1[0] + pdx, ph1[2] + pdz
    px = jnp.where(lower, lanes_by(ph1[0], 1), 0.0)
    pz = jnp.where(lower, lanes_by(ph1[2], 1), 0.0)
    pe1[0] = pe1[0] + pscale * (pdz - pz)
    pe1[1] = pe1[1] + pscale * ((pdx - lanes_by(pdx, COLUMNS)) - (pdz - x_before(pdz)))
    pe1[2] = pe1[2] + pscale * (px - pdx)
    for c in range(3):
        pe_out[c], ph1_out[c], pe1_out[c] = pe[c], ph1[c], pe1[c]
    pscale_out[...] = pscale
    read = slab_reader(e, h, a, scale, halo)
    lane = lane_ids()
    first, last = lane == 0, lane == LANES - 1
    zero = jnp.zeros((EXT, LANES), jnp.float32)
    made = {}
    for i, z in enumerate(END_H):
        ez = [read(c, z) for c in range(3)]
        above = (read(0, z + 1), read(1, z + 1)) if z < SLABS - 1 else (zero, zero)
        made[z] = h_slab([read(3 + c, z) for c in range(3)], ez, above, y_next_pair(ez, pe, z, last), factor)
        for c in range(3):
            h1_out[c, i] = made[z][c]
    ends = {}
    for i, z in enumerate(END_E):
        below = made[z - 1][:2] if z else (zero, zero)
        ends[z] = e_slab(
            [read(6 + c, z) for c in range(3)], read(9, z), made[z], below, y_before_pair(made[z], ph1, z, first)
        )
        for c in range(3):
            e1_out[c, i] = ends[z][c]
    top = SLABS - 1
    up = [made[top][0], made[top][1], *ends[top], read(9, top)]
    packed_up = [ph1[0], ph1[1], *pe1, pscale]
    low = [ends[0][0], ends[0][1], read(9, 0), read(0, 0), read(1, 0)]
    packed_down = [pe1[0], pe1[1], pscale, pe[0], pe[1]]
    for slabs, columns, z_from in ((up, packed_up, SLABS), (low, packed_down, 1)):
        together = zero
        for i, column in enumerate(columns):
            together = jnp.where(z_at == i, lanes_by(column, (i - z_from) * COLUMNS), together)
        slabs.insert(0, together)
    to_swap(is_even(flags, 2), up_out, down_out, up, low)


def middle_kernel(
    e, h, a, scale, halo, pe_in, pscale, ph1_in, pe1_in, h1_in, e1_in, flags,
    e1_out, h2_out, e2_out, h1, h2,
):
    z_at, slot = packed_places()
    factor = row_factor(flags)
    packed_factor = jnp.where(slot < 2, factor * flags[1], factor)
    pe, ph1, pe1 = ([ref[c] for c in range(3)] for ref in (pe_in, ph1_in, pe1_in))
    read = slab_reader(e, h, a, scale, halo)
    lane = lane_ids()
    first, last = lane == 0, lane == LANES - 1
    zero = jnp.zeros((EXT, LANES), jnp.float32)

    def h1_of(c, z):
        return h1_in[c, END_H.index(z)] if z in END_H else h1[c, z]

    for z in range(1, 14):
        ez = [read(c, z) for c in range(3)]
        new = h_slab(
            [read(3 + c, z) for c in range(3)], ez, (read(0, z + 1), read(1, z + 1)), y_next_pair(ez, pe, z, last), factor
        )
        for c in range(3):
            h1[c, z] = new[c]
    for z in range(1, 15):
        hz = [h1_of(c, z) for c in range(3)]
        new = e_slab(
            [read(6 + c, z) for c in range(3)], read(9, z), hz, (h1_of(0, z - 1), h1_of(1, z - 1)),
            y_before_pair(hz, ph1, z, first),
        )
        for c in range(3):
            e1_out[c, z] = new[c]
    for i, z in enumerate(END_E):
        for c in range(3):
            e1_out[c, z] = e1_in[c, i]
    ph2 = packed_h(ph1, pe1, packed_factor)
    for z in range(1, 14):
        ez = [e1_out[c, z] for c in range(3)]
        new = h_slab(
            [h1[c, z] for c in range(3)], ez, (e1_out[0, z + 1], e1_out[1, z + 1]), y_next_pair(ez, pe1, z, last), factor
        )
        for c in range(3):
            h2[c, z] = new[c]
            h2_out[c, z * ROWS : (z + 1) * ROWS, :] = new[c][:ROWS]
    for z in range(1, 14):
        hz = [h2[c, z] for c in range(3)]
        below = (h2[0, z - 1], h2[1, z - 1]) if z > 1 else (zero, zero)
        new = e_slab(
            [e1_out[c, z] for c in range(3)], read(9, z), hz, below, y_before_pair(hz, ph2, z, first)
        )
        for c in range(3):
            e2_out[c, z * ROWS : (z + 1) * ROWS, :] = new[c][:ROWS]


def blocks_kernel(
    scale, e1, h2, e2, inverse, runs, cells, count, decay, restore, drive, pol, cur,
    e_to, h_to, pol_out, cur_out, e_rest, j_rest, gain_out, e_out, rows, j_rows, gain_rows, sems,
):
    middle = pl.ds(ROWS, 13 * ROWS)
    h_copy = pltpu.make_async_copy(h2.at[:, middle, :], h_to.at[:, middle, :], sems.at[0])
    h_copy.start()
    gather_rows(e1, EXT, runs, rows)
    j_rows[...] = jnp.zeros_like(j_rows)
    gain = advance_blocks(
        cells, inverse, runs, count, decay, restore, drive, pol, cur, pol_out, cur_out, rows, j_rows
    )
    gain_rows[...] = jnp.broadcast_to(gain, gain_rows.shape)
    gain_out[...] = jnp.zeros_like(gain_out)
    for b in range(gain_rows.shape[0]):
        gain_out[pl.ds(runs[0, b], 1), :] = gain_rows[pl.ds(b, 1), :]
    for c in range(3):
        for z in range(2, 14):
            at = slice(z * ROWS, (z + 1) * ROWS)
            e_out[c, at, :] = e2[c, at, :] - scale[at, :] * j_rows[c, at, :]
        for i, z in enumerate(END_SLABS):
            at = slice(z * ROWS, (z + 1) * ROWS)
            j_rest[c, i] = j_rows[c, at, :]
        e_rest[c] = e2[c, ROWS : 2 * ROWS, :]
    most = pl.ds(2 * ROWS, 12 * ROWS)
    e_copy = pltpu.make_async_copy(e_out.at[:, most, :], e_to.at[:, most, :], sems.at[1])
    e_copy.start()
    h_copy.wait()
    e_copy.wait()


END_SLABS = (0, 1, 14, 15)


def last_kernel(
    e, scale, halo, got_first, got_second, flags, pe_in, pscale_in, ph1_in, pe1_in, h1_in, e1_ends, e1_in, h2_in,
    e_most, h_most, e_rest, j_rest, gains, runs, cells, pol, cur,
    e_to, h_to, pol_to, cur_to, e_out, h_out, pol_out, cur_out, late, rows, gain_rows, sems,
):
    started = []

    def send(source, target):
        copy = pltpu.make_async_copy(source, target, sems.at[len(started)])
        copy.start()
        started.append(copy)

    even = is_even(flags, 2)
    from_above, from_below = Swapped(even, got_first, got_second), Swapped(even, got_second, got_first)
    z_at, slot = packed_places()
    factor = row_factor(flags)
    below_factor = factor * flags[2]
    packed_factor = jnp.where(slot < 2, factor * flags[1], factor)
    packed_factor = jnp.where(z_at == 0, packed_factor * flags[2], packed_factor)
    packed_factor = jnp.where(z_at <= SLABS, packed_factor, 0.0)
    lane = lane_ids()
    first, last = lane == 0, lane == LANES - 1
    top = SLABS - 1

    def field(f, z):
        if f == 9:
            own = scale[z * ROWS : (z + 1) * ROWS, :]
        else:
            own = e[f, z * ROWS : (z + 1) * ROWS, :]
        return jnp.concatenate([own, halo[f, z * HALO : (z + 1) * HALO, :]], axis=0)

    below_columns, above_columns = from_below[0], from_above[0]

    def columns_below(i):
        return jnp.where(z_at == 0, lanes_by(below_columns, -i * COLUMNS), 0.0)

    def columns_above(i):
        return jnp.where(z_at == SLABS + 1, lanes_by(above_columns, (SLABS + 1 - i) * COLUMNS), 0.0)

    in_z = jnp.logical_and(z_at >= 1, z_at <= SLABS)
    far_e = [columns_above(3 + c) + jnp.where(z_at == 1, pe_in[c], 0.0) for c in range(2)]
    pdx = packed_factor * lanes_by(far_e[1], -COLUMNS)
    pdy = -(packed_factor * lanes_by(far_e[0], -COLUMNS))
    ph1 = [
        jnp.where(in_z, ph1_in[0], columns_below(0)) + pdx,
        jnp.where(in_z, ph1_in[1], columns_below(1)) + pdy,
        ph1_in[2],
    ]
    pscale = jnp.where(in_z, pscale_in[...], columns_below(5) + columns_above(2))
    edge = jnp.logical_or(z_at == 1, z_at == SLABS + 1)
    px = jnp.where(edge, lanes_by(ph1[0], COLUMNS), 0.0)
    py = jnp.where(edge, lanes_by(ph1[1], COLUMNS), 0.0)
    pe1 = [
        jnp.where(in_z, pe1_in[0], columns_below(2) + columns_above(0)) + pscale * (py - pdy),
        jnp.where(in_z, pe1_in[1], columns_below(3) + columns_above(1)) + pscale * (pdx - px),
        jnp.where(in_z, pe1_in[2], columns_below(4))
        + pscale * ((pdy - x_before(pdy)) - (pdx - lanes_by(pdx, 1))),
    ]
    ph2 = packed_h(ph1, pe1, packed_factor)

    def shifted_curl(dx, dy, z):
        dx_before = jnp.where(first, column_of(pdx, z, 1, 0), lanes_by(dx, 1))
        return (dy - x_before(dy)) - (dx - dx_before)

    dx, dy = factor * from_above[5], -(factor * from_above[4])
    h1_top = [h1_in[0, 2] + dx, h1_in[1, 2] + dy, h1_in[2, 2]]
    scale_top = field(9, top)
    late_top = (-(scale_top * dy), scale_top * dx, scale_top * shifted_curl(dx, dy, top))
    e1_top = [e1_ends[c, 1] + late_top[c] for c in range(3)]
    e1_over = (from_above[1] + from_above[3] * h1_top[1], from_above[2] - from_above[3] * h1_top[0])
    dx, dy = below_factor * field(1, 0), -(below_factor * field(0, 0))
    h1_under = (from_below[1] + dx, from_below[2] + dy)
    scale_under = from_below[6]
    e1_under = [
        from_below[3] - scale_under * dy,
        from_below[4] + scale_under * dx,
        from_below[5] + scale_under * shifted_curl(dx, dy, -1),
    ]
    scale_0 = field(9, 0)
    late_0 = (scale_0 * h1_under[1], -(scale_0 * h1_under[0]))
    e1_0 = [e1_ends[0, 0] + late_0[0], e1_ends[1, 0] + late_0[1], e1_ends[2, 0]]

    late[...] = jnp.zeros_like(late)
    for c in range(3):
        if c < 2:
            late[c, 0:ROWS, :] = late_0[c][:ROWS]
        late[c, ROWS : 2 * ROWS, :] = late_top[c][:ROWS]
    for b in range(rows.shape[1]):
        run = runs[0, b]
        at = jnp.where(run < ROWS, run, jnp.where(run >= top * ROWS, run - (top - 1) * ROWS, 2 * ROWS))
        gain_rows[pl.ds(b, 1), :] = gains[pl.ds(run, 1), :]
        for c in range(3):
            rows[c, pl.ds(b, 1), :] = late[c, pl.ds(at, 1), :]
    offsets = lax.bitwise_and(cells[...], LANES - 1)
    for c in range(3):
        more = gain_rows[...] * jnp.take_along_axis(rows[c], offsets, axis=1)
        cur_out[c] = cur[c] + more
        pol_out[c] = pol[c] + TIME_STEP * more
    send(pol_out, pol_to)
    send(cur_out, cur_to)

    e1_1, e1_14 = ([e1_in[c, z] for c in range(3)] for z in (1, 14))
    under = h_slab(
        (*h1_under, h1_under[0]), e1_under, e1_0[:2], y_next_pair(e1_under, pe1, -1, last), below_factor
    )[:2]
    h2_0 = h_slab([h1_in[c, 0] for c in range(3)], e1_0, e1_1[:2], y_next_pair(e1_0, pe1, 0, last), factor)
    h2_14 = h_slab([h1_in[c, 1] for c in range(3)], e1_14, e1_top[:2], y_next_pair(e1_14, pe1, 14, last), factor)
    h2_top = h_slab(h1_top, e1_top, e1_over, y_next_pair(e1_top, pe1, top, last), factor)
    pad = jnp.zeros((HALO, LANES), jnp.float32)
    h2_13 = tuple(jnp.concatenate([h2_in[c, 13 * ROWS : 14 * ROWS, :], pad], axis=0) for c in range(2))
    e2 = {
        0: e_slab(e1_0, scale_0, h2_0, under, y_before_pair(h2_0, ph2, 0, first)),
        14: e_slab(e1_14, field(9, 14), h2_14, h2_13, y_before_pair(h2_14, ph2, 14, first)),
        top: e_slab(e1_top, scale_top, h2_top, h2_14[:2], y_before_pair(h2_top, ph2, top, first)),
    }
    ends = {0: (h2_0, slice(0, ROWS)), 14: (h2_14, slice(ROWS, 2 * ROWS)), top: (h2_top, slice(2 * ROWS, 3 * ROWS))}
    for value, at in ends.values():
        for c in range(3):
            h_out[c, at, :] = value[c][:ROWS]
    send(h_out.at[:, pl.ds(0, ROWS), :], h_to.at[:, pl.ds(0, ROWS), :])
    send(h_out.at[:, pl.ds(ROWS, 2 * ROWS), :], h_to.at[:, pl.ds(14 * ROWS, 2 * ROWS), :])
    for i, z in enumerate(END_SLABS):
        at = slice(z * ROWS, (z + 1) * ROWS)
        own_scale = scale[at, :]
        for c in range(3):
            value = e2[z][c][:ROWS] if z in e2 else e_rest[c]
            placed = j_rest[c, i]
            if z == 0 and c < 2:
                placed = placed + gains[at, :] * late_0[c][:ROWS]
            if z == top:
                placed = placed + gains[at, :] * late_top[c][:ROWS]
            if z == 1 and c == 0:
                value = value + own_scale * h2_0[1][:ROWS]
            if z == 1 and c == 1:
                value = value - own_scale * h2_0[0][:ROWS]
            e_out[c, i * ROWS : (i + 1) * ROWS, :] = value - own_scale * placed
    send(e_out.at[:, pl.ds(0, 2 * ROWS), :], e_to.at[:, pl.ds(0, 2 * ROWS), :])
    send(e_out.at[:, pl.ds(2 * ROWS, 2 * ROWS), :], e_to.at[:, pl.ds(14 * ROWS, 2 * ROWS), :])
    for copy in started:
        copy.wait()


def on_device(
    e_field, h_field, material, inv_permittivity, block_cells, block_count,
    block_decay, block_restore, block_drive, polarization, current,
):
    slots, width = block_cells.shape
    shape = e_field.shape
    runs_all = SLABS * ROWS
    f32, i32 = jnp.float32, jnp.int32
    vmem, smem, hbm = (pl.BlockSpec(memory_space=space) for space in (pltpu.VMEM, pltpu.SMEM, pltpu.HBM))
    params = pltpu.CompilerParams(vmem_limit_bytes=VMEM_LIMIT)

    def arr(*dims, dtype=f32):
        return jax.ShapeDtypeStruct(dims, dtype)

    def call(kernel, outs, ins, name, scratch=(), in_hbm=(), out_hbm=(), aliases={}):
        specs = [smem if id(v) in scalars else hbm if i in in_hbm else vmem for i, v in enumerate(ins)]
        ins = [pltpu.with_memory_space_constraint(v, pltpu.HBM) if i in in_hbm else v for i, v in enumerate(ins)]
        out_specs = [hbm if i in out_hbm else vmem for i in range(len(outs))]
        return pl.pallas_call(
            kernel, out_shape=outs, in_specs=specs, out_specs=out_specs, scratch_shapes=list(scratch),
            input_output_aliases=aliases, compiler_params=params, name=name,
        )(*ins)

    e, h = (v.reshape(3, runs_all, width) for v in (e_field, h_field))
    coefficients = [v.reshape(1, slots) for v in (block_decay, block_restore, block_drive)]
    place = [lax.axis_index(name) for name in ("gx", "gy", "gz")]
    flags = jnp.stack([k > 0 for k in place] + [k % 2 == 0 for k in place]).astype(f32)
    scalars = {id(flags), id(block_count)}
    blocks, flat, ext, tile = arr(3, slots, width), arr(3, runs_all, width), arr(3, EXT, width), arr(EXT, width)
    row = arr(1, slots)
    blocks_vmem, flat_vmem = pltpu.VMEM((3, slots, width), f32), pltpu.VMEM((3, runs_all, width), f32)
    e, h, pol1, cur1, a, scale, inverse, cells, runs, decay, restore, drive, x_first, x_second = call(
        first_kernel,
        [
            flat, flat, blocks, blocks, flat, arr(runs_all, width), arr(slots, width, dtype=i32),
            arr(slots, width, dtype=i32), arr(1, slots, dtype=i32), row, row, row,
            arr(len(UP_X), SLABS, width), arr(len(UP_X), SLABS, width),
        ],
        [
            e, h, material.reshape(runs_all, width), inv_permittivity, block_cells, block_count, *coefficients,
            polarization, current, flags,
        ],
        "first",
        [
            pltpu.VMEM((runs_all, width), i32), pltpu.SMEM(inv_permittivity.shape, f32), blocks_vmem, blocks_vmem,
            blocks_vmem, flat_vmem, pltpu.VMEM((1, slots), i32), pltpu.SMEM((1, slots), i32),
            pltpu.SemaphoreType.DMA((11,)),
        ],
        in_hbm=(0, 1, 2, 3, 4, 6, 7, 8, 9, 10),
    )
    x_first, x_second = swapped(x_first, "gx", 0), swapped(x_second, "gx", 1)
    (own,) = call(own_kernel, [arr(FIELDS, ROWS, width)], [e, h, a, scale], "own")
    halo, pe, pscale, ph1, pe1, y_first, y_second = call(
        faces_kernel,
        [arr(FIELDS, SLABS * HALO, width), ext, tile, ext, ext, arr(1, EXT, width), arr(1, EXT, width)],
        [x_first, x_second, own, flags],
        "faces",
    )
    y_first, y_second = swapped(y_first, "gy", 0), swapped(y_second, "gy", 1)
    pe, pscale, ph1, pe1, h1_ends, e1_ends, z_first, z_second = call(
        ends_kernel,
        [ext, tile, ext, ext, arr(3, 3, EXT, width), arr(3, 2, EXT, width), arr(7, EXT, width), arr(7, EXT, width)],
        [e, h, a, scale, halo, pe, pscale, ph1, pe1, y_first, y_second, flags],
        "ends",
    )
    z_first, z_second = swapped(z_first, "gz", 0), swapped(z_second, "gz", 1)
    slabs = (3, SLABS, EXT, width)
    e1, h2, e2 = call(
        middle_kernel,
        [arr(*slabs), flat, flat],
        [e, h, a, scale, halo, pe, pscale, ph1, pe1, h1_ends, e1_ends, flags],
        "middle",
        [pltpu.VMEM(slabs, f32), pltpu.VMEM(slabs, f32)],
    )
    scalars.add(id(runs))
    dma = pltpu.SemaphoreType.DMA
    e_most, h_most, pol2, cur2, e_rest, j_rest, gains = call(
        blocks_kernel,
        [flat, flat, blocks, blocks, arr(3, ROWS, width), arr(3, len(END_SLABS), ROWS, width), arr(runs_all, width)],
        [
            scale, e1.reshape(3, SLABS * EXT, width), h2, e2, inverse, runs, cells, block_count,
            decay, restore, drive, pol1, cur1,
        ],
        "blocks",
        [flat_vmem, blocks_vmem, flat_vmem, pltpu.VMEM((slots, width), f32), dma((2,))],
        out_hbm=(0, 1),
    )
    e_out, h_out, pol2, cur2 = call(
        last_kernel,
        [flat, flat, blocks, blocks],
        [
            e, scale, halo, z_first, z_second, flags, pe, pscale, ph1, pe1, h1_ends, e1_ends, e1, h2,
            e_most, h_most, e_rest, j_rest, gains, runs, cells, pol2, cur2,
        ],
        "last",
        [
            pltpu.VMEM((3, 4 * ROWS, width), f32), pltpu.VMEM((3, 3 * ROWS, width), f32), blocks_vmem, blocks_vmem,
            pltpu.VMEM((3, 2 * ROWS + 8, width), f32), blocks_vmem, pltpu.VMEM((slots, width), f32), dma((6,)),
        ],
        in_hbm=(14, 15),
        out_hbm=(0, 1, 2, 3),
        aliases={14: 0, 15: 1},
    )
    return e_out.reshape(shape), h_out.reshape(shape), pol2, cur2


def solution(mesh):
    grid = P(None, "gz", "gx", "gy")
    rows = ("gx", "gy", "gz")
    return jax.shard_map(
        on_device,
        mesh=mesh,
        in_specs=(
            grid, grid, P("gz", "gx", "gy"), P(), P(rows, None), P(rows), P(rows), P(rows), P(rows),
            P(None, rows, None), P(None, rows, None),
        ),
        out_specs=(grid, grid, P(None, rows, None), P(None, rows, None)),
        check_vma=False,
    )
```

```python
import jax
import jax.numpy as jnp
from jax import lax
from jax.experimental import pallas as pl
from jax.experimental.pallas import tpu as pltpu
from jax.sharding import PartitionSpec as P

TIME_STEP = 0.5
VMEM_LIMIT = 32 * 1024 * 1024

SLABS, ROWS, HALO, LANES, COLUMNS = 16, 32, 8, 128, 7
EXT = ROWS + HALO

FIELDS = 10
UP_X = [(f, 30, 6) for f in (0, 1, 2, 4, 5)] + [(f, 31, 7) for f in range(FIELDS)]
DOWN_X = [(f, 0, 0) for f in (0, 1, 2, 3, 4, 5, 7, 8, 9)] + [(f, 1, 1) for f in (1, 2)]


def swapped(value, axis, first):
    pairs = [(k, k + 1) for k in range(first, lax.axis_size(axis) - 1, 2)]
    return lax.ppermute(value, axis, pairs + [(upper, lower) for lower, upper in pairs])


def is_even(flags, axis):
    return flags[3 + axis] > 0.5


def to_swap(even, even_out, odd_out, up, down):
    for i, value in enumerate(up):
        if i < len(down):
            even_out[i] = jnp.where(even, value, down[i])
            odd_out[i] = jnp.where(even, down[i], value)
        else:
            even_out[i] = value
            odd_out[i] = value


class Swapped:
    def __init__(self, even, when_even, when_odd):
        self.even, self.when_even, self.when_odd = even, when_even, when_odd

    def __getitem__(self, at):
        return jnp.where(self.even, self.when_even[at], self.when_odd[at])


def lanes_by(value, shift):
    shift = shift % LANES
    return pltpu.roll(value, shift, 1) if shift else value


def x_next(value):
    return pltpu.roll(value, EXT - 1, 0)


def x_before(value):
    return pltpu.roll(value, 1, 0)


def lane_ids(rows=EXT):
    return lax.broadcasted_iota(jnp.int32, (rows, LANES), 1)


def column_of(packed, z, slot, lane):
    return lanes_by(packed, lane - ((z + 1) * COLUMNS + slot))


def row_factor(flags):
    row = lax.broadcasted_iota(jnp.int32, (EXT, LANES), 0)
    return jnp.where(row >= ROWS + 4, TIME_STEP * flags[0], TIME_STEP)


def packed_places(rows=EXT):
    lane = lane_ids(rows)
    z_at = lax.shift_right_logical(lane * 9363, 16)
    return z_at, lane - z_at * COLUMNS


def h_slab(h, e, e_above, e_y, factor):
    return (
        h[0] - factor * ((e_y[1] - e[2]) - (e_above[1] - e[1])),
        h[1] - factor * ((e_above[0] - e[0]) - (x_next(e[2]) - e[2])),
        h[2] - factor * ((x_next(e[1]) - e[1]) - (e_y[0] - e[0])),
    )


def e_slab(a, scale, h, h_below, h_y):
    return (
        a[0] + scale * ((h[2] - h_y[1]) - (h[1] - h_below[1])),
        a[1] + scale * ((h[0] - h_below[0]) - (h[2] - x_before(h[2]))),
        a[2] + scale * ((h[1] - x_before(h[1])) - (h[0] - h_y[0])),
    )


def y_next_pair(e, packed_e, z, last):
    return tuple(
        jnp.where(last, column_of(packed_e[c], z, 5, LANES - 1), lanes_by(e[c], -1)) for c in (0, 2)
    )


def y_before_pair(h, packed_h, z, first):
    return tuple(jnp.where(first, column_of(packed_h[c], z, 1, 0), lanes_by(h[c], 1)) for c in (0, 2))


def as_column(row_ref, eye):
    return jnp.sum(jnp.where(eye, row_ref[...], 0.0), axis=1, keepdims=True)


def gather_rows(e, pitch, runs, rows):
    for b in range(rows.shape[1]):
        run = runs[0, b]
        at = run + lax.shift_right_logical(run, 5) * (pitch - ROWS)
        for comp in range(3):
            rows[comp, pl.ds(b, 1), :] = e[comp, pl.ds(at, 1), :]


def advance_blocks(cells, inverse, runs, count, decay, restore, drive, pol, cur, pol_out, cur_out, rows, j_rows):
    slots, width = cells.shape
    offsets = lax.bitwise_and(cells[...], width - 1)
    down = lax.broadcasted_iota(jnp.int32, (slots, width), 0)
    across = lax.broadcasted_iota(jnp.int32, (slots, width), 1)
    eye = down == across
    live = down < count[0]
    decay_c, restore_c, drive_c = (as_column(ref, eye) for ref in (decay, restore, drive))
    back = inverse[...]
    for comp in range(3):
        at_cells = jnp.take_along_axis(rows[comp], offsets, axis=1)
        held, polar = cur[comp], pol[comp]
        new = jnp.where(live, decay_c * held - restore_c * polar + drive_c * at_cells, held)
        cur_out[comp] = new
        pol_out[comp] = jnp.where(live, polar + TIME_STEP * new, polar)
        rows[comp] = jnp.take_along_axis(jnp.where(live, new, 0.0), back, axis=1)
    for b in range(slots):
        run = runs[0, b]
        for comp in range(3):
            j_rows[comp, pl.ds(run, 1), :] = rows[comp, pl.ds(b, 1), :]
    return jnp.where(live, drive_c, 0.0)


def spread(value):
    return value * 0x01010101


def invert_rows(offsets, lane):
    words = jnp.full(lane.shape, -0x7F7F7F80, jnp.int32)
    for t, part in enumerate(offsets):
        words = lax.bitwise_or(words, lax.shift_left(lax.bitwise_and(part - lane, LANES - 1), 8 * t))
    low, high = {}, {}
    for s in range(1, LANES):
        misses = lax.bitwise_xor(pltpu.roll(words, s, 1), spread(s)) - spread(1)
        for table, at in ((low, s % 8), (high, s // 8)):
            table[at] = lax.bitwise_and(table[at], misses) if at in table else misses
    found = jnp.zeros(lane.shape, jnp.int32)
    for bit in range(7):
        table, mask = (low, 1 << bit) if bit < 3 else (high, 1 << (bit - 3))
        every = None
        for at, value in table.items():
            if at & mask:
                every = value if every is None else lax.bitwise_and(every, value)
        hit = lax.bitwise_and(lax.shift_right_logical(lax.bitwise_xor(every, -1), 7), spread(1))
        found = lax.bitwise_or(found, lax.shift_left(hit, bit))
    return [
        lax.bitwise_and(lane - lax.bitwise_and(lax.shift_right_logical(found, 8 * t), LANES - 1), LANES - 1)
        for t in range(len(offsets))
    ]


def first_kernel(
    e_in, h_in, material_in, inv_perm_in, cells_in, count, decay_in, restore_in, drive_in, pol_in, cur_in, flags,
    e, h, pol_out, cur_out, a_out, scale_out, inverse_out, cells, runs_out, decay, restore, drive, up_out, down_out,
    material, inv_perm, pol, cur, rows, j_rows, run_row, runs, sems,
):
    copies = {}
    for i, (name, source, target) in enumerate(
        (
            ("cells", cells_in, cells), ("inv_perm", inv_perm_in, inv_perm), ("material", material_in, material),
            ("decay", decay_in, decay), ("restore", restore_in, restore), ("drive", drive_in, drive),
            ("e", e_in, e), ("cur", cur_in, cur), ("pol", pol_in, pol), ("h", h_in, h),
        )
    ):
        copies[name] = pltpu.make_async_copy(source, target, sems.at[i])
        copies[name].start()
    slots, width = cells.shape
    down = lax.broadcasted_iota(jnp.int32, (slots, width), 0)
    across = lax.broadcasted_iota(jnp.int32, (slots, width), 1)
    lane = lane_ids(8)
    j_rows[...] = jnp.zeros_like(j_rows)
    copies["cells"].wait()
    run_of = lax.shift_right_logical(cells[...], 7)
    run_row[...] = jnp.sum(jnp.where(down == across, run_of, 0), axis=0, keepdims=True)
    runs_out[...] = run_row[...]
    copy = pltpu.make_async_copy(run_row, runs, sems.at[10])
    copy.start()
    for row in range(0, slots, 32):
        parts = [lax.bitwise_and(cells[row + 8 * t : row + 8 * t + 8, :], width - 1) for t in range(4)]
        for t, part in enumerate(invert_rows(parts, lane)):
            inverse_out[row + 8 * t : row + 8 * t + 8, :] = part

    copies["inv_perm"].wait()
    copies["material"].wait()
    table = jnp.zeros((8, width), jnp.float32)
    for kind in range(inv_perm.shape[0]):
        table = jnp.where(lane == kind, TIME_STEP * inv_perm[kind], table)
    for row in range(0, material.shape[0], 8):
        scale_out[row : row + 8, :] = jnp.take_along_axis(table, material[row : row + 8, :], axis=1)
    for name in ("decay", "restore", "drive", "e", "cur", "pol"):
        copies[name].wait()
    copy.wait()
    gather_rows(e, ROWS, runs, rows)
    advance_blocks(
        cells, inverse_out, runs, count, decay, restore, drive, pol, cur, pol_out, cur_out, rows, j_rows
    )
    for comp in range(3):
        a_out[comp] = e[comp] - scale_out[...] * j_rows[comp]
    copies["h"].wait()

    def plane(f, x):
        at = pl.ds(x, SLABS, stride=ROWS)
        if f == 9:
            return scale_out[at, :]
        return (e, h, a_out)[f // 3][f % 3, at, :]

    up, down = ([plane(f, x) for f, x, _ in planes] for planes in (UP_X, DOWN_X))
    to_swap(is_even(flags, 0), up_out, down_out, up, down)


def pack_tiles(tile, tiles):
    lane = lane_ids(8)
    z_at, slot = packed_places(8)
    low = jnp.logical_or(slot == 2, slot == 3)
    inside = jnp.logical_and(z_at >= 1, z_at <= SLABS)
    low, high = jnp.logical_and(low, inside), jnp.logical_and(slot >= 5, inside)
    tops = [jnp.zeros((8, LANES), jnp.float32) for _ in range(tiles)]
    bottoms = list(tops)
    for z in range(SLABS):
        place = (z + 1) * COLUMNS + 5
        top_at, bottom_at = lane >= place, lane >= place + 2
        for t in range(tiles):
            moved = lanes_by(tile(z, t), place - (LANES - 2))
            tops[t] = jnp.where(top_at, moved, tops[t])
            bottoms[t] = jnp.where(bottom_at, moved, bottoms[t])
    return [
        jnp.where(high, top, jnp.where(low, lanes_by(bottom, -5), 0.0)) for top, bottom in zip(tops, bottoms)
    ]


def own_kernel(e, h, a, scale, own_out):
    for f in range(FIELDS):
        def tile(z, t):
            at = slice(z * ROWS + t * 8, z * ROWS + t * 8 + 8)
            return scale[at, :] if f == 9 else (e, h, a)[f // 3][f % 3, at, :]

        for t, value in enumerate(pack_tiles(tile, ROWS // 8)):
            own_out[f, t * 8 : t * 8 + 8, :] = value


UP_E0X, UP_E0Y, UP_E0Y_2, UP_H1Y = 1, 2, 3, 4
DOWN_H1Y = 1


def faces_kernel(got_second, got_first, own, flags, halo_out, pe_out, pscale_out, ph1_out, pe1_out, up_out, down_out):
    even = is_even(flags, 0)
    from_above, from_below = Swapped(even, got_first, got_second), Swapped(even, got_second, got_first)
    halo_out[...] = jnp.zeros_like(halo_out)
    for got, planes in ((from_below, UP_X), (from_above, DOWN_X)):
        for i, (f, _, row) in enumerate(planes):
            halo_out[f, pl.ds(row, SLABS, stride=HALO), :] = got[i]
    packed = []
    for f in range(FIELDS):
        (tile,) = pack_tiles(lambda z, t: halo_out[f, z * HALO : z * HALO + 8, :], 1)
        packed.append(jnp.concatenate([own[f], tile], axis=0))
    z_at, slot = packed_places()
    inside = jnp.logical_and(z_at >= 1, z_at <= SLABS)
    factor = jnp.where(inside, row_factor(flags), 0.0)
    factor = jnp.where(jnp.logical_or(slot >= 5, jnp.logical_or(slot == 2, slot == 3)), factor, 0.0)
    pe, pscale = packed[0:3], packed[9]
    ph1 = packed_h(packed[3:6], pe, factor)
    pe1 = e_slab(
        packed[6:9], pscale, ph1, (lanes_by(ph1[0], COLUMNS), lanes_by(ph1[1], COLUMNS)),
        (lanes_by(ph1[0], 1), lanes_by(ph1[2], 1)),
    )
    for c in range(3):
        pe_out[c], ph1_out[c], pe1_out[c] = pe[c], ph1[c], pe1[c]
    pscale_out[...] = pscale
    up = jnp.zeros((EXT, LANES), jnp.float32)
    for i, value in enumerate((ph1[0], ph1[2], *pe1, pscale)):
        up = jnp.where(slot == i, lanes_by(value, i - 6), up)
    for z_to, value, slot_from, z_from in (
        (UP_E0X, pe[0], 6, 1), (UP_E0Y, pe[1], 6, 1), (UP_E0Y_2, pe[1], 5, 1), (UP_H1Y, ph1[1], 6, SLABS),
    ):
        here = jnp.logical_and(slot == 6, z_at == z_to)
        up = jnp.where(here, lanes_by(value, 6 - slot_from + (z_to - z_from) * COLUMNS), up)
    low = jnp.zeros((EXT, LANES), jnp.float32)
    for i, value in enumerate((pe1[0], pe1[2], pscale, pe[0], pe[2], pe[1])):
        low = jnp.where(slot == i, lanes_by(value, i - 2), low)
    here = jnp.logical_and(slot == 6, z_at == DOWN_H1Y)
    low = jnp.where(here, lanes_by(ph1[1], 4 + (DOWN_H1Y - SLABS) * COLUMNS), low)
    to_swap(is_even(flags, 1), up_out, down_out, [up], [low])


def slab_reader(e, h, a, scale, halo):
    def read(f, z):
        if f == 9:
            own = scale[z * ROWS : (z + 1) * ROWS, :]
        else:
            own = (e, h, a)[f // 3][f % 3, z * ROWS : (z + 1) * ROWS, :]
        return jnp.concatenate([own, halo[f, z * HALO : (z + 1) * HALO, :]], axis=0)

    return read


def packed_h(h, e, factor):
    return h_slab(
        h, e, (lanes_by(e[0], -COLUMNS), lanes_by(e[1], -COLUMNS)), (lanes_by(e[0], -1), lanes_by(e[2], -1)), factor
    )


END_H = (0, 14, 15)
END_E = (0, 15)


def ends_kernel(
    e, h, a, scale, halo, pe_in, pscale_in, ph1_in, pe1_in, got_second, got_first, flags,
    pe_out, pscale_out, ph1_out, pe1_out, h1_out, e1_out, up_out, down_out,
):
    z_at, slot = packed_places()
    inside = jnp.logical_and(z_at >= 1, z_at <= SLABS)
    factor = row_factor(flags)
    packed_factor = jnp.where(slot < 2, factor * flags[1], factor)
    packed_factor = jnp.where(inside, packed_factor, 0.0)
    even = is_even(flags, 1)
    up_got, down_got = Swapped(even, got_second, got_first)[0], Swapped(even, got_first, got_second)[0]
    last_low, first_high = slot == 1, slot == 5

    def columns(value, low=None, high=None):
        value = jnp.where(slot == 2, value, jnp.where(slot == 4, lanes_by(value, -2), 0.0))
        if low is not None:
            value = jnp.where(last_low, lanes_by(up_got, 1 - low), value)
        if high is not None:
            value = jnp.where(first_high, lanes_by(down_got, 5 - high), value)
        return jnp.where(inside, value, 0.0)

    def single(got, slot_to, z_to, z_from, value):
        here = jnp.logical_and(slot == slot_to, z_at == z_to)
        return jnp.where(here, lanes_by(got, slot_to - 6 + (z_to - z_from) * COLUMNS), value)

    pe = [columns(pe_in[0], None, 3), columns(pe_in[1], None, 5), columns(pe_in[2], None, 4)]
    pe[0] = single(up_got, 1, 1, UP_E0X, pe[0])
    pe[1] = single(up_got, 1, 1, UP_E0Y, pe[1])
    pe[1] = single(up_got, 0, 1, UP_E0Y_2, pe[1])
    pscale = columns(pscale_in[...], 5, 2)
    ph1 = [columns(ph1_in[0], 0), columns(ph1_in[1]), columns(ph1_in[2], 1)]
    ph1[1] = single(up_got, 1, SLABS, UP_H1Y, ph1[1])
    ph1[1] = single(down_got, 5, SLABS, DOWN_H1Y, ph1[1])
    pe1 = [columns(pe1_in[0], 2, 0), columns(pe1_in[1], 3), columns(pe1_in[2], 4, 1)]
    upper = jnp.logical_or(slot == 1, slot == 4)
    lower = jnp.logical_or(slot == 2, slot == 5)
    step = jnp.where(upper, packed_factor, 0.0)
    pdx = -(step * lanes_by(pe[2], -1))
    pdz = step * lanes_by(pe[0], -1)
    ph1[0], ph1[2] = ph1[0] + pdx, ph1[2] + pdz
    px = jnp.where(lower, lanes_by(ph1[0], 1), 0.0)
    pz = jnp.where(lower, lanes_by(ph1[2], 1), 0.0)
    pe1[0] = pe1[0] + pscale * (pdz - pz)
    pe1[1] = pe1[1] + pscale * ((pdx - lanes_by(pdx, COLUMNS)) - (pdz - x_before(pdz)))
    pe1[2] = pe1[2] + pscale * (px - pdx)
    for c in range(3):
        pe_out[c], ph1_out[c], pe1_out[c] = pe[c], ph1[c], pe1[c]
    pscale_out[...] = pscale
    read = slab_reader(e, h, a, scale, halo)
    lane = lane_ids()
    first, last = lane == 0, lane == LANES - 1
    zero = jnp.zeros((EXT, LANES), jnp.float32)
    made = {}
    for i, z in enumerate(END_H):
        ez = [read(c, z) for c in range(3)]
        above = (read(0, z + 1), read(1, z + 1)) if z < SLABS - 1 else (zero, zero)
        made[z] = h_slab([read(3 + c, z) for c in range(3)], ez, above, y_next_pair(ez, pe, z, last), factor)
        for c in range(3):
            h1_out[c, i] = made[z][c]
    ends = {}
    for i, z in enumerate(END_E):
        below = made[z - 1][:2] if z else (zero, zero)
        ends[z] = e_slab(
            [read(6 + c, z) for c in range(3)], read(9, z), made[z], below, y_before_pair(made[z], ph1, z, first)
        )
        for c in range(3):
            e1_out[c, i] = ends[z][c]
    top = SLABS - 1
    up = [made[top][0], made[top][1], *ends[top], read(9, top)]
    packed_up = [ph1[0], ph1[1], *pe1, pscale]
    low = [ends[0][0], ends[0][1], read(9, 0), read(0, 0), read(1, 0)]
    packed_down = [pe1[0], pe1[1], pscale, pe[0], pe[1]]
    for slabs, columns, z_from in ((up, packed_up, SLABS), (low, packed_down, 1)):
        together = zero
        for i, column in enumerate(columns):
            together = jnp.where(z_at == i, lanes_by(column, (i - z_from) * COLUMNS), together)
        slabs.insert(0, together)
    to_swap(is_even(flags, 2), up_out, down_out, up, low)


def middle_kernel(
    e, h, a, scale, halo, pe_in, pscale, ph1_in, pe1_in, h1_in, e1_in, flags,
    e1_out, h2_out, e2_out, h1, h2,
):
    z_at, slot = packed_places()
    factor = row_factor(flags)
    packed_factor = jnp.where(slot < 2, factor * flags[1], factor)
    pe, ph1, pe1 = ([ref[c] for c in range(3)] for ref in (pe_in, ph1_in, pe1_in))
    read = slab_reader(e, h, a, scale, halo)
    lane = lane_ids()
    first, last = lane == 0, lane == LANES - 1
    zero = jnp.zeros((EXT, LANES), jnp.float32)

    def h1_of(c, z):
        return h1_in[c, END_H.index(z)] if z in END_H else h1[c, z]

    for z in range(1, 14):
        ez = [read(c, z) for c in range(3)]
        new = h_slab(
            [read(3 + c, z) for c in range(3)], ez, (read(0, z + 1), read(1, z + 1)), y_next_pair(ez, pe, z, last), factor
        )
        for c in range(3):
            h1[c, z] = new[c]
    for z in range(1, 15):
        hz = [h1_of(c, z) for c in range(3)]
        new = e_slab(
            [read(6 + c, z) for c in range(3)], read(9, z), hz, (h1_of(0, z - 1), h1_of(1, z - 1)),
            y_before_pair(hz, ph1, z, first),
        )
        for c in range(3):
            e1_out[c, z] = new[c]
    for i, z in enumerate(END_E):
        for c in range(3):
            e1_out[c, z] = e1_in[c, i]
    ph2 = packed_h(ph1, pe1, packed_factor)
    for z in range(1, 14):
        ez = [e1_out[c, z] for c in range(3)]
        new = h_slab(
            [h1[c, z] for c in range(3)], ez, (e1_out[0, z + 1], e1_out[1, z + 1]), y_next_pair(ez, pe1, z, last), factor
        )
        for c in range(3):
            h2[c, z] = new[c]
            h2_out[c, z * ROWS : (z + 1) * ROWS, :] = new[c][:ROWS]
    for z in range(1, 14):
        hz = [h2[c, z] for c in range(3)]
        below = (h2[0, z - 1], h2[1, z - 1]) if z > 1 else (zero, zero)
        new = e_slab(
            [e1_out[c, z] for c in range(3)], read(9, z), hz, below, y_before_pair(hz, ph2, z, first)
        )
        for c in range(3):
            e2_out[c, z * ROWS : (z + 1) * ROWS, :] = new[c][:ROWS]


def blocks_kernel(
    scale, e1, e2, inverse, runs, cells, count, decay, restore, drive, pol, cur,
    e_most, pol_out, cur_out, j_rest, gain_out, rows, j_rows, gain_rows,
):
    gather_rows(e1, EXT, runs, rows)
    j_rows[...] = jnp.zeros_like(j_rows)
    gain = advance_blocks(
        cells, inverse, runs, count, decay, restore, drive, pol, cur, pol_out, cur_out, rows, j_rows
    )
    gain_rows[...] = jnp.broadcast_to(gain, gain_rows.shape)
    gain_out[...] = jnp.zeros_like(gain_out)
    for b in range(gain_rows.shape[0]):
        gain_out[pl.ds(runs[0, b], 1), :] = gain_rows[pl.ds(b, 1), :]
    for c in range(3):
        for z in range(2, 14):
            at = slice(z * ROWS, (z + 1) * ROWS)
            e_most[c, (z - 2) * ROWS : (z - 1) * ROWS, :] = e2[c, at, :] - scale[at, :] * j_rows[c, at, :]
        for i, z in enumerate(END_SLABS):
            at = slice(z * ROWS, (z + 1) * ROWS)
            j_rest[c, i] = j_rows[c, at, :]


END_SLABS = (0, 1, 14, 15)


def last_kernel(
    e, scale, halo, got_first, got_second, flags, pe_in, pscale_in, ph1_in, pe1_in, h1_in, e1_ends, e1_in, h2_in, e2_in,
    e_most, j_rest, gains, runs, cells, pol, cur,
    e_to, h_to, pol_to, cur_to, e_out, h_out, pol_out, cur_out, late, rows, gain_rows, sems,
):
    started = []

    def send(source, target):
        copy = pltpu.make_async_copy(source, target, sems.at[len(started)])
        copy.start()
        started.append(copy)

    send(h2_in.at[:, pl.ds(ROWS, 13 * ROWS), :], h_to.at[:, pl.ds(ROWS, 13 * ROWS), :])
    send(e_most, e_to.at[:, pl.ds(2 * ROWS, 12 * ROWS), :])
    even = is_even(flags, 2)
    from_above, from_below = Swapped(even, got_first, got_second), Swapped(even, got_second, got_first)
    z_at, slot = packed_places()
    factor = row_factor(flags)
    below_factor = factor * flags[2]
    packed_factor = jnp.where(slot < 2, factor * flags[1], factor)
    packed_factor = jnp.where(z_at == 0, packed_factor * flags[2], packed_factor)
    packed_factor = jnp.where(z_at <= SLABS, packed_factor, 0.0)
    lane = lane_ids()
    first, last = lane == 0, lane == LANES - 1
    top = SLABS - 1

    def field(f, z):
        if f == 9:
            own = scale[z * ROWS : (z + 1) * ROWS, :]
        else:
            own = e[f, z * ROWS : (z + 1) * ROWS, :]
        return jnp.concatenate([own, halo[f, z * HALO : (z + 1) * HALO, :]], axis=0)

    below_columns, above_columns = from_below[0], from_above[0]

    def columns_below(i):
        return jnp.where(z_at == 0, lanes_by(below_columns, -i * COLUMNS), 0.0)

    def columns_above(i):
        return jnp.where(z_at == SLABS + 1, lanes_by(above_columns, (SLABS + 1 - i) * COLUMNS), 0.0)

    in_z = jnp.logical_and(z_at >= 1, z_at <= SLABS)
    far_e = [columns_above(3 + c) + jnp.where(z_at == 1, pe_in[c], 0.0) for c in range(2)]
    pdx = packed_factor * lanes_by(far_e[1], -COLUMNS)
    pdy = -(packed_factor * lanes_by(far_e[0], -COLUMNS))
    ph1 = [
        jnp.where(in_z, ph1_in[0], columns_below(0)) + pdx,
        jnp.where(in_z, ph1_in[1], columns_below(1)) + pdy,
        ph1_in[2],
    ]
    pscale = jnp.where(in_z, pscale_in[...], columns_below(5) + columns_above(2))
    edge = jnp.logical_or(z_at == 1, z_at == SLABS + 1)
    px = jnp.where(edge, lanes_by(ph1[0], COLUMNS), 0.0)
    py = jnp.where(edge, lanes_by(ph1[1], COLUMNS), 0.0)
    pe1 = [
        jnp.where(in_z, pe1_in[0], columns_below(2) + columns_above(0)) + pscale * (py - pdy),
        jnp.where(in_z, pe1_in[1], columns_below(3) + columns_above(1)) + pscale * (pdx - px),
        jnp.where(in_z, pe1_in[2], columns_below(4))
        + pscale * ((pdy - x_before(pdy)) - (pdx - lanes_by(pdx, 1))),
    ]
    ph2 = packed_h(ph1, pe1, packed_factor)

    def shifted_curl(dx, dy, z):
        dx_before = jnp.where(first, column_of(pdx, z, 1, 0), lanes_by(dx, 1))
        return (dy - x_before(dy)) - (dx - dx_before)

    dx, dy = factor * from_above[5], -(factor * from_above[4])
    h1_top = [h1_in[0, 2] + dx, h1_in[1, 2] + dy, h1_in[2, 2]]
    scale_top = field(9, top)
    late_top = (-(scale_top * dy), scale_top * dx, scale_top * shifted_curl(dx, dy, top))
    e1_top = [e1_ends[c, 1] + late_top[c] for c in range(3)]
    e1_over = (from_above[1] + from_above[3] * h1_top[1], from_above[2] - from_above[3] * h1_top[0])
    dx, dy = below_factor * field(1, 0), -(below_factor * field(0, 0))
    h1_under = (from_below[1] + dx, from_below[2] + dy)
    scale_under = from_below[6]
    e1_under = [
        from_below[3] - scale_under * dy,
        from_below[4] + scale_under * dx,
        from_below[5] + scale_under * shifted_curl(dx, dy, -1),
    ]
    scale_0 = field(9, 0)
    late_0 = (scale_0 * h1_under[1], -(scale_0 * h1_under[0]))
    e1_0 = [e1_ends[0, 0] + late_0[0], e1_ends[1, 0] + late_0[1], e1_ends[2, 0]]

    late[...] = jnp.zeros_like(late)
    for c in range(3):
        if c < 2:
            late[c, 0:ROWS, :] = late_0[c][:ROWS]
        late[c, ROWS : 2 * ROWS, :] = late_top[c][:ROWS]
    for b in range(rows.shape[1]):
        run = runs[0, b]
        at = jnp.where(run < ROWS, run, jnp.where(run >= top * ROWS, run - (top - 1) * ROWS, 2 * ROWS))
        gain_rows[pl.ds(b, 1), :] = gains[pl.ds(run, 1), :]
        for c in range(3):
            rows[c, pl.ds(b, 1), :] = late[c, pl.ds(at, 1), :]
    offsets = lax.bitwise_and(cells[...], LANES - 1)
    for c in range(3):
        more = gain_rows[...] * jnp.take_along_axis(rows[c], offsets, axis=1)
        cur_out[c] = cur[c] + more
        pol_out[c] = pol[c] + TIME_STEP * more
    send(pol_out, pol_to)
    send(cur_out, cur_to)

    e1_1, e1_14 = ([e1_in[c, z] for c in range(3)] for z in (1, 14))
    under = h_slab(
        (*h1_under, h1_under[0]), e1_under, e1_0[:2], y_next_pair(e1_under, pe1, -1, last), below_factor
    )[:2]
    h2_0 = h_slab([h1_in[c, 0] for c in range(3)], e1_0, e1_1[:2], y_next_pair(e1_0, pe1, 0, last), factor)
    h2_14 = h_slab([h1_in[c, 1] for c in range(3)], e1_14, e1_top[:2], y_next_pair(e1_14, pe1, 14, last), factor)
    h2_top = h_slab(h1_top, e1_top, e1_over, y_next_pair(e1_top, pe1, top, last), factor)
    pad = jnp.zeros((HALO, LANES), jnp.float32)
    h2_13 = tuple(jnp.concatenate([h2_in[c, 13 * ROWS : 14 * ROWS, :], pad], axis=0) for c in range(2))
    e2 = {
        0: e_slab(e1_0, scale_0, h2_0, under, y_before_pair(h2_0, ph2, 0, first)),
        14: e_slab(e1_14, field(9, 14), h2_14, h2_13, y_before_pair(h2_14, ph2, 14, first)),
        top: e_slab(e1_top, scale_top, h2_top, h2_14[:2], y_before_pair(h2_top, ph2, top, first)),
    }
    ends = {0: (h2_0, slice(0, ROWS)), 14: (h2_14, slice(ROWS, 2 * ROWS)), top: (h2_top, slice(2 * ROWS, 3 * ROWS))}
    for value, at in ends.values():
        for c in range(3):
            h_out[c, at, :] = value[c][:ROWS]
    send(h_out.at[:, pl.ds(0, ROWS), :], h_to.at[:, pl.ds(0, ROWS), :])
    send(h_out.at[:, pl.ds(ROWS, 2 * ROWS), :], h_to.at[:, pl.ds(14 * ROWS, 2 * ROWS), :])
    for i, z in enumerate(END_SLABS):
        at = slice(z * ROWS, (z + 1) * ROWS)
        own_scale = scale[at, :]
        for c in range(3):
            value = e2[z][c][:ROWS] if z in e2 else e2_in[c, at, :]
            placed = j_rest[c, i]
            if z == 0 and c < 2:
                placed = placed + gains[at, :] * late_0[c][:ROWS]
            if z == top:
                placed = placed + gains[at, :] * late_top[c][:ROWS]
            if z == 1 and c == 0:
                value = value + own_scale * h2_0[1][:ROWS]
            if z == 1 and c == 1:
                value = value - own_scale * h2_0[0][:ROWS]
            e_out[c, i * ROWS : (i + 1) * ROWS, :] = value - own_scale * placed
    send(e_out.at[:, pl.ds(0, 2 * ROWS), :], e_to.at[:, pl.ds(0, 2 * ROWS), :])
    send(e_out.at[:, pl.ds(2 * ROWS, 2 * ROWS), :], e_to.at[:, pl.ds(14 * ROWS, 2 * ROWS), :])
    for copy in started:
        copy.wait()


def on_device(
    e_field, h_field, material, inv_permittivity, block_cells, block_count,
    block_decay, block_restore, block_drive, polarization, current,
):
    slots, width = block_cells.shape
    shape = e_field.shape
    runs_all = SLABS * ROWS
    f32, i32 = jnp.float32, jnp.int32
    vmem, smem, hbm = (pl.BlockSpec(memory_space=space) for space in (pltpu.VMEM, pltpu.SMEM, pltpu.HBM))
    params = pltpu.CompilerParams(vmem_limit_bytes=VMEM_LIMIT)

    def arr(*dims, dtype=f32):
        return jax.ShapeDtypeStruct(dims, dtype)

    def call(kernel, outs, ins, name, scratch=(), in_hbm=(), out_hbm=()):
        specs = [smem if id(v) in scalars else hbm if i in in_hbm else vmem for i, v in enumerate(ins)]
        ins = [pltpu.with_memory_space_constraint(v, pltpu.HBM) if i in in_hbm else v for i, v in enumerate(ins)]
        out_specs = [hbm if i in out_hbm else vmem for i in range(len(outs))]
        return pl.pallas_call(
            kernel, out_shape=outs, in_specs=specs, out_specs=out_specs, scratch_shapes=list(scratch),
            compiler_params=params, name=name,
        )(*ins)

    e, h = (v.reshape(3, runs_all, width) for v in (e_field, h_field))
    coefficients = [v.reshape(1, slots) for v in (block_decay, block_restore, block_drive)]
    place = [lax.axis_index(name) for name in ("gx", "gy", "gz")]
    flags = jnp.stack([k > 0 for k in place] + [k % 2 == 0 for k in place]).astype(f32)
    scalars = {id(flags), id(block_count)}
    blocks, flat, ext, tile = arr(3, slots, width), arr(3, runs_all, width), arr(3, EXT, width), arr(EXT, width)
    row = arr(1, slots)
    blocks_vmem, flat_vmem = pltpu.VMEM((3, slots, width), f32), pltpu.VMEM((3, runs_all, width), f32)
    e, h, pol1, cur1, a, scale, inverse, cells, runs, decay, restore, drive, x_first, x_second = call(
        first_kernel,
        [
            flat, flat, blocks, blocks, flat, arr(runs_all, width), arr(slots, width, dtype=i32),
            arr(slots, width, dtype=i32), arr(1, slots, dtype=i32), row, row, row,
            arr(len(UP_X), SLABS, width), arr(len(UP_X), SLABS, width),
        ],
        [
            e, h, material.reshape(runs_all, width), inv_permittivity, block_cells, block_count, *coefficients,
            polarization, current, flags,
        ],
        "first",
        [
            pltpu.VMEM((runs_all, width), i32), pltpu.SMEM(inv_permittivity.shape, f32), blocks_vmem, blocks_vmem,
            blocks_vmem, flat_vmem, pltpu.VMEM((1, slots), i32), pltpu.SMEM((1, slots), i32),
            pltpu.SemaphoreType.DMA((11,)),
        ],
        in_hbm=(0, 1, 2, 3, 4, 6, 7, 8, 9, 10),
    )
    x_second = swapped(x_second, "gx", 1)
    x_first = swapped(x_first, "gx", 0)
    (own,) = call(own_kernel, [arr(FIELDS, ROWS, width)], [e, h, a, scale], "own")
    halo, pe, pscale, ph1, pe1, y_first, y_second = call(
        faces_kernel,
        [arr(FIELDS, SLABS * HALO, width), ext, tile, ext, ext, arr(1, EXT, width), arr(1, EXT, width)],
        [x_second, x_first, own, flags],
        "faces",
    )
    y_second = swapped(y_second, "gy", 1)
    y_first = swapped(y_first, "gy", 0)
    pe, pscale, ph1, pe1, h1_ends, e1_ends, z_first, z_second = call(
        ends_kernel,
        [ext, tile, ext, ext, arr(3, 3, EXT, width), arr(3, 2, EXT, width), arr(7, EXT, width), arr(7, EXT, width)],
        [e, h, a, scale, halo, pe, pscale, ph1, pe1, y_second, y_first, flags],
        "ends",
    )
    z_first, z_second = swapped(z_first, "gz", 0), swapped(z_second, "gz", 1)
    slabs = (3, SLABS, EXT, width)
    e1, h2, e2 = call(
        middle_kernel,
        [arr(*slabs), flat, flat],
        [e, h, a, scale, halo, pe, pscale, ph1, pe1, h1_ends, e1_ends, flags],
        "middle",
        [pltpu.VMEM(slabs, f32), pltpu.VMEM(slabs, f32)],
    )
    scalars.add(id(runs))
    dma = pltpu.SemaphoreType.DMA
    e_most, pol2, cur2, j_rest, gains = call(
        blocks_kernel,
        [arr(3, 12 * ROWS, width), blocks, blocks, arr(3, len(END_SLABS), ROWS, width), arr(runs_all, width)],
        [
            scale, e1.reshape(3, SLABS * EXT, width), e2, inverse, runs, cells, block_count,
            decay, restore, drive, pol1, cur1,
        ],
        "blocks",
        [blocks_vmem, flat_vmem, pltpu.VMEM((slots, width), f32)],
    )
    e_out, h_out, pol2, cur2 = call(
        last_kernel,
        [flat, flat, blocks, blocks],
        [
            e, scale, halo, z_first, z_second, flags, pe, pscale, ph1, pe1, h1_ends, e1_ends, e1, h2, e2,
            e_most, j_rest, gains, runs, cells, pol2, cur2,
        ],
        "last",
        [
            pltpu.VMEM((3, 4 * ROWS, width), f32), pltpu.VMEM((3, 3 * ROWS, width), f32), blocks_vmem, blocks_vmem,
            pltpu.VMEM((3, 2 * ROWS + 8, width), f32), blocks_vmem, pltpu.VMEM((slots, width), f32),
            pltpu.SemaphoreType.DMA((8,)),
        ],
        out_hbm=(0, 1, 2, 3),
    )
    return e_out.reshape(shape), h_out.reshape(shape), pol2, cur2


def solution(mesh):
    grid = P(None, "gz", "gx", "gy")
    rows = ("gx", "gy", "gz")
    return jax.shard_map(
        on_device,
        mesh=mesh,
        in_specs=(
            grid, grid, P("gz", "gx", "gy"), P(), P(rows, None), P(rows), P(rows), P(rows), P(rows),
            P(None, rows, None), P(None, rows, None),
        ),
        out_specs=(grid, grid, P(None, rows, None), P(None, rows, None)),
        check_vma=False,
    )
```

```python
import jax
import jax.numpy as jnp
from jax import lax
from jax.experimental import pallas as pl
from jax.experimental.pallas import tpu as pltpu
from jax.sharding import PartitionSpec as P

TIME_STEP = 0.5
VMEM_LIMIT = 32 * 1024 * 1024

SLABS, ROWS, HALO, LANES, COLUMNS = 16, 32, 8, 128, 7
EXT = ROWS + HALO

FIELDS = 10
UP_X = [(f, 30, 6) for f in (0, 1, 2, 4, 5)] + [(f, 31, 7) for f in range(FIELDS)]
DOWN_X = [(f, 0, 0) for f in (0, 1, 2, 3, 4, 5, 7, 8, 9)] + [(f, 1, 1) for f in (1, 2)]


def swapped(value, axis, first):
    pairs = [(k, k + 1) for k in range(first, lax.axis_size(axis) - 1, 2)]
    return lax.ppermute(value, axis, pairs + [(upper, lower) for lower, upper in pairs])


def is_even(flags, axis):
    return flags[3 + axis] > 0.5


def to_swap(even, even_out, odd_out, up, down):
    for i, value in enumerate(up):
        if i < len(down):
            even_out[i] = jnp.where(even, value, down[i])
            odd_out[i] = jnp.where(even, down[i], value)
        else:
            even_out[i] = value
            odd_out[i] = value


class Swapped:
    def __init__(self, even, when_even, when_odd):
        self.even, self.when_even, self.when_odd = even, when_even, when_odd

    def __getitem__(self, at):
        return jnp.where(self.even, self.when_even[at], self.when_odd[at])


def lanes_by(value, shift):
    shift = shift % LANES
    return pltpu.roll(value, shift, 1) if shift else value


def x_next(value):
    return pltpu.roll(value, EXT - 1, 0)


def x_before(value):
    return pltpu.roll(value, 1, 0)


def lane_ids(rows=EXT):
    return lax.broadcasted_iota(jnp.int32, (rows, LANES), 1)


def column_of(packed, z, slot, lane):
    return lanes_by(packed, lane - ((z + 1) * COLUMNS + slot))


def row_factor(flags):
    row = lax.broadcasted_iota(jnp.int32, (EXT, LANES), 0)
    return jnp.where(row >= ROWS + 4, TIME_STEP * flags[0], TIME_STEP)


def packed_places(rows=EXT):
    lane = lane_ids(rows)
    z_at = lax.shift_right_logical(lane * 9363, 16)
    return z_at, lane - z_at * COLUMNS


def h_slab(h, e, e_above, e_y, factor):
    return (
        h[0] - factor * ((e_y[1] - e[2]) - (e_above[1] - e[1])),
        h[1] - factor * ((e_above[0] - e[0]) - (x_next(e[2]) - e[2])),
        h[2] - factor * ((x_next(e[1]) - e[1]) - (e_y[0] - e[0])),
    )


def e_slab(a, scale, h, h_below, h_y):
    return (
        a[0] + scale * ((h[2] - h_y[1]) - (h[1] - h_below[1])),
        a[1] + scale * ((h[0] - h_below[0]) - (h[2] - x_before(h[2]))),
        a[2] + scale * ((h[1] - x_before(h[1])) - (h[0] - h_y[0])),
    )


def y_next_pair(e, packed_e, z, last):
    return tuple(
        jnp.where(last, column_of(packed_e[c], z, 5, LANES - 1), lanes_by(e[c], -1)) for c in (0, 2)
    )


def y_before_pair(h, packed_h, z, first):
    return tuple(jnp.where(first, column_of(packed_h[c], z, 1, 0), lanes_by(h[c], 1)) for c in (0, 2))


def as_column(row_ref, eye):
    return jnp.sum(jnp.where(eye, row_ref[...], 0.0), axis=1, keepdims=True)


def gather_rows(e, pitch, runs, rows):
    for b in range(rows.shape[1]):
        run = runs[0, b]
        at = run + lax.shift_right_logical(run, 5) * (pitch - ROWS)
        for comp in range(3):
            rows[comp, pl.ds(b, 1), :] = e[comp, pl.ds(at, 1), :]


def advance_blocks(cells, inverse, runs, count, decay, restore, drive, pol, cur, pol_out, cur_out, rows, j_rows):
    slots, width = cells.shape
    offsets = lax.bitwise_and(cells[...], width - 1)
    down = lax.broadcasted_iota(jnp.int32, (slots, width), 0)
    across = lax.broadcasted_iota(jnp.int32, (slots, width), 1)
    eye = down == across
    live = down < count[0]
    decay_c, restore_c, drive_c = (as_column(ref, eye) for ref in (decay, restore, drive))
    back = inverse[...]
    for comp in range(3):
        at_cells = jnp.take_along_axis(rows[comp], offsets, axis=1)
        held, polar = cur[comp], pol[comp]
        new = jnp.where(live, decay_c * held - restore_c * polar + drive_c * at_cells, held)
        cur_out[comp] = new
        pol_out[comp] = jnp.where(live, polar + TIME_STEP * new, polar)
        rows[comp] = jnp.take_along_axis(jnp.where(live, new, 0.0), back, axis=1)
    for b in range(slots):
        run = runs[0, b]
        for comp in range(3):
            j_rows[comp, pl.ds(run, 1), :] = rows[comp, pl.ds(b, 1), :]
    return jnp.where(live, drive_c, 0.0)


def spread(value):
    return value * 0x01010101


def invert_rows(offsets, lane):
    words = jnp.full(lane.shape, -0x7F7F7F80, jnp.int32)
    for t, part in enumerate(offsets):
        words = lax.bitwise_or(words, lax.shift_left(lax.bitwise_and(part - lane, LANES - 1), 8 * t))
    low, high = {}, {}
    for s in range(1, LANES):
        misses = lax.bitwise_xor(pltpu.roll(words, s, 1), spread(s)) - spread(1)
        for table, at in ((low, s % 8), (high, s // 8)):
            table[at] = lax.bitwise_and(table[at], misses) if at in table else misses
    found = jnp.zeros(lane.shape, jnp.int32)
    for bit in range(7):
        table, mask = (low, 1 << bit) if bit < 3 else (high, 1 << (bit - 3))
        every = None
        for at, value in table.items():
            if at & mask:
                every = value if every is None else lax.bitwise_and(every, value)
        hit = lax.bitwise_and(lax.shift_right_logical(lax.bitwise_xor(every, -1), 7), spread(1))
        found = lax.bitwise_or(found, lax.shift_left(hit, bit))
    return [
        lax.bitwise_and(lane - lax.bitwise_and(lax.shift_right_logical(found, 8 * t), LANES - 1), LANES - 1)
        for t in range(len(offsets))
    ]


def first_kernel(
    e_in, h_in, material_in, inv_perm_in, cells_in, count, decay_in, restore_in, drive_in, pol_in, cur_in, flags,
    e, h, pol_out, cur_out, a_out, scale_out, inverse_out, cells, runs_out, decay, restore, drive, up_out, down_out,
    material, inv_perm, pol, cur, rows, j_rows, run_row, runs, sems,
):
    copies = {}
    for i, (name, source, target) in enumerate(
        (
            ("cells", cells_in, cells), ("inv_perm", inv_perm_in, inv_perm), ("material", material_in, material),
            ("decay", decay_in, decay), ("restore", restore_in, restore), ("drive", drive_in, drive),
            ("e", e_in, e), ("cur", cur_in, cur), ("pol", pol_in, pol), ("h", h_in, h),
        )
    ):
        copies[name] = pltpu.make_async_copy(source, target, sems.at[i])
        copies[name].start()
    slots, width = cells.shape
    down = lax.broadcasted_iota(jnp.int32, (slots, width), 0)
    across = lax.broadcasted_iota(jnp.int32, (slots, width), 1)
    lane = lane_ids(8)
    j_rows[...] = jnp.zeros_like(j_rows)
    copies["cells"].wait()
    run_of = lax.shift_right_logical(cells[...], 7)
    run_row[...] = jnp.sum(jnp.where(down == across, run_of, 0), axis=0, keepdims=True)
    runs_out[...] = run_row[...]
    copy = pltpu.make_async_copy(run_row, runs, sems.at[10])
    copy.start()
    for row in range(0, slots, 32):
        parts = [lax.bitwise_and(cells[row + 8 * t : row + 8 * t + 8, :], width - 1) for t in range(4)]
        for t, part in enumerate(invert_rows(parts, lane)):
            inverse_out[row + 8 * t : row + 8 * t + 8, :] = part

    copies["inv_perm"].wait()
    copies["material"].wait()
    table = jnp.zeros((8, width), jnp.float32)
    for kind in range(inv_perm.shape[0]):
        table = jnp.where(lane == kind, TIME_STEP * inv_perm[kind], table)
    for row in range(0, material.shape[0], 8):
        scale_out[row : row + 8, :] = jnp.take_along_axis(table, material[row : row + 8, :], axis=1)
    for name in ("decay", "restore", "drive", "e", "cur", "pol"):
        copies[name].wait()
    copy.wait()
    gather_rows(e, ROWS, runs, rows)
    advance_blocks(
        cells, inverse_out, runs, count, decay, restore, drive, pol, cur, pol_out, cur_out, rows, j_rows
    )
    for comp in range(3):
        a_out[comp] = e[comp] - scale_out[...] * j_rows[comp]
    copies["h"].wait()

    def plane(f, x):
        at = pl.ds(x, SLABS, stride=ROWS)
        if f == 9:
            return scale_out[at, :]
        return (e, h, a_out)[f // 3][f % 3, at, :]

    up, down = ([plane(f, x) for f, x, _ in planes] for planes in (UP_X, DOWN_X))
    to_swap(is_even(flags, 0), up_out, down_out, up, down)


def pack_tiles(tile, tiles):
    lane = lane_ids(8)
    z_at, slot = packed_places(8)
    low = jnp.logical_or(slot == 2, slot == 3)
    inside = jnp.logical_and(z_at >= 1, z_at <= SLABS)
    low, high = jnp.logical_and(low, inside), jnp.logical_and(slot >= 5, inside)
    tops = [jnp.zeros((8, LANES), jnp.float32) for _ in range(tiles)]
    bottoms = list(tops)
    for z in range(SLABS):
        place = (z + 1) * COLUMNS + 5
        top_at, bottom_at = lane >= place, lane >= place + 2
        for t in range(tiles):
            moved = lanes_by(tile(z, t), place - (LANES - 2))
            tops[t] = jnp.where(top_at, moved, tops[t])
            bottoms[t] = jnp.where(bottom_at, moved, bottoms[t])
    return [
        jnp.where(high, top, jnp.where(low, lanes_by(bottom, -5), 0.0)) for top, bottom in zip(tops, bottoms)
    ]


def own_kernel(e, h, a, scale, own_out):
    for f in range(FIELDS):
        def tile(z, t):
            at = slice(z * ROWS + t * 8, z * ROWS + t * 8 + 8)
            return scale[at, :] if f == 9 else (e, h, a)[f // 3][f % 3, at, :]

        for t, value in enumerate(pack_tiles(tile, ROWS // 8)):
            own_out[f, t * 8 : t * 8 + 8, :] = value


UP_E0X, UP_E0Y, UP_E0Y_2, UP_H1Y = 1, 2, 3, 4
DOWN_H1Y = 1


def faces_kernel(got_second, got_first, own, flags, halo_out, pe_out, pscale_out, ph1_out, pe1_out, up_out, down_out):
    even = is_even(flags, 0)
    from_above, from_below = Swapped(even, got_first, got_second), Swapped(even, got_second, got_first)
    halo_out[...] = jnp.zeros_like(halo_out)
    for got, planes in ((from_below, UP_X), (from_above, DOWN_X)):
        for i, (f, _, row) in enumerate(planes):
            halo_out[f, pl.ds(row, SLABS, stride=HALO), :] = got[i]
    packed = []
    for f in range(FIELDS):
        (tile,) = pack_tiles(lambda z, t: halo_out[f, z * HALO : z * HALO + 8, :], 1)
        packed.append(jnp.concatenate([own[f], tile], axis=0))
    z_at, slot = packed_places()
    inside = jnp.logical_and(z_at >= 1, z_at <= SLABS)
    factor = jnp.where(inside, row_factor(flags), 0.0)
    factor = jnp.where(jnp.logical_or(slot >= 5, jnp.logical_or(slot == 2, slot == 3)), factor, 0.0)
    pe, pscale = packed[0:3], packed[9]
    ph1 = packed_h(packed[3:6], pe, factor)
    pe1 = e_slab(
        packed[6:9], pscale, ph1, (lanes_by(ph1[0], COLUMNS), lanes_by(ph1[1], COLUMNS)),
        (lanes_by(ph1[0], 1), lanes_by(ph1[2], 1)),
    )
    for c in range(3):
        pe_out[c], ph1_out[c], pe1_out[c] = pe[c], ph1[c], pe1[c]
    pscale_out[...] = pscale
    up = jnp.zeros((EXT, LANES), jnp.float32)
    for i, value in enumerate((ph1[0], ph1[2], *pe1, pscale)):
        up = jnp.where(slot == i, lanes_by(value, i - 6), up)
    for z_to, value, slot_from, z_from in (
        (UP_E0X, pe[0], 6, 1), (UP_E0Y, pe[1], 6, 1), (UP_E0Y_2, pe[1], 5, 1), (UP_H1Y, ph1[1], 6, SLABS),
    ):
        here = jnp.logical_and(slot == 6, z_at == z_to)
        up = jnp.where(here, lanes_by(value, 6 - slot_from + (z_to - z_from) * COLUMNS), up)
    low = jnp.zeros((EXT, LANES), jnp.float32)
    for i, value in enumerate((pe1[0], pe1[2], pscale, pe[0], pe[2], pe[1])):
        low = jnp.where(slot == i, lanes_by(value, i - 2), low)
    here = jnp.logical_and(slot == 6, z_at == DOWN_H1Y)
    low = jnp.where(here, lanes_by(ph1[1], 4 + (DOWN_H1Y - SLABS) * COLUMNS), low)
    to_swap(is_even(flags, 1), up_out, down_out, [up], [low])


def slab_reader(e, h, a, scale, halo):
    def read(f, z):
        if f == 9:
            own = scale[z * ROWS : (z + 1) * ROWS, :]
        else:
            own = (e, h, a)[f // 3][f % 3, z * ROWS : (z + 1) * ROWS, :]
        return jnp.concatenate([own, halo[f, z * HALO : (z + 1) * HALO, :]], axis=0)

    return read


def packed_h(h, e, factor):
    return h_slab(
        h, e, (lanes_by(e[0], -COLUMNS), lanes_by(e[1], -COLUMNS)), (lanes_by(e[0], -1), lanes_by(e[2], -1)), factor
    )


END_H = (0, 14, 15)
END_E = (0, 15)


def ends_kernel(
    e, h, a, scale, halo, pe_in, pscale_in, ph1_in, pe1_in, got_second, got_first, flags,
    pe_out, pscale_out, ph1_out, pe1_out, h1_out, e1_out, up_out, down_out,
):
    z_at, slot = packed_places()
    inside = jnp.logical_and(z_at >= 1, z_at <= SLABS)
    factor = row_factor(flags)
    packed_factor = jnp.where(slot < 2, factor * flags[1], factor)
    packed_factor = jnp.where(inside, packed_factor, 0.0)
    even = is_even(flags, 1)
    up_got, down_got = Swapped(even, got_second, got_first)[0], Swapped(even, got_first, got_second)[0]
    last_low, first_high = slot == 1, slot == 5

    def columns(value, low=None, high=None):
        value = jnp.where(slot == 2, value, jnp.where(slot == 4, lanes_by(value, -2), 0.0))
        if low is not None:
            value = jnp.where(last_low, lanes_by(up_got, 1 - low), value)
        if high is not None:
            value = jnp.where(first_high, lanes_by(down_got, 5 - high), value)
        return jnp.where(inside, value, 0.0)

    def single(got, slot_to, z_to, z_from, value):
        here = jnp.logical_and(slot == slot_to, z_at == z_to)
        return jnp.where(here, lanes_by(got, slot_to - 6 + (z_to - z_from) * COLUMNS), value)

    pe = [columns(pe_in[0], None, 3), columns(pe_in[1], None, 5), columns(pe_in[2], None, 4)]
    pe[0] = single(up_got, 1, 1, UP_E0X, pe[0])
    pe[1] = single(up_got, 1, 1, UP_E0Y, pe[1])
    pe[1] = single(up_got, 0, 1, UP_E0Y_2, pe[1])
    pscale = columns(pscale_in[...], 5, 2)
    ph1 = [columns(ph1_in[0], 0), columns(ph1_in[1]), columns(ph1_in[2], 1)]
    ph1[1] = single(up_got, 1, SLABS, UP_H1Y, ph1[1])
    ph1[1] = single(down_got, 5, SLABS, DOWN_H1Y, ph1[1])
    pe1 = [columns(pe1_in[0], 2, 0), columns(pe1_in[1], 3), columns(pe1_in[2], 4, 1)]
    upper = jnp.logical_or(slot == 1, slot == 4)
    lower = jnp.logical_or(slot == 2, slot == 5)
    step = jnp.where(upper, packed_factor, 0.0)
    pdx = -(step * lanes_by(pe[2], -1))
    pdz = step * lanes_by(pe[0], -1)
    ph1[0], ph1[2] = ph1[0] + pdx, ph1[2] + pdz
    px = jnp.where(lower, lanes_by(ph1[0], 1), 0.0)
    pz = jnp.where(lower, lanes_by(ph1[2], 1), 0.0)
    pe1[0] = pe1[0] + pscale * (pdz - pz)
    pe1[1] = pe1[1] + pscale * ((pdx - lanes_by(pdx, COLUMNS)) - (pdz - x_before(pdz)))
    pe1[2] = pe1[2] + pscale * (px - pdx)
    for c in range(3):
        pe_out[c], ph1_out[c], pe1_out[c] = pe[c], ph1[c], pe1[c]
    pscale_out[...] = pscale
    read = slab_reader(e, h, a, scale, halo)
    lane = lane_ids()
    first, last = lane == 0, lane == LANES - 1
    zero = jnp.zeros((EXT, LANES), jnp.float32)
    made = {}
    for i, z in enumerate(END_H):
        ez = [read(c, z) for c in range(3)]
        above = (read(0, z + 1), read(1, z + 1)) if z < SLABS - 1 else (zero, zero)
        made[z] = h_slab([read(3 + c, z) for c in range(3)], ez, above, y_next_pair(ez, pe, z, last), factor)
        for c in range(3):
            h1_out[c, i] = made[z][c]
    ends = {}
    for i, z in enumerate(END_E):
        below = made[z - 1][:2] if z else (zero, zero)
        ends[z] = e_slab(
            [read(6 + c, z) for c in range(3)], read(9, z), made[z], below, y_before_pair(made[z], ph1, z, first)
        )
        for c in range(3):
            e1_out[c, i] = ends[z][c]
    top = SLABS - 1
    up = [made[top][0], made[top][1], *ends[top], read(9, top)]
    packed_up = [ph1[0], ph1[1], *pe1, pscale]
    low = [ends[0][0], ends[0][1], read(9, 0), read(0, 0), read(1, 0)]
    packed_down = [pe1[0], pe1[1], pscale, pe[0], pe[1]]
    for slabs, columns, z_from in ((up, packed_up, SLABS), (low, packed_down, 1)):
        together = zero
        for i, column in enumerate(columns):
            together = jnp.where(z_at == i, lanes_by(column, (i - z_from) * COLUMNS), together)
        slabs.insert(0, together)
    to_swap(is_even(flags, 2), up_out, down_out, up, low)


def middle_kernel(
    e, h, a, scale, halo, pe_in, pscale, ph1_in, pe1_in, h1_in, e1_in, flags,
    e1_out, h2_out, e2_out, h1, h2,
):
    z_at, slot = packed_places()
    factor = row_factor(flags)
    packed_factor = jnp.where(slot < 2, factor * flags[1], factor)
    pe, ph1, pe1 = ([ref[c] for c in range(3)] for ref in (pe_in, ph1_in, pe1_in))
    read = slab_reader(e, h, a, scale, halo)
    lane = lane_ids()
    first, last = lane == 0, lane == LANES - 1
    zero = jnp.zeros((EXT, LANES), jnp.float32)

    def h1_of(c, z):
        return h1_in[c, END_H.index(z)] if z in END_H else h1[c, z]

    for z in range(1, 14):
        ez = [read(c, z) for c in range(3)]
        new = h_slab(
            [read(3 + c, z) for c in range(3)], ez, (read(0, z + 1), read(1, z + 1)), y_next_pair(ez, pe, z, last), factor
        )
        for c in range(3):
            h1[c, z] = new[c]
    for z in range(1, 15):
        hz = [h1_of(c, z) for c in range(3)]
        new = e_slab(
            [read(6 + c, z) for c in range(3)], read(9, z), hz, (h1_of(0, z - 1), h1_of(1, z - 1)),
            y_before_pair(hz, ph1, z, first),
        )
        for c in range(3):
            e1_out[c, z] = new[c]
    for i, z in enumerate(END_E):
        for c in range(3):
            e1_out[c, z] = e1_in[c, i]
    ph2 = packed_h(ph1, pe1, packed_factor)
    for z in range(1, 14):
        ez = [e1_out[c, z] for c in range(3)]
        new = h_slab(
            [h1[c, z] for c in range(3)], ez, (e1_out[0, z + 1], e1_out[1, z + 1]), y_next_pair(ez, pe1, z, last), factor
        )
        for c in range(3):
            h2[c, z] = new[c]
            h2_out[c, z * ROWS : (z + 1) * ROWS, :] = new[c][:ROWS]
    for z in range(1, 14):
        hz = [h2[c, z] for c in range(3)]
        below = (h2[0, z - 1], h2[1, z - 1]) if z > 1 else (zero, zero)
        new = e_slab(
            [e1_out[c, z] for c in range(3)], read(9, z), hz, below, y_before_pair(hz, ph2, z, first)
        )
        for c in range(3):
            e2_out[c, z * ROWS : (z + 1) * ROWS, :] = new[c][:ROWS]


def blocks_kernel(
    scale, e1, e2, inverse, runs, cells, count, decay, restore, drive, pol, cur,
    e_most, pol_out, cur_out, j_rest, gain_out, rows, j_rows, gain_rows,
):
    gather_rows(e1, EXT, runs, rows)
    j_rows[...] = jnp.zeros_like(j_rows)
    gain = advance_blocks(
        cells, inverse, runs, count, decay, restore, drive, pol, cur, pol_out, cur_out, rows, j_rows
    )
    gain_rows[...] = jnp.broadcast_to(gain, gain_rows.shape)
    gain_out[...] = jnp.zeros_like(gain_out)
    for b in range(gain_rows.shape[0]):
        gain_out[pl.ds(runs[0, b], 1), :] = gain_rows[pl.ds(b, 1), :]
    for c in range(3):
        for z in range(2, 14):
            at = slice(z * ROWS, (z + 1) * ROWS)
            e_most[c, (z - 2) * ROWS : (z - 1) * ROWS, :] = e2[c, at, :] - scale[at, :] * j_rows[c, at, :]
        for i, z in enumerate(END_SLABS):
            at = slice(z * ROWS, (z + 1) * ROWS)
            j_rest[c, i] = j_rows[c, at, :]


END_SLABS = (0, 1, 14, 15)


def last_kernel(
    e, scale, halo, got_second, got_first, flags, pe_in, pscale_in, ph1_in, pe1_in, h1_in, e1_ends, e1_in, h2_in, e2_in,
    e_most, j_rest, gains, runs, cells, pol, cur,
    e_to, h_to, pol_to, cur_to, e_out, h_out, pol_out, cur_out, late, rows, gain_rows, sems,
):
    started = []

    def send(source, target):
        copy = pltpu.make_async_copy(source, target, sems.at[len(started)])
        copy.start()
        started.append(copy)

    send(h2_in.at[:, pl.ds(ROWS, 13 * ROWS), :], h_to.at[:, pl.ds(ROWS, 13 * ROWS), :])
    send(e_most, e_to.at[:, pl.ds(2 * ROWS, 12 * ROWS), :])
    even = is_even(flags, 2)
    from_above, from_below = Swapped(even, got_first, got_second), Swapped(even, got_second, got_first)
    z_at, slot = packed_places()
    factor = row_factor(flags)
    below_factor = factor * flags[2]
    packed_factor = jnp.where(slot < 2, factor * flags[1], factor)
    packed_factor = jnp.where(z_at == 0, packed_factor * flags[2], packed_factor)
    packed_factor = jnp.where(z_at <= SLABS, packed_factor, 0.0)
    lane = lane_ids()
    first, last = lane == 0, lane == LANES - 1
    top = SLABS - 1

    def field(f, z):
        if f == 9:
            own = scale[z * ROWS : (z + 1) * ROWS, :]
        else:
            own = e[f, z * ROWS : (z + 1) * ROWS, :]
        return jnp.concatenate([own, halo[f, z * HALO : (z + 1) * HALO, :]], axis=0)

    below_columns, above_columns = from_below[0], from_above[0]

    def columns_below(i):
        return jnp.where(z_at == 0, lanes_by(below_columns, -i * COLUMNS), 0.0)

    def columns_above(i):
        return jnp.where(z_at == SLABS + 1, lanes_by(above_columns, (SLABS + 1 - i) * COLUMNS), 0.0)

    in_z = jnp.logical_and(z_at >= 1, z_at <= SLABS)
    far_e = [columns_above(3 + c) + jnp.where(z_at == 1, pe_in[c], 0.0) for c in range(2)]
    pdx = packed_factor * lanes_by(far_e[1], -COLUMNS)
    pdy = -(packed_factor * lanes_by(far_e[0], -COLUMNS))
    ph1 = [
        jnp.where(in_z, ph1_in[0], columns_below(0)) + pdx,
        jnp.where(in_z, ph1_in[1], columns_below(1)) + pdy,
        ph1_in[2],
    ]
    pscale = jnp.where(in_z, pscale_in[...], columns_below(5) + columns_above(2))
    edge = jnp.logical_or(z_at == 1, z_at == SLABS + 1)
    px = jnp.where(edge, lanes_by(ph1[0], COLUMNS), 0.0)
    py = jnp.where(edge, lanes_by(ph1[1], COLUMNS), 0.0)
    pe1 = [
        jnp.where(in_z, pe1_in[0], columns_below(2) + columns_above(0)) + pscale * (py - pdy),
        jnp.where(in_z, pe1_in[1], columns_below(3) + columns_above(1)) + pscale * (pdx - px),
        jnp.where(in_z, pe1_in[2], columns_below(4))
        + pscale * ((pdy - x_before(pdy)) - (pdx - lanes_by(pdx, 1))),
    ]
    ph2 = packed_h(ph1, pe1, packed_factor)

    def shifted_curl(dx, dy, z):
        dx_before = jnp.where(first, column_of(pdx, z, 1, 0), lanes_by(dx, 1))
        return (dy - x_before(dy)) - (dx - dx_before)

    dx, dy = factor * from_above[5], -(factor * from_above[4])
    h1_top = [h1_in[0, 2] + dx, h1_in[1, 2] + dy, h1_in[2, 2]]
    scale_top = field(9, top)
    late_top = (-(scale_top * dy), scale_top * dx, scale_top * shifted_curl(dx, dy, top))
    e1_top = [e1_ends[c, 1] + late_top[c] for c in range(3)]
    e1_over = (from_above[1] + from_above[3] * h1_top[1], from_above[2] - from_above[3] * h1_top[0])
    dx, dy = below_factor * field(1, 0), -(below_factor * field(0, 0))
    h1_under = (from_below[1] + dx, from_below[2] + dy)
    scale_under = from_below[6]
    e1_under = [
        from_below[3] - scale_under * dy,
        from_below[4] + scale_under * dx,
        from_below[5] + scale_under * shifted_curl(dx, dy, -1),
    ]
    scale_0 = field(9, 0)
    late_0 = (scale_0 * h1_under[1], -(scale_0 * h1_under[0]))
    e1_0 = [e1_ends[0, 0] + late_0[0], e1_ends[1, 0] + late_0[1], e1_ends[2, 0]]

    late[...] = jnp.zeros_like(late)
    for c in range(3):
        if c < 2:
            late[c, 0:ROWS, :] = late_0[c][:ROWS]
        late[c, ROWS : 2 * ROWS, :] = late_top[c][:ROWS]
    for b in range(rows.shape[1]):
        run = runs[0, b]
        at = jnp.where(run < ROWS, run, jnp.where(run >= top * ROWS, run - (top - 1) * ROWS, 2 * ROWS))
        gain_rows[pl.ds(b, 1), :] = gains[pl.ds(run, 1), :]
        for c in range(3):
            rows[c, pl.ds(b, 1), :] = late[c, pl.ds(at, 1), :]
    offsets = lax.bitwise_and(cells[...], LANES - 1)
    for c in range(3):
        more = gain_rows[...] * jnp.take_along_axis(rows[c], offsets, axis=1)
        cur_out[c] = cur[c] + more
        pol_out[c] = pol[c] + TIME_STEP * more
    send(pol_out, pol_to)
    send(cur_out, cur_to)

    e1_1, e1_14 = ([e1_in[c, z] for c in range(3)] for z in (1, 14))
    under = h_slab(
        (*h1_under, h1_under[0]), e1_under, e1_0[:2], y_next_pair(e1_under, pe1, -1, last), below_factor
    )[:2]
    h2_0 = h_slab([h1_in[c, 0] for c in range(3)], e1_0, e1_1[:2], y_next_pair(e1_0, pe1, 0, last), factor)
    h2_14 = h_slab([h1_in[c, 1] for c in range(3)], e1_14, e1_top[:2], y_next_pair(e1_14, pe1, 14, last), factor)
    h2_top = h_slab(h1_top, e1_top, e1_over, y_next_pair(e1_top, pe1, top, last), factor)
    pad = jnp.zeros((HALO, LANES), jnp.float32)
    h2_13 = tuple(jnp.concatenate([h2_in[c, 13 * ROWS : 14 * ROWS, :], pad], axis=0) for c in range(2))
    e2 = {
        0: e_slab(e1_0, scale_0, h2_0, under, y_before_pair(h2_0, ph2, 0, first)),
        14: e_slab(e1_14, field(9, 14), h2_14, h2_13, y_before_pair(h2_14, ph2, 14, first)),
        top: e_slab(e1_top, scale_top, h2_top, h2_14[:2], y_before_pair(h2_top, ph2, top, first)),
    }
    ends = {0: (h2_0, slice(0, ROWS)), 14: (h2_14, slice(ROWS, 2 * ROWS)), top: (h2_top, slice(2 * ROWS, 3 * ROWS))}
    for value, at in ends.values():
        for c in range(3):
            h_out[c, at, :] = value[c][:ROWS]
    send(h_out.at[:, pl.ds(0, ROWS), :], h_to.at[:, pl.ds(0, ROWS), :])
    send(h_out.at[:, pl.ds(ROWS, 2 * ROWS), :], h_to.at[:, pl.ds(14 * ROWS, 2 * ROWS), :])
    for i, z in enumerate(END_SLABS):
        at = slice(z * ROWS, (z + 1) * ROWS)
        own_scale = scale[at, :]
        for c in range(3):
            value = e2[z][c][:ROWS] if z in e2 else e2_in[c, at, :]
            placed = j_rest[c, i]
            if z == 0 and c < 2:
                placed = placed + gains[at, :] * late_0[c][:ROWS]
            if z == top:
                placed = placed + gains[at, :] * late_top[c][:ROWS]
            if z == 1 and c == 0:
                value = value + own_scale * h2_0[1][:ROWS]
            if z == 1 and c == 1:
                value = value - own_scale * h2_0[0][:ROWS]
            e_out[c, i * ROWS : (i + 1) * ROWS, :] = value - own_scale * placed
    send(e_out.at[:, pl.ds(0, 2 * ROWS), :], e_to.at[:, pl.ds(0, 2 * ROWS), :])
    send(e_out.at[:, pl.ds(2 * ROWS, 2 * ROWS), :], e_to.at[:, pl.ds(14 * ROWS, 2 * ROWS), :])
    for copy in started:
        copy.wait()


def on_device(
    e_field, h_field, material, inv_permittivity, block_cells, block_count,
    block_decay, block_restore, block_drive, polarization, current,
):
    slots, width = block_cells.shape
    shape = e_field.shape
    runs_all = SLABS * ROWS
    f32, i32 = jnp.float32, jnp.int32
    vmem, smem, hbm = (pl.BlockSpec(memory_space=space) for space in (pltpu.VMEM, pltpu.SMEM, pltpu.HBM))
    params = pltpu.CompilerParams(vmem_limit_bytes=VMEM_LIMIT)

    def arr(*dims, dtype=f32):
        return jax.ShapeDtypeStruct(dims, dtype)

    def call(kernel, outs, ins, name, scratch=(), in_hbm=(), out_hbm=()):
        specs = [smem if id(v) in scalars else hbm if i in in_hbm else vmem for i, v in enumerate(ins)]
        ins = [pltpu.with_memory_space_constraint(v, pltpu.HBM) if i in in_hbm else v for i, v in enumerate(ins)]
        out_specs = [hbm if i in out_hbm else vmem for i in range(len(outs))]
        return pl.pallas_call(
            kernel, out_shape=outs, in_specs=specs, out_specs=out_specs, scratch_shapes=list(scratch),
            compiler_params=params, name=name,
        )(*ins)

    e, h = (v.reshape(3, runs_all, width) for v in (e_field, h_field))
    coefficients = [v.reshape(1, slots) for v in (block_decay, block_restore, block_drive)]
    place = [lax.axis_index(name) for name in ("gx", "gy", "gz")]
    flags = jnp.stack([k > 0 for k in place] + [k % 2 == 0 for k in place]).astype(f32)
    scalars = {id(flags), id(block_count)}
    blocks, flat, ext, tile = arr(3, slots, width), arr(3, runs_all, width), arr(3, EXT, width), arr(EXT, width)
    row = arr(1, slots)
    blocks_vmem, flat_vmem = pltpu.VMEM((3, slots, width), f32), pltpu.VMEM((3, runs_all, width), f32)
    e, h, pol1, cur1, a, scale, inverse, cells, runs, decay, restore, drive, x_first, x_second = call(
        first_kernel,
        [
            flat, flat, blocks, blocks, flat, arr(runs_all, width), arr(slots, width, dtype=i32),
            arr(slots, width, dtype=i32), arr(1, slots, dtype=i32), row, row, row,
            arr(len(UP_X), SLABS, width), arr(len(UP_X), SLABS, width),
        ],
        [
            e, h, material.reshape(runs_all, width), inv_permittivity, block_cells, block_count, *coefficients,
            polarization, current, flags,
        ],
        "first",
        [
            pltpu.VMEM((runs_all, width), i32), pltpu.SMEM(inv_permittivity.shape, f32), blocks_vmem, blocks_vmem,
            blocks_vmem, flat_vmem, pltpu.VMEM((1, slots), i32), pltpu.SMEM((1, slots), i32),
            pltpu.SemaphoreType.DMA((11,)),
        ],
        in_hbm=(0, 1, 2, 3, 4, 6, 7, 8, 9, 10),
    )
    x_second = swapped(x_second, "gx", 1)
    x_first = swapped(x_first, "gx", 0)
    (own,) = call(own_kernel, [arr(FIELDS, ROWS, width)], [e, h, a, scale], "own")
    halo, pe, pscale, ph1, pe1, y_first, y_second = call(
        faces_kernel,
        [arr(FIELDS, SLABS * HALO, width), ext, tile, ext, ext, arr(1, EXT, width), arr(1, EXT, width)],
        [x_second, x_first, own, flags],
        "faces",
    )
    y_second = swapped(y_second, "gy", 1)
    y_first = swapped(y_first, "gy", 0)
    pe, pscale, ph1, pe1, h1_ends, e1_ends, z_first, z_second = call(
        ends_kernel,
        [ext, tile, ext, ext, arr(3, 3, EXT, width), arr(3, 2, EXT, width), arr(7, EXT, width), arr(7, EXT, width)],
        [e, h, a, scale, halo, pe, pscale, ph1, pe1, y_second, y_first, flags],
        "ends",
    )
    z_second = swapped(z_second, "gz", 1)
    z_first = swapped(z_first, "gz", 0)
    slabs = (3, SLABS, EXT, width)
    e1, h2, e2 = call(
        middle_kernel,
        [arr(*slabs), flat, flat],
        [e, h, a, scale, halo, pe, pscale, ph1, pe1, h1_ends, e1_ends, flags],
        "middle",
        [pltpu.VMEM(slabs, f32), pltpu.VMEM(slabs, f32)],
    )
    scalars.add(id(runs))
    dma = pltpu.SemaphoreType.DMA
    e_most, pol2, cur2, j_rest, gains = call(
        blocks_kernel,
        [arr(3, 12 * ROWS, width), blocks, blocks, arr(3, len(END_SLABS), ROWS, width), arr(runs_all, width)],
        [
            scale, e1.reshape(3, SLABS * EXT, width), e2, inverse, runs, cells, block_count,
            decay, restore, drive, pol1, cur1,
        ],
        "blocks",
        [blocks_vmem, flat_vmem, pltpu.VMEM((slots, width), f32)],
    )
    e_out, h_out, pol2, cur2 = call(
        last_kernel,
        [flat, flat, blocks, blocks],
        [
            e, scale, halo, z_second, z_first, flags, pe, pscale, ph1, pe1, h1_ends, e1_ends, e1, h2, e2,
            e_most, j_rest, gains, runs, cells, pol2, cur2,
        ],
        "last",
        [
            pltpu.VMEM((3, 4 * ROWS, width), f32), pltpu.VMEM((3, 3 * ROWS, width), f32), blocks_vmem, blocks_vmem,
            pltpu.VMEM((3, 2 * ROWS + 8, width), f32), blocks_vmem, pltpu.VMEM((slots, width), f32),
            pltpu.SemaphoreType.DMA((8,)),
        ],
        out_hbm=(0, 1, 2, 3),
    )
    return e_out.reshape(shape), h_out.reshape(shape), pol2, cur2


def solution(mesh):
    grid = P(None, "gz", "gx", "gy")
    rows = ("gx", "gy", "gz")
    return jax.shard_map(
        on_device,
        mesh=mesh,
        in_specs=(
            grid, grid, P("gz", "gx", "gy"), P(), P(rows, None), P(rows), P(rows), P(rows), P(rows),
            P(None, rows, None), P(None, rows, None),
        ),
        out_specs=(grid, grid, P(None, rows, None), P(None, rows, None)),
        check_vma=False,
    )
```

```python
import jax
import jax.numpy as jnp
from jax import lax
from jax.experimental import pallas as pl
from jax.experimental.pallas import tpu as pltpu
from jax.sharding import PartitionSpec as P

TIME_STEP = 0.5
VMEM_LIMIT = 32 * 1024 * 1024

SLABS, ROWS, HALO, LANES, COLUMNS = 16, 32, 8, 128, 7
EXT = ROWS + HALO

FIELDS = 10
UP_X = [(f, 30, 6) for f in (0, 1, 2, 4, 5)] + [(f, 31, 7) for f in range(FIELDS)]
DOWN_X = [(f, 0, 0) for f in (0, 1, 2, 3, 4, 5, 7, 8, 9)] + [(f, 1, 1) for f in (1, 2)]


def swapped(value, axis, first):
    pairs = [(k, k + 1) for k in range(first, lax.axis_size(axis) - 1, 2)]
    return lax.ppermute(value, axis, pairs + [(upper, lower) for lower, upper in pairs])


def is_even(flags, axis):
    return flags[3 + axis] > 0.5


def to_swap(even, even_out, odd_out, up, down):
    for i, value in enumerate(up):
        if i < len(down):
            even_out[i] = jnp.where(even, value, down[i])
            odd_out[i] = jnp.where(even, down[i], value)
        else:
            even_out[i] = value
            odd_out[i] = value


class Swapped:
    def __init__(self, even, when_even, when_odd):
        self.even, self.when_even, self.when_odd = even, when_even, when_odd

    def __getitem__(self, at):
        return jnp.where(self.even, self.when_even[at], self.when_odd[at])


def lanes_by(value, shift):
    shift = shift % LANES
    return pltpu.roll(value, shift, 1) if shift else value


def x_next(value):
    return pltpu.roll(value, EXT - 1, 0)


def x_before(value):
    return pltpu.roll(value, 1, 0)


def lane_ids(rows=EXT):
    return lax.broadcasted_iota(jnp.int32, (rows, LANES), 1)


def column_of(packed, z, slot, lane):
    return lanes_by(packed, lane - ((z + 1) * COLUMNS + slot))


def row_factor(flags):
    row = lax.broadcasted_iota(jnp.int32, (EXT, LANES), 0)
    return jnp.where(row >= ROWS + 4, TIME_STEP * flags[0], TIME_STEP)


def packed_places(rows=EXT):
    lane = lane_ids(rows)
    z_at = lax.shift_right_logical(lane * 9363, 16)
    return z_at, lane - z_at * COLUMNS


def h_slab(h, e, e_above, e_y, factor):
    return (
        h[0] - factor * ((e_y[1] - e[2]) - (e_above[1] - e[1])),
        h[1] - factor * ((e_above[0] - e[0]) - (x_next(e[2]) - e[2])),
        h[2] - factor * ((x_next(e[1]) - e[1]) - (e_y[0] - e[0])),
    )


def e_slab(a, scale, h, h_below, h_y):
    return (
        a[0] + scale * ((h[2] - h_y[1]) - (h[1] - h_below[1])),
        a[1] + scale * ((h[0] - h_below[0]) - (h[2] - x_before(h[2]))),
        a[2] + scale * ((h[1] - x_before(h[1])) - (h[0] - h_y[0])),
    )


def y_next_pair(e, packed_e, z, last):
    return tuple(
        jnp.where(last, column_of(packed_e[c], z, 5, LANES - 1), lanes_by(e[c], -1)) for c in (0, 2)
    )


def y_before_pair(h, packed_h, z, first):
    return tuple(jnp.where(first, column_of(packed_h[c], z, 1, 0), lanes_by(h[c], 1)) for c in (0, 2))


def as_column(row_ref, eye):
    return jnp.sum(jnp.where(eye, row_ref[...], 0.0), axis=1, keepdims=True)


def gather_rows(e, pitch, runs, rows):
    for b in range(rows.shape[1]):
        run = runs[0, b]
        at = run + lax.shift_right_logical(run, 5) * (pitch - ROWS)
        for comp in range(3):
            rows[comp, pl.ds(b, 1), :] = e[comp, pl.ds(at, 1), :]


def advance_blocks(cells, inverse, runs, count, decay, restore, drive, pol, cur, pol_out, cur_out, rows, j_rows):
    slots, width = cells.shape
    offsets = lax.bitwise_and(cells[...], width - 1)
    down = lax.broadcasted_iota(jnp.int32, (slots, width), 0)
    across = lax.broadcasted_iota(jnp.int32, (slots, width), 1)
    eye = down == across
    live = down < count[0]
    decay_c, restore_c, drive_c = (as_column(ref, eye) for ref in (decay, restore, drive))
    back = inverse[...]
    for comp in range(3):
        at_cells = jnp.take_along_axis(rows[comp], offsets, axis=1)
        held, polar = cur[comp], pol[comp]
        new = jnp.where(live, decay_c * held - restore_c * polar + drive_c * at_cells, held)
        cur_out[comp] = new
        pol_out[comp] = jnp.where(live, polar + TIME_STEP * new, polar)
        rows[comp] = jnp.take_along_axis(jnp.where(live, new, 0.0), back, axis=1)
    for b in range(slots):
        run = runs[0, b]
        for comp in range(3):
            j_rows[comp, pl.ds(run, 1), :] = rows[comp, pl.ds(b, 1), :]
    return jnp.where(live, drive_c, 0.0)


def spread(value):
    return value * 0x01010101


def invert_rows(offsets, lane):
    words = jnp.full(lane.shape, -0x7F7F7F80, jnp.int32)
    for t, part in enumerate(offsets):
        words = lax.bitwise_or(words, lax.shift_left(lax.bitwise_and(part - lane, LANES - 1), 8 * t))
    low, high = {}, {}
    for s in range(1, LANES):
        misses = lax.bitwise_xor(pltpu.roll(words, s, 1), spread(s)) - spread(1)
        for table, at in ((low, s % 8), (high, s // 8)):
            table[at] = lax.bitwise_and(table[at], misses) if at in table else misses
    found = jnp.zeros(lane.shape, jnp.int32)
    for bit in range(7):
        table, mask = (low, 1 << bit) if bit < 3 else (high, 1 << (bit - 3))
        every = None
        for at, value in table.items():
            if at & mask:
                every = value if every is None else lax.bitwise_and(every, value)
        hit = lax.bitwise_and(lax.shift_right_logical(lax.bitwise_xor(every, -1), 7), spread(1))
        found = lax.bitwise_or(found, lax.shift_left(hit, bit))
    return [
        lax.bitwise_and(lane - lax.bitwise_and(lax.shift_right_logical(found, 8 * t), LANES - 1), LANES - 1)
        for t in range(len(offsets))
    ]


def first_kernel(
    e_in, h_in, material_in, inv_perm_in, cells_in, count, decay_in, restore_in, drive_in, pol_in, cur_in, flags,
    e, h, pol_out, cur_out, a_out, scale_out, inverse_out, cells, runs_out, decay, restore, drive, up_out, down_out,
    material, inv_perm, pol, cur, rows, j_rows, run_row, runs, sems,
):
    copies = {}
    for i, (name, source, target) in enumerate(
        (
            ("cells", cells_in, cells), ("inv_perm", inv_perm_in, inv_perm), ("material", material_in, material),
            ("decay", decay_in, decay), ("restore", restore_in, restore), ("drive", drive_in, drive),
            ("e", e_in, e), ("cur", cur_in, cur), ("pol", pol_in, pol), ("h", h_in, h),
        )
    ):
        copies[name] = pltpu.make_async_copy(source, target, sems.at[i])
        copies[name].start()
    slots, width = cells.shape
    down = lax.broadcasted_iota(jnp.int32, (slots, width), 0)
    across = lax.broadcasted_iota(jnp.int32, (slots, width), 1)
    lane = lane_ids(8)
    j_rows[...] = jnp.zeros_like(j_rows)
    copies["cells"].wait()
    run_of = lax.shift_right_logical(cells[...], 7)
    run_row[...] = jnp.sum(jnp.where(down == across, run_of, 0), axis=0, keepdims=True)
    runs_out[...] = run_row[...]
    copy = pltpu.make_async_copy(run_row, runs, sems.at[10])
    copy.start()
    for row in range(0, slots, 32):
        parts = [lax.bitwise_and(cells[row + 8 * t : row + 8 * t + 8, :], width - 1) for t in range(4)]
        for t, part in enumerate(invert_rows(parts, lane)):
            inverse_out[row + 8 * t : row + 8 * t + 8, :] = part

    copies["inv_perm"].wait()
    copies["material"].wait()
    table = jnp.zeros((8, width), jnp.float32)
    for kind in range(inv_perm.shape[0]):
        table = jnp.where(lane == kind, TIME_STEP * inv_perm[kind], table)
    for row in range(0, material.shape[0], 8):
        scale_out[row : row + 8, :] = jnp.take_along_axis(table, material[row : row + 8, :], axis=1)
    for name in ("decay", "restore", "drive", "e", "cur", "pol"):
        copies[name].wait()
    copy.wait()
    gather_rows(e, ROWS, runs, rows)
    advance_blocks(
        cells, inverse_out, runs, count, decay, restore, drive, pol, cur, pol_out, cur_out, rows, j_rows
    )
    for comp in range(3):
        a_out[comp] = e[comp] - scale_out[...] * j_rows[comp]
    copies["h"].wait()

    def plane(f, x):
        at = pl.ds(x, SLABS, stride=ROWS)
        if f == 9:
            return scale_out[at, :]
        return (e, h, a_out)[f // 3][f % 3, at, :]

    up, down = ([plane(f, x) for f, x, _ in planes] for planes in (UP_X, DOWN_X))
    to_swap(is_even(flags, 0), up_out, down_out, up, down)


def pack_tiles(tile, tiles):
    lane = lane_ids(8)
    z_at, slot = packed_places(8)
    low = jnp.logical_or(slot == 2, slot == 3)
    inside = jnp.logical_and(z_at >= 1, z_at <= SLABS)
    low, high = jnp.logical_and(low, inside), jnp.logical_and(slot >= 5, inside)
    tops = [jnp.zeros((8, LANES), jnp.float32) for _ in range(tiles)]
    bottoms = list(tops)
    for z in range(SLABS):
        place = (z + 1) * COLUMNS + 5
        top_at, bottom_at = lane >= place, lane >= place + 2
        for t in range(tiles):
            moved = lanes_by(tile(z, t), place - (LANES - 2))
            tops[t] = jnp.where(top_at, moved, tops[t])
            bottoms[t] = jnp.where(bottom_at, moved, bottoms[t])
    return [
        jnp.where(high, top, jnp.where(low, lanes_by(bottom, -5), 0.0)) for top, bottom in zip(tops, bottoms)
    ]


def own_kernel(e, h, a, scale, own_out):
    for f in range(FIELDS):
        def tile(z, t):
            at = slice(z * ROWS + t * 8, z * ROWS + t * 8 + 8)
            return scale[at, :] if f == 9 else (e, h, a)[f // 3][f % 3, at, :]

        for t, value in enumerate(pack_tiles(tile, ROWS // 8)):
            own_out[f, t * 8 : t * 8 + 8, :] = value


UP_E0X, UP_E0Y, UP_E0Y_2, UP_H1Y = 1, 2, 3, 4
DOWN_H1Y = 1


def faces_kernel(got_second, got_first, own, flags, halo_out, pe_out, pscale_out, ph1_out, pe1_out, up_out, down_out):
    even = is_even(flags, 0)
    from_above, from_below = Swapped(even, got_first, got_second), Swapped(even, got_second, got_first)
    halo_out[...] = jnp.zeros_like(halo_out)
    for got, planes in ((from_below, UP_X), (from_above, DOWN_X)):
        for i, (f, _, row) in enumerate(planes):
            halo_out[f, pl.ds(row, SLABS, stride=HALO), :] = got[i]
    packed = []
    for f in range(FIELDS):
        (tile,) = pack_tiles(lambda z, t: halo_out[f, z * HALO : z * HALO + 8, :], 1)
        packed.append(jnp.concatenate([own[f], tile], axis=0))
    z_at, slot = packed_places()
    inside = jnp.logical_and(z_at >= 1, z_at <= SLABS)
    factor = jnp.where(inside, row_factor(flags), 0.0)
    factor = jnp.where(jnp.logical_or(slot >= 5, jnp.logical_or(slot == 2, slot == 3)), factor, 0.0)
    pe, pscale = packed[0:3], packed[9]
    ph1 = packed_h(packed[3:6], pe, factor)
    pe1 = e_slab(
        packed[6:9], pscale, ph1, (lanes_by(ph1[0], COLUMNS), lanes_by(ph1[1], COLUMNS)),
        (lanes_by(ph1[0], 1), lanes_by(ph1[2], 1)),
    )
    for c in range(3):
        pe_out[c], ph1_out[c], pe1_out[c] = pe[c], ph1[c], pe1[c]
    pscale_out[...] = pscale
    up = jnp.zeros((EXT, LANES), jnp.float32)
    for i, value in enumerate((ph1[0], ph1[2], *pe1, pscale)):
        up = jnp.where(slot == i, lanes_by(value, i - 6), up)
    for z_to, value, slot_from, z_from in (
        (UP_E0X, pe[0], 6, 1), (UP_E0Y, pe[1], 6, 1), (UP_E0Y_2, pe[1], 5, 1), (UP_H1Y, ph1[1], 6, SLABS),
    ):
        here = jnp.logical_and(slot == 6, z_at == z_to)
        up = jnp.where(here, lanes_by(value, 6 - slot_from + (z_to - z_from) * COLUMNS), up)
    low = jnp.zeros((EXT, LANES), jnp.float32)
    for i, value in enumerate((pe1[0], pe1[2], pscale, pe[0], pe[2], pe[1])):
        low = jnp.where(slot == i, lanes_by(value, i - 2), low)
    here = jnp.logical_and(slot == 6, z_at == DOWN_H1Y)
    low = jnp.where(here, lanes_by(ph1[1], 4 + (DOWN_H1Y - SLABS) * COLUMNS), low)
    to_swap(is_even(flags, 1), up_out, down_out, [up], [low])


def slab_reader(e, h, a, scale, halo):
    def read(f, z):
        if f == 9:
            own = scale[z * ROWS : (z + 1) * ROWS, :]
        else:
            own = (e, h, a)[f // 3][f % 3, z * ROWS : (z + 1) * ROWS, :]
        return jnp.concatenate([own, halo[f, z * HALO : (z + 1) * HALO, :]], axis=0)

    return read


def packed_h(h, e, factor):
    return h_slab(
        h, e, (lanes_by(e[0], -COLUMNS), lanes_by(e[1], -COLUMNS)), (lanes_by(e[0], -1), lanes_by(e[2], -1)), factor
    )


END_H = (0, 14, 15)
END_E = (0, 15)


def ends_kernel(
    e, h, a, scale, halo, pe_in, pscale_in, ph1_in, pe1_in, got_second, got_first, flags,
    pe_out, pscale_out, ph1_out, pe1_out, h1_out, e1_out, up_out, down_out,
):
    z_at, slot = packed_places()
    inside = jnp.logical_and(z_at >= 1, z_at <= SLABS)
    factor = row_factor(flags)
    packed_factor = jnp.where(slot < 2, factor * flags[1], factor)
    packed_factor = jnp.where(inside, packed_factor, 0.0)
    even = is_even(flags, 1)
    up_got, down_got = Swapped(even, got_second, got_first)[0], Swapped(even, got_first, got_second)[0]
    last_low, first_high = slot == 1, slot == 5

    def columns(value, low=None, high=None):
        value = jnp.where(slot == 2, value, jnp.where(slot == 4, lanes_by(value, -2), 0.0))
        if low is not None:
            value = jnp.where(last_low, lanes_by(up_got, 1 - low), value)
        if high is not None:
            value = jnp.where(first_high, lanes_by(down_got, 5 - high), value)
        return jnp.where(inside, value, 0.0)

    def single(got, slot_to, z_to, z_from, value):
        here = jnp.logical_and(slot == slot_to, z_at == z_to)
        return jnp.where(here, lanes_by(got, slot_to - 6 + (z_to - z_from) * COLUMNS), value)

    pe = [columns(pe_in[0], None, 3), columns(pe_in[1], None, 5), columns(pe_in[2], None, 4)]
    pe[0] = single(up_got, 1, 1, UP_E0X, pe[0])
    pe[1] = single(up_got, 1, 1, UP_E0Y, pe[1])
    pe[1] = single(up_got, 0, 1, UP_E0Y_2, pe[1])
    pscale = columns(pscale_in[...], 5, 2)
    ph1 = [columns(ph1_in[0], 0), columns(ph1_in[1]), columns(ph1_in[2], 1)]
    ph1[1] = single(up_got, 1, SLABS, UP_H1Y, ph1[1])
    ph1[1] = single(down_got, 5, SLABS, DOWN_H1Y, ph1[1])
    pe1 = [columns(pe1_in[0], 2, 0), columns(pe1_in[1], 3), columns(pe1_in[2], 4, 1)]
    upper = jnp.logical_or(slot == 1, slot == 4)
    lower = jnp.logical_or(slot == 2, slot == 5)
    step = jnp.where(upper, packed_factor, 0.0)
    pdx = -(step * lanes_by(pe[2], -1))
    pdz = step * lanes_by(pe[0], -1)
    ph1[0], ph1[2] = ph1[0] + pdx, ph1[2] + pdz
    px = jnp.where(lower, lanes_by(ph1[0], 1), 0.0)
    pz = jnp.where(lower, lanes_by(ph1[2], 1), 0.0)
    pe1[0] = pe1[0] + pscale * (pdz - pz)
    pe1[1] = pe1[1] + pscale * ((pdx - lanes_by(pdx, COLUMNS)) - (pdz - x_before(pdz)))
    pe1[2] = pe1[2] + pscale * (px - pdx)
    for c in range(3):
        pe_out[c], ph1_out[c], pe1_out[c] = pe[c], ph1[c], pe1[c]
    pscale_out[...] = pscale
    read = slab_reader(e, h, a, scale, halo)
    lane = lane_ids()
    first, last = lane == 0, lane == LANES - 1
    zero = jnp.zeros((EXT, LANES), jnp.float32)
    made = {}
    for i, z in enumerate(END_H):
        ez = [read(c, z) for c in range(3)]
        above = (read(0, z + 1), read(1, z + 1)) if z < SLABS - 1 else (zero, zero)
        made[z] = h_slab([read(3 + c, z) for c in range(3)], ez, above, y_next_pair(ez, pe, z, last), factor)
        for c in range(3):
            h1_out[c, i] = made[z][c]
    ends = {}
    for i, z in enumerate(END_E):
        below = made[z - 1][:2] if z else (zero, zero)
        ends[z] = e_slab(
            [read(6 + c, z) for c in range(3)], read(9, z), made[z], below, y_before_pair(made[z], ph1, z, first)
        )
        for c in range(3):
            e1_out[c, i] = ends[z][c]
    top = SLABS - 1
    up = [made[top][0], made[top][1], *ends[top], read(9, top)]
    packed_up = [ph1[0], ph1[1], *pe1, pscale]
    low = [ends[0][0], ends[0][1], read(9, 0), read(0, 0), read(1, 0)]
    packed_down = [pe1[0], pe1[1], pscale, pe[0], pe[1]]
    for slabs, columns, z_from in ((up, packed_up, SLABS), (low, packed_down, 1)):
        together = zero
        for i, column in enumerate(columns):
            together = jnp.where(z_at == i, lanes_by(column, (i - z_from) * COLUMNS), together)
        slabs.insert(0, together)
    to_swap(is_even(flags, 2), up_out, down_out, up, low)


def middle_kernel(
    e, h, a, scale, halo, pe_in, pscale, ph1_in, pe1_in, h1_in, e1_in, flags,
    e1_out, h2_out, e2_out, h1, h2,
):
    z_at, slot = packed_places()
    factor = row_factor(flags)
    packed_factor = jnp.where(slot < 2, factor * flags[1], factor)
    pe, ph1, pe1 = ([ref[c] for c in range(3)] for ref in (pe_in, ph1_in, pe1_in))
    read = slab_reader(e, h, a, scale, halo)
    lane = lane_ids()
    first, last = lane == 0, lane == LANES - 1
    zero = jnp.zeros((EXT, LANES), jnp.float32)

    def h1_of(c, z):
        return h1_in[c, END_H.index(z)] if z in END_H else h1[c, z]

    for z in range(1, 14):
        ez = [read(c, z) for c in range(3)]
        new = h_slab(
            [read(3 + c, z) for c in range(3)], ez, (read(0, z + 1), read(1, z + 1)), y_next_pair(ez, pe, z, last), factor
        )
        for c in range(3):
            h1[c, z] = new[c]
    for z in range(1, 15):
        hz = [h1_of(c, z) for c in range(3)]
        new = e_slab(
            [read(6 + c, z) for c in range(3)], read(9, z), hz, (h1_of(0, z - 1), h1_of(1, z - 1)),
            y_before_pair(hz, ph1, z, first),
        )
        for c in range(3):
            e1_out[c, z] = new[c]
    for i, z in enumerate(END_E):
        for c in range(3):
            e1_out[c, z] = e1_in[c, i]
    ph2 = packed_h(ph1, pe1, packed_factor)
    for z in range(1, 14):
        ez = [e1_out[c, z] for c in range(3)]
        new = h_slab(
            [h1[c, z] for c in range(3)], ez, (e1_out[0, z + 1], e1_out[1, z + 1]), y_next_pair(ez, pe1, z, last), factor
        )
        for c in range(3):
            h2[c, z] = new[c]
            h2_out[c, z * ROWS : (z + 1) * ROWS, :] = new[c][:ROWS]
    for z in range(1, 14):
        hz = [h2[c, z] for c in range(3)]
        below = (h2[0, z - 1], h2[1, z - 1]) if z > 1 else (zero, zero)
        new = e_slab(
            [e1_out[c, z] for c in range(3)], read(9, z), hz, below, y_before_pair(hz, ph2, z, first)
        )
        for c in range(3):
            e2_out[c, z * ROWS : (z + 1) * ROWS, :] = new[c][:ROWS]


def blocks_kernel(
    scale, e1, e2, inverse, runs, cells, count, decay, restore, drive, pol, cur,
    e_most, pol_out, cur_out, j_rest, gain_out, gain_rows, rows, j_rows,
):
    gather_rows(e1, EXT, runs, rows)
    j_rows[...] = jnp.zeros_like(j_rows)
    gain = advance_blocks(
        cells, inverse, runs, count, decay, restore, drive, pol, cur, pol_out, cur_out, rows, j_rows
    )
    gain_rows[...] = jnp.broadcast_to(gain, gain_rows.shape)
    gain_out[...] = jnp.zeros_like(gain_out)
    for b in range(gain_rows.shape[0]):
        gain_out[pl.ds(runs[0, b], 1), :] = gain_rows[pl.ds(b, 1), :]
    for c in range(3):
        for z in range(2, 14):
            at = slice(z * ROWS, (z + 1) * ROWS)
            e_most[c, (z - 2) * ROWS : (z - 1) * ROWS, :] = e2[c, at, :] - scale[at, :] * j_rows[c, at, :]
        for i, z in enumerate(END_SLABS):
            at = slice(z * ROWS, (z + 1) * ROWS)
            j_rest[c, i] = j_rows[c, at, :]


END_SLABS = (0, 1, 14, 15)


def last_kernel(
    e, scale, halo, got_first, got_second, flags, pe_in, pscale_in, ph1_in, pe1_in, h1_in, e1_ends, e1_in, h2_in, e2_in,
    e_most, j_rest, gains, gain_rows, runs, cells, pol, cur,
    e_to, h_to, pol_to, cur_to, e_out, h_out, pol_out, cur_out, late, rows, sems,
):
    started = []

    def send(source, target):
        copy = pltpu.make_async_copy(source, target, sems.at[len(started)])
        copy.start()
        started.append(copy)

    send(h2_in.at[:, pl.ds(ROWS, 13 * ROWS), :], h_to.at[:, pl.ds(ROWS, 13 * ROWS), :])
    send(e_most, e_to.at[:, pl.ds(2 * ROWS, 12 * ROWS), :])
    even = is_even(flags, 2)
    from_above, from_below = Swapped(even, got_first, got_second), Swapped(even, got_second, got_first)
    z_at, slot = packed_places()
    factor = row_factor(flags)
    below_factor = factor * flags[2]
    packed_factor = jnp.where(slot < 2, factor * flags[1], factor)
    packed_factor = jnp.where(z_at == 0, packed_factor * flags[2], packed_factor)
    packed_factor = jnp.where(z_at <= SLABS, packed_factor, 0.0)
    lane = lane_ids()
    first, last = lane == 0, lane == LANES - 1
    top = SLABS - 1

    def field(f, z):
        if f == 9:
            own = scale[z * ROWS : (z + 1) * ROWS, :]
        else:
            own = e[f, z * ROWS : (z + 1) * ROWS, :]
        return jnp.concatenate([own, halo[f, z * HALO : (z + 1) * HALO, :]], axis=0)

    below_columns, above_columns = from_below[0], from_above[0]

    def columns_below(i):
        return jnp.where(z_at == 0, lanes_by(below_columns, -i * COLUMNS), 0.0)

    def columns_above(i):
        return jnp.where(z_at == SLABS + 1, lanes_by(above_columns, (SLABS + 1 - i) * COLUMNS), 0.0)

    in_z = jnp.logical_and(z_at >= 1, z_at <= SLABS)
    far_e = [columns_above(3 + c) + jnp.where(z_at == 1, pe_in[c], 0.0) for c in range(2)]
    pdx = packed_factor * lanes_by(far_e[1], -COLUMNS)
    pdy = -(packed_factor * lanes_by(far_e[0], -COLUMNS))
    ph1 = [
        jnp.where(in_z, ph1_in[0], columns_below(0)) + pdx,
        jnp.where(in_z, ph1_in[1], columns_below(1)) + pdy,
        ph1_in[2],
    ]
    pscale = jnp.where(in_z, pscale_in[...], columns_below(5) + columns_above(2))
    edge = jnp.logical_or(z_at == 1, z_at == SLABS + 1)
    px = jnp.where(edge, lanes_by(ph1[0], COLUMNS), 0.0)
    py = jnp.where(edge, lanes_by(ph1[1], COLUMNS), 0.0)
    pe1 = [
        jnp.where(in_z, pe1_in[0], columns_below(2) + columns_above(0)) + pscale * (py - pdy),
        jnp.where(in_z, pe1_in[1], columns_below(3) + columns_above(1)) + pscale * (pdx - px),
        jnp.where(in_z, pe1_in[2], columns_below(4))
        + pscale * ((pdy - x_before(pdy)) - (pdx - lanes_by(pdx, 1))),
    ]
    ph2 = packed_h(ph1, pe1, packed_factor)

    def shifted_curl(dx, dy, z):
        dx_before = jnp.where(first, column_of(pdx, z, 1, 0), lanes_by(dx, 1))
        return (dy - x_before(dy)) - (dx - dx_before)

    dx, dy = factor * from_above[5], -(factor * from_above[4])
    h1_top = [h1_in[0, 2] + dx, h1_in[1, 2] + dy, h1_in[2, 2]]
    scale_top = field(9, top)
    late_top = (-(scale_top * dy), scale_top * dx, scale_top * shifted_curl(dx, dy, top))
    e1_top = [e1_ends[c, 1] + late_top[c] for c in range(3)]
    e1_over = (from_above[1] + from_above[3] * h1_top[1], from_above[2] - from_above[3] * h1_top[0])
    dx, dy = below_factor * field(1, 0), -(below_factor * field(0, 0))
    h1_under = (from_below[1] + dx, from_below[2] + dy)
    scale_under = from_below[6]
    e1_under = [
        from_below[3] - scale_under * dy,
        from_below[4] + scale_under * dx,
        from_below[5] + scale_under * shifted_curl(dx, dy, -1),
    ]
    scale_0 = field(9, 0)
    late_0 = (scale_0 * h1_under[1], -(scale_0 * h1_under[0]))
    e1_0 = [e1_ends[0, 0] + late_0[0], e1_ends[1, 0] + late_0[1], e1_ends[2, 0]]

    late[...] = jnp.zeros_like(late)
    for c in range(3):
        if c < 2:
            late[c, 0:ROWS, :] = late_0[c][:ROWS]
        late[c, ROWS : 2 * ROWS, :] = late_top[c][:ROWS]
    for b in range(rows.shape[1]):
        run = runs[0, b]
        at = jnp.where(run < ROWS, run, jnp.where(run >= top * ROWS, run - (top - 1) * ROWS, 2 * ROWS))
        for c in range(3):
            rows[c, pl.ds(b, 1), :] = late[c, pl.ds(at, 1), :]
    offsets = lax.bitwise_and(cells[...], LANES - 1)
    for c in range(3):
        more = gain_rows[...] * jnp.take_along_axis(rows[c], offsets, axis=1)
        cur_out[c] = cur[c] + more
        pol_out[c] = pol[c] + TIME_STEP * more
    send(pol_out, pol_to)
    send(cur_out, cur_to)

    e1_1, e1_14 = ([e1_in[c, z] for c in range(3)] for z in (1, 14))
    under = h_slab(
        (*h1_under, h1_under[0]), e1_under, e1_0[:2], y_next_pair(e1_under, pe1, -1, last), below_factor
    )[:2]
    h2_0 = h_slab([h1_in[c, 0] for c in range(3)], e1_0, e1_1[:2], y_next_pair(e1_0, pe1, 0, last), factor)
    h2_14 = h_slab([h1_in[c, 1] for c in range(3)], e1_14, e1_top[:2], y_next_pair(e1_14, pe1, 14, last), factor)
    h2_top = h_slab(h1_top, e1_top, e1_over, y_next_pair(e1_top, pe1, top, last), factor)
    pad = jnp.zeros((HALO, LANES), jnp.float32)
    h2_13 = tuple(jnp.concatenate([h2_in[c, 13 * ROWS : 14 * ROWS, :], pad], axis=0) for c in range(2))
    e2 = {
        0: e_slab(e1_0, scale_0, h2_0, under, y_before_pair(h2_0, ph2, 0, first)),
        14: e_slab(e1_14, field(9, 14), h2_14, h2_13, y_before_pair(h2_14, ph2, 14, first)),
        top: e_slab(e1_top, scale_top, h2_top, h2_14[:2], y_before_pair(h2_top, ph2, top, first)),
    }
    ends = {0: (h2_0, slice(0, ROWS)), 14: (h2_14, slice(ROWS, 2 * ROWS)), top: (h2_top, slice(2 * ROWS, 3 * ROWS))}
    for value, at in ends.values():
        for c in range(3):
            h_out[c, at, :] = value[c][:ROWS]
    send(h_out.at[:, pl.ds(0, ROWS), :], h_to.at[:, pl.ds(0, ROWS), :])
    send(h_out.at[:, pl.ds(ROWS, 2 * ROWS), :], h_to.at[:, pl.ds(14 * ROWS, 2 * ROWS), :])
    for i, z in enumerate(END_SLABS):
        at = slice(z * ROWS, (z + 1) * ROWS)
        own_scale = scale[at, :]
        for c in range(3):
            value = e2[z][c][:ROWS] if z in e2 else e2_in[c, at, :]
            placed = j_rest[c, i]
            if z == 0 and c < 2:
                placed = placed + gains[at, :] * late_0[c][:ROWS]
            if z == top:
                placed = placed + gains[at, :] * late_top[c][:ROWS]
            if z == 1 and c == 0:
                value = value + own_scale * h2_0[1][:ROWS]
            if z == 1 and c == 1:
                value = value - own_scale * h2_0[0][:ROWS]
            e_out[c, i * ROWS : (i + 1) * ROWS, :] = value - own_scale * placed
    send(e_out.at[:, pl.ds(0, 2 * ROWS), :], e_to.at[:, pl.ds(0, 2 * ROWS), :])
    send(e_out.at[:, pl.ds(2 * ROWS, 2 * ROWS), :], e_to.at[:, pl.ds(14 * ROWS, 2 * ROWS), :])
    for copy in started:
        copy.wait()


def on_device(
    e_field, h_field, material, inv_permittivity, block_cells, block_count,
    block_decay, block_restore, block_drive, polarization, current,
):
    slots, width = block_cells.shape
    shape = e_field.shape
    runs_all = SLABS * ROWS
    f32, i32 = jnp.float32, jnp.int32
    vmem, smem, hbm = (pl.BlockSpec(memory_space=space) for space in (pltpu.VMEM, pltpu.SMEM, pltpu.HBM))
    params = pltpu.CompilerParams(vmem_limit_bytes=VMEM_LIMIT)

    def arr(*dims, dtype=f32):
        return jax.ShapeDtypeStruct(dims, dtype)

    def call(kernel, outs, ins, name, scratch=(), in_hbm=(), out_hbm=()):
        specs = [smem if id(v) in scalars else hbm if i in in_hbm else vmem for i, v in enumerate(ins)]
        ins = [pltpu.with_memory_space_constraint(v, pltpu.HBM) if i in in_hbm else v for i, v in enumerate(ins)]
        out_specs = [hbm if i in out_hbm else vmem for i in range(len(outs))]
        return pl.pallas_call(
            kernel, out_shape=outs, in_specs=specs, out_specs=out_specs, scratch_shapes=list(scratch),
            compiler_params=params, name=name,
        )(*ins)

    e, h = (v.reshape(3, runs_all, width) for v in (e_field, h_field))
    coefficients = [v.reshape(1, slots) for v in (block_decay, block_restore, block_drive)]
    place = [lax.axis_index(name) for name in ("gx", "gy", "gz")]
    flags = jnp.stack([k > 0 for k in place] + [k % 2 == 0 for k in place]).astype(f32)
    scalars = {id(flags), id(block_count)}
    blocks, flat, ext, tile = arr(3, slots, width), arr(3, runs_all, width), arr(3, EXT, width), arr(EXT, width)
    row = arr(1, slots)
    blocks_vmem, flat_vmem = pltpu.VMEM((3, slots, width), f32), pltpu.VMEM((3, runs_all, width), f32)
    e, h, pol1, cur1, a, scale, inverse, cells, runs, decay, restore, drive, x_first, x_second = call(
        first_kernel,
        [
            flat, flat, blocks, blocks, flat, arr(runs_all, width), arr(slots, width, dtype=i32),
            arr(slots, width, dtype=i32), arr(1, slots, dtype=i32), row, row, row,
            arr(len(UP_X), SLABS, width), arr(len(UP_X), SLABS, width),
        ],
        [
            e, h, material.reshape(runs_all, width), inv_permittivity, block_cells, block_count, *coefficients,
            polarization, current, flags,
        ],
        "first",
        [
            pltpu.VMEM((runs_all, width), i32), pltpu.SMEM(inv_permittivity.shape, f32), blocks_vmem, blocks_vmem,
            blocks_vmem, flat_vmem, pltpu.VMEM((1, slots), i32), pltpu.SMEM((1, slots), i32),
            pltpu.SemaphoreType.DMA((11,)),
        ],
        in_hbm=(0, 1, 2, 3, 4, 6, 7, 8, 9, 10),
    )
    x_second = swapped(x_second, "gx", 1)
    x_first = swapped(x_first, "gx", 0)
    (own,) = call(own_kernel, [arr(FIELDS, ROWS, width)], [e, h, a, scale], "own")
    halo, pe, pscale, ph1, pe1, y_first, y_second = call(
        faces_kernel,
        [arr(FIELDS, SLABS * HALO, width), ext, tile, ext, ext, arr(1, EXT, width), arr(1, EXT, width)],
        [x_second, x_first, own, flags],
        "faces",
    )
    y_second = swapped(y_second, "gy", 1)
    y_first = swapped(y_first, "gy", 0)
    pe, pscale, ph1, pe1, h1_ends, e1_ends, z_first, z_second = call(
        ends_kernel,
        [ext, tile, ext, ext, arr(3, 3, EXT, width), arr(3, 2, EXT, width), arr(7, EXT, width), arr(7, EXT, width)],
        [e, h, a, scale, halo, pe, pscale, ph1, pe1, y_second, y_first, flags],
        "ends",
    )
    z_first, z_second = swapped(z_first, "gz", 0), swapped(z_second, "gz", 1)
    slabs = (3, SLABS, EXT, width)
    e1, h2, e2 = call(
        middle_kernel,
        [arr(*slabs), flat, flat],
        [e, h, a, scale, halo, pe, pscale, ph1, pe1, h1_ends, e1_ends, flags],
        "middle",
        [pltpu.VMEM(slabs, f32), pltpu.VMEM(slabs, f32)],
    )
    scalars.add(id(runs))
    dma = pltpu.SemaphoreType.DMA
    e_most, pol2, cur2, j_rest, gains, gain_rows = call(
        blocks_kernel,
        [arr(3, 12 * ROWS, width), blocks, blocks, arr(3, len(END_SLABS), ROWS, width), arr(runs_all, width), arr(slots, width)],
        [
            scale, e1.reshape(3, SLABS * EXT, width), e2, inverse, runs, cells, block_count,
            decay, restore, drive, pol1, cur1,
        ],
        "blocks",
        [blocks_vmem, flat_vmem],
    )
    e_out, h_out, pol2, cur2 = call(
        last_kernel,
        [flat, flat, blocks, blocks],
        [
            e, scale, halo, z_first, z_second, flags, pe, pscale, ph1, pe1, h1_ends, e1_ends, e1, h2, e2,
            e_most, j_rest, gains, gain_rows, runs, cells, pol2, cur2,
        ],
        "last",
        [
            pltpu.VMEM((3, 4 * ROWS, width), f32), pltpu.VMEM((3, 3 * ROWS, width), f32), blocks_vmem, blocks_vmem,
            pltpu.VMEM((3, 2 * ROWS + 8, width), f32), blocks_vmem,
            pltpu.SemaphoreType.DMA((8,)),
        ],
        out_hbm=(0, 1, 2, 3),
    )
    return e_out.reshape(shape), h_out.reshape(shape), pol2, cur2


def solution(mesh):
    grid = P(None, "gz", "gx", "gy")
    rows = ("gx", "gy", "gz")
    return jax.shard_map(
        on_device,
        mesh=mesh,
        in_specs=(
            grid, grid, P("gz", "gx", "gy"), P(), P(rows, None), P(rows), P(rows), P(rows), P(rows),
            P(None, rows, None), P(None, rows, None),
        ),
        out_specs=(grid, grid, P(None, rows, None), P(None, rows, None)),
        check_vma=False,
    )
```
